32 devices in a mesh: dp: 16 (over z, x, core), section: 2 (over y).
Axes of the slice: x: 2, y: 2, z: 4, core: 2. Of those that a mesh axis runs over, the one named last changes fastest.
Arguments:
- inputs: bfloat16 [2, 2048, 768], P(None, 'dp'), may hold values from -6 to 6
- cotangent: bfloat16 [2, 2048, 768], P(None, 'dp'), may hold values from -6 to 6
- lengths: int32 [2, 16, 3], P(None, 'dp'), may hold values from 1 to 32, 64 in all within a row
- gain_one: float32 [2, 768], P('section'), may hold values from 0.5 to 1.5
- w_qkv: bfloat16 [2, 768, 2304], P('section'), may hold values from -0.21875 to 0.21875
- w_out: bfloat16 [2, 768, 768], P('section'), may hold values from -0.625 to 0.625
- gain_two: float32 [2, 768], P('section'), may hold values from 0.5 to 1.5
- w_up: bfloat16 [2, 768, 3072], P('section'), may hold values from -0.21875 to 0.21875
- b_up: float32 [2, 3072], P('section'), may hold values from -2 to 2
- w_down: bfloat16 [2, 3072, 768], P('section'), may hold values from -0.109375 to 0.109375
- b_down: float32 [2, 768], P('section'), may hold values from -2 to 2
Outputs:
- section_out: bfloat16 [2, 2, 2048, 768], P('section', None, 'dp')
- section_grad: bfloat16 [2, 2, 2048, 768], P('section', None, 'dp')
- grad_gain_one: float32 [2, 768], P('section', 'dp')
- grad_qkv: float32 [2, 768, 2304], P('section', 'dp')
- grad_out: float32 [2, 768, 768], P('section', 'dp')
- grad_gain_two: float32 [2, 768], P('section', 'dp')
- grad_up: float32 [2, 768, 3072], P('section', 'dp')
- grad_bias_up: float32 [2, 3072], P('section', 'dp')
- grad_down: float32 [2, 3072, 768], P('section', 'dp')
- grad_bias_down: float32 [2, 768], P('section', 'dp')
The draws below stay inside these ranges and needn't reach their ends.
Inputs may be any that keep to these rules, and one draw needn't show every extreme that they name: Each row of 3 entries sums to 64: the first 2 are the lengths of the slot's documents in order, the last the padding rows at its end.
All inputs are finite; a program needn't handle non-finite values.
Results may differ from the reference program's by a relative error of at most 0.015.
Values may be sent and summed in bfloat16 or wider, within the bound.
A program may use at most 320 MiB of HBM per device.

```python
import math
import jax
import jax.numpy as jnp
import numpy as np
from jax import lax

D = 768
FF = 3072
HEADS = 12
HEAD_DIM = 64
BLOCK = 16
SEGS = 3
MICRO = 2
SEQ_TOK = 64
SLOTS = 16
ROWS = 2048


def block_levels(rng, dims, pieces, low, top_value):
    def one(dim, blocks):
        steps = jax.random.uniform(jax.random.fold_in(jax.random.fold_in(rng, 6), dim), (blocks,), jnp.float32, low / len(pieces), top_value / len(pieces))
        return jnp.repeat(jnp.exp(steps), dims[dim] // blocks).reshape((-1,) + (1,) * (len(dims) - dim - 1))

    level = one(*pieces[0])
    for cut in pieces[1:]:
        level = level * one(*cut)
    return level


def split_up(amount, total, reach, slope):
    loads = [(1 << 20) // math.isqrt(standing ** slope) + 1 for standing in range(2, amount + 1)]
    spare, counts = total - reach - (amount - 1), [1] * (amount - 1)
    while spare > 0:
        candidates = [i for i in range(amount - 1) if counts[i] < reach]
        whole, remaining = sum([loads[i] for i in candidates]), spare
        for i in candidates:
            more = min(reach - counts[i], max(1, remaining * loads[i] // whole), spare)
            counts[i] = counts[i] + more
            spare = spare - more
    return np.array([reach] + counts)


def uneven_parts(rng, amount, total, limit, skew):
    if amount == 2:
        one = jax.random.randint(rng, (), max(1, total - limit), min(limit, total - 1) + 1)
        return jnp.stack([one, total - one])
    sizes = jnp.asarray(split_up(amount, total, limit, skew), jnp.int32)
    couples = (amount - 1) // 2
    source_of, sink = sizes[1:1 + 2 * couples:2], sizes[2:2 + 2 * couples:2]
    margin = jnp.minimum(source_of - 1, limit - sink)
    moved = jax.random.randint(jax.random.fold_in(rng, 1), (couples,), 0, 1 << 20) % (margin + 1)
    sizes = sizes.at[1:1 + 2 * couples:2].set(source_of - moved).at[2:2 + 2 * couples:2].set(sink + moved)
    return sizes[jax.random.permutation(jax.random.fold_in(rng, 2), amount)]


def normal_values(key, shape, spread, reach, split=(), kind=jnp.bfloat16):
    array = spread * jax.random.normal(key, shape, jnp.float32)
    if split:
        array = array * block_levels(key, shape, split, -0.22, 0.18)
    return jnp.clip(array, -reach, reach).astype(kind)


def setup_inputs(seed: int = 0) -> dict:
    arg_keys = jax.random.split(jax.random.key(seed), 12)
    return {
        "inputs": normal_values(arg_keys[0], (MICRO, ROWS, D), 1.0, 6.0, ((1, 16),)),
        "cotangent": normal_values(arg_keys[1], (MICRO, ROWS, D), 1.0, 6.0, ((1, 16),)),
        "lengths": jax.vmap(lambda own: uneven_parts(own, SEGS, SEQ_TOK, SEQ_TOK // 2, 2))(jax.random.split(arg_keys[2], MICRO * SLOTS)).reshape((MICRO, SLOTS, SEGS)).astype(jnp.int32),
        "gain_one": jnp.clip(1.0 + 0.1 * jax.random.normal(arg_keys[3], (2, D), jnp.float32), 0.5, 1.5),
        "w_qkv": normal_values(arg_keys[4], (2, D, 3 * D), D ** -0.5, 0.21875, ((0, 2),)),
        "w_out": normal_values(arg_keys[5], (2, D, D), (D // 8) ** -0.5, 0.625, ((0, 2),)),
        "gain_two": jnp.clip(1.0 + 0.1 * jax.random.normal(arg_keys[6], (2, D), jnp.float32), 0.5, 1.5),
        "w_up": normal_values(arg_keys[7], (2, D, FF), D ** -0.5, 0.21875, ((0, 2),)),
        "b_up": normal_values(arg_keys[8], (2, FF), 0.3, 2.0, ((0, 2),), jnp.float32),
        "w_down": normal_values(arg_keys[9], (2, FF, D), FF ** -0.5, 0.109375, ((0, 2),)),
        "b_down": normal_values(arg_keys[10], (2, D), 0.3, 2.0, ((0, 2),), jnp.float32),
    }


EPSILON = 1e-05

@jax.custom_vjp
def low(v):
    return lax.optimization_barrier(v.astype(jnp.bfloat16)).astype(jnp.float32)

@jax.custom_vjp
def low_back(v):
    return v

def low_keep(v):
    return (low(v), None)

def low_pass(kept, grad):
    return (grad,)

def back_keep(v):
    return (v, None)

def back_low(kept, grad):
    return (low(grad),)
low.defvjp(low_keep, low_pass)
low_back.defvjp(back_keep, back_low)

def row_tables(lengths_row):
    steps_all = jnp.arange(SEQ_TOK, dtype=jnp.int32)
    bounds = jnp.cumsum(lengths_row).astype(jnp.int32)
    passed = (steps_all[:, None] >= bounds[None, :]).astype(jnp.int32)
    document = lax.optimization_barrier(jnp.sum(passed, axis=1)).astype(jnp.int32)
    offset = lax.optimization_barrier(jnp.sum(passed * lengths_row[None, :], axis=1)).astype(jnp.int32)
    position = steps_all - offset
    inside = document < SEGS - 1
    document_rows = jnp.concatenate([document, document])
    position_rows = jnp.concatenate([position, position])
    inside_rows = jnp.concatenate([inside, inside])
    copies = jnp.concatenate([jnp.zeros((SEQ_TOK,), jnp.int32), jnp.ones((SEQ_TOK,), jnp.int32)])
    blocks = position_rows // BLOCK
    query_block = blocks[:, None]
    key_block = blocks[None, :]
    noisy_query = (copies == 0)[:, None]
    noisy_key = (copies == 0)[None, :]
    ruling = jnp.where(noisy_query, jnp.where(noisy_key, key_block == query_block, key_block < query_block), jnp.logical_and(jnp.logical_not(noisy_key), key_block <= query_block))
    same_doc = (document_rows[:, None] == document_rows[None, :]) & inside_rows[:, None] & inside_rows[None, :]
    indices = jnp.arange(2 * SEQ_TOK, dtype=jnp.int32)
    allowed = same_doc & ruling | (indices[:, None] == indices[None, :])
    frequency = jnp.exp(jnp.arange(HEAD_DIM // 2).astype(jnp.float32) * (-2.0 * math.log(10000.0) / HEAD_DIM))
    angles = position_rows.astype(jnp.float32)[:, None] * frequency[None, :]
    return (allowed, jnp.cos(angles), jnp.sin(angles))

def rotate(tensor, cosine, sine):
    halfway = tensor.shape[-1] // 2
    upper_part = tensor[..., :halfway]
    lower_part = tensor[..., halfway:]
    cos_rows = cosine[:, None, :]
    sin_rows = sine[:, None, :]
    return jnp.concatenate([upper_part * cos_rows - lower_part * sin_rows, upper_part * sin_rows + lower_part * cos_rows], axis=-1)

def normalize(values):
    centred = values - lax.optimization_barrier(jnp.mean(values, axis=-1, keepdims=True))
    return centred * lax.rsqrt(lax.optimization_barrier(jnp.mean(centred * centred, axis=-1, keepdims=True)) + EPSILON)

def layer_forward(state, lengths_row, gain_a, w_qkv, w_out, gain_b, w_up, b_up, w_down, b_down):
    allowed, cosine, sine = row_tables(lengths_row)
    count = state.shape[0]
    state = low_back(state)
    normed = low(normalize(state) * gain_a)
    joined = low_back(jnp.dot(normed, w_qkv, precision=lax.Precision.HIGHEST))
    query = low(rotate(joined[:, :D].reshape(count, HEADS, HEAD_DIM), cosine, sine))
    keyset = low(rotate(joined[:, D:2 * D].reshape(count, HEADS, HEAD_DIM), cosine, sine))
    valueset = low(joined[:, 2 * D:].reshape(count, HEADS, HEAD_DIM))
    scores = low_back(jnp.einsum('qhd,khd->hqk', query, keyset, precision=lax.Precision.HIGHEST) * HEAD_DIM ** (-0.5))
    scores = jnp.where(allowed[None], scores, -1e+30)
    probs = low(jax.nn.softmax(scores, axis=-1))
    mixed = jnp.einsum('hqk,khd->qhd', probs, valueset, precision=lax.Precision.HIGHEST).reshape(count, D)
    mixed = low_back(low(mixed))
    branch = low_back(jnp.dot(mixed, w_out, precision=lax.Precision.HIGHEST))
    hidden = state + branch
    normed_two = low(normalize(hidden) * gain_b)
    inner = low_back(jnp.dot(normed_two, w_up, precision=lax.Precision.HIGHEST) + b_up)
    activated = low(jax.nn.gelu(inner, approximate=True))
    branch_two = low_back(jnp.dot(activated, w_down, precision=lax.Precision.HIGHEST) + b_down)
    return low(hidden + branch_two)

def reference(inputs, cotangent, lengths, gain_one, w_qkv, w_out, gain_two, w_up, b_up, w_down, b_down):
    count = 2 * SEQ_TOK
    slots_all = MICRO * SLOTS
    states = inputs.astype(jnp.float32).reshape(slots_all, count, D)
    targets = cotangent.astype(jnp.float32).reshape(slots_all, count, D)
    slot_lengths = lengths.reshape(slots_all, SEGS).astype(jnp.int32)
    params = (gain_one.astype(jnp.float32), w_qkv.astype(jnp.float32), w_out.astype(jnp.float32), gain_two.astype(jnp.float32), w_up.astype(jnp.float32), b_up.astype(jnp.float32), w_down.astype(jnp.float32), b_down.astype(jnp.float32))
    probe = jnp.zeros_like(states)

    def forward(states, params, probe):

        def slot_pass(item):
            state, extra, lengths_row = item
            first = layer_forward(state, lengths_row, *[param[0] for param in params])
            second = layer_forward(first + extra, lengths_row, *[param[1] for param in params])
            return (first, second)
        return lax.map(jax.checkpoint(slot_pass), (states, probe, slot_lengths))
    (first, second), pullback = jax.vjp(forward, states, params, probe)
    d_states, d_params, d_probe = pullback((jnp.zeros_like(first), targets))
    section_out = jnp.stack([first, second]).reshape(2, MICRO, SLOTS * count, D).astype(jnp.bfloat16)
    section_grad = jnp.stack([d_states, d_probe]).reshape(2, MICRO, SLOTS * count, D).astype(jnp.bfloat16)
    grad_gain_one, grad_qkv, grad_out, grad_gain_two, grad_up, grad_bias_up, grad_down, grad_bias_down = d_params
    return (section_out, section_grad, grad_gain_one, grad_qkv, grad_out, grad_gain_two, grad_up, grad_bias_up, grad_down, grad_bias_down)
```

```python
from functools import partial
import math

from types import SimpleNamespace

import jax
import jax.numpy as jnp
from jax import lax
from jax.experimental import pallas as pl
from jax.experimental.pallas import tpu as pltpu
from jax.sharding import PartitionSpec as P

D = 768
FF = 3072
HEADS = 12
HEAD_DIM = 64
BLOCK = 16
SEGS = 3
SEQ_TOK = 64
EPSILON = 1e-05

F32 = jnp.float32
BF16 = jnp.bfloat16
MESH = pl.DeviceIdType.MESH
MICRO = 2
SLOT = 2 * SEQ_TOK
ROWS = MICRO * SLOT
PAIRS = HEADS // 2
LANES = 128
PART = 48
UNITS = 12
WIDE = 768
SCALE = HEAD_DIM ** (-0.5)

UNIT_LEFT = (0, 1, 2, 3, 4, 4, 4, 4, 5, 6, 6, 6)
UNIT_RIGHT = (0, 0, 0, 0, 1, 2, 3, 4, 5, 6, 7, 8)
LEFTS = 7
RIGHTS = 9
SUM_Z_FIRST = 2


def dot(a, b):
    return jnp.dot(a, b, preferred_element_type=F32)


def dot_nt(a, b):
    return lax.dot_general(a, b, (((1,), (1,)), ((), ())), preferred_element_type=F32)


def dot_tn(a, b):
    return lax.dot_general(a, b, (((0,), (0,)), ((), ())), preferred_element_type=F32)


def normalize(values):
    centred = values - jnp.mean(values, axis=-1, keepdims=True)
    inverse = lax.rsqrt(jnp.mean(centred * centred, axis=-1, keepdims=True) + EPSILON)
    return centred * inverse, inverse


def normal_back(d_normed, normed, inverse):
    return inverse * (
        d_normed
        - jnp.mean(d_normed, axis=-1, keepdims=True)
        - normed * jnp.mean(d_normed * normed, axis=-1, keepdims=True)
    )


def token_tables(token, first, second):
    one = (token >= first).astype(jnp.int32)
    two = (token >= first + second).astype(jnp.int32)
    return one + two, token - one * first - two * second


def swap_halves(values):
    lane = lax.broadcasted_iota(jnp.int32, values.shape, 1)
    low = (lane % HEAD_DIM) < HEAD_DIM // 2
    up = pltpu.roll(values, LANES - HEAD_DIM // 2, 1)
    down = pltpu.roll(values, HEAD_DIM // 2, 1)
    return jnp.where(low, up, down)


def head_masked(pair):
    lane = lax.broadcasted_iota(jnp.int32, pair.shape, 1)
    zero = jnp.zeros_like(pair)
    return jnp.concatenate(
        [jnp.where(lane < HEAD_DIM, pair, zero), jnp.where(lane < HEAD_DIM, zero, pair)], axis=0
    )


def build_tables(lengths, cos_t, sin_t, mask_t):
    for m in range(MICRO):
        first, second = lengths[m, 0], lengths[m, 1]
        row = lax.broadcasted_iota(jnp.int32, (SLOT, LANES), 0)
        col = lax.broadcasted_iota(jnp.int32, (SLOT, LANES), 1)
        doc_r, pos_r = token_tables(row % SEQ_TOK, first, second)
        doc_c, pos_c = token_tables(col % SEQ_TOK, first, second)
        block_r, block_c = pos_r // BLOCK, pos_c // BLOCK
        noisy_r, noisy_c = row < SEQ_TOK, col < SEQ_TOK
        same = (doc_r == doc_c) & (doc_r < SEGS - 1)
        ruling = (noisy_r & noisy_c & (block_r == block_c)) | (
            jnp.logical_not(noisy_c)
            & (
                (noisy_r & (block_c < block_r))
                | (jnp.logical_not(noisy_r) & (block_c <= block_r))
            )
        )
        allowed = (same & ruling) | (row == col)
        mask_t[m] = jnp.where(allowed, 1.0, 0.0)
        half = HEAD_DIM // 2
        frequency = jnp.exp((col % half).astype(F32) * (-2.0 * math.log(10000.0) / HEAD_DIM))
        angle = pos_r.astype(F32) * frequency
        sign = jnp.where((col % HEAD_DIM) < half, -1.0, 1.0)
        cos_t[m] = jnp.cos(angle)
        sin_t[m] = jnp.sin(angle) * sign


def rotate_pair(values, cosine, sine):
    return values * cosine + swap_halves(values) * sine


def gelu_both(v):
    c = math.sqrt(2.0 / math.pi)
    square = v * v
    t = jnp.tanh(c * (v + 0.044715 * (v * square)))
    half = 0.5 * (1.0 + t)
    slope = half + (0.5 * c) * v * (1.0 - t * t) * (1.0 + (3.0 * 0.044715) * square)
    return v * half, slope


def forward(R, m, waits):
    rows = pl.ds(pl.multiple_of(m * SLOT, SLOT), SLOT)
    lane = lax.broadcasted_iota(jnp.int32, (SLOT, LANES), 1)
    normed, inverse = normalize(R.x[rows, :].astype(F32))
    R.normed[rows, :] = normed
    R.inv[rows, :] = jnp.broadcast_to(inverse, (SLOT, LANES))
    entry = (normed * R.gain_a[...]).astype(BF16)
    R.entry[rows, :] = entry
    waits(0)
    cosine, sine = R.cos[m], R.sin[m]
    for t in range(9):
        joined = dot(entry, R.w_qkv[:, t * 256 : (t + 1) * 256])
        kept = (R.q, R.k, R.v)[t // 3]
        for j in range(2):
            at = (t * 256 + j * LANES) % D
            piece = joined[:, j * LANES : (j + 1) * LANES]
            if t < 6:
                piece = rotate_pair(piece, cosine, sine)
            kept[rows, at : at + LANES] = piece.astype(BF16)
    keep = jnp.concatenate([R.mask[m], R.mask[m]], axis=0) > 0.5
    for p in range(PAIRS):
        lanes = pl.ds(p * LANES, LANES)
        q2 = head_masked(R.q[rows, lanes])
        raw = dot_nt(q2, R.k[rows, lanes]) * SCALE
        scores = jnp.where(keep, raw, -1e30)
        exponent = jnp.exp(scores - jnp.max(scores, axis=-1, keepdims=True))
        probs = exponent / jnp.sum(exponent, axis=-1, keepdims=True)
        R.probs[m * PAIRS + p] = probs
        pv = dot(probs.astype(BF16), R.v[rows, lanes])
        R.mixed[rows, lanes] = jnp.where(lane < HEAD_DIM, pv[:SLOT], pv[SLOT:]).astype(BF16)
    waits(1)
    hidden = R.x[rows, :].astype(F32) + dot(R.mixed[rows, :], R.w_out[...])
    R.hidden[rows, :] = hidden
    normed, inverse = normalize(hidden)
    R.normed2[rows, :] = normed
    R.inv2[rows, :] = jnp.broadcast_to(inverse, (SLOT, LANES))
    entry2 = (normed * R.gain_b[...]).astype(BF16)
    R.entry2[rows, :] = entry2
    waits(2)
    for t in range(FF // 256):
        cols = pl.ds(t * 256, 256)
        inner = dot(entry2, R.w_up[:, cols]) + R.b_up[:, cols]
        act, slope = gelu_both(inner)
        R.act[rows, cols] = act.astype(BF16)
        R.slope[rows, cols] = slope
    waits(3)
    R.y[rows, :] = (
        R.hidden[rows, :] + dot(R.act[rows, :], R.w_down[...]) + R.b_down[...]
    ).astype(BF16)


def backward_feed(R):
    g = R.right[0]
    for t in range(12):
        d_act = dot_nt(g, R.w_down[t * 256 : (t + 1) * 256, :])
        d_inner = (R.slope[:, t * 256 : (t + 1) * 256] * d_act).astype(BF16)
        R.right[1 + t // 3, :, (t % 3) * 256 : (t % 3 + 1) * 256] = d_inner
        R.vec[3 + t // 3 : 4 + t // 3, (t % 3) * 256 : (t % 3 + 1) * 256] = jnp.sum(
            d_inner.astype(F32), axis=0, keepdims=True
        )
    R.vec[2:3, :] = jnp.sum(g.astype(F32), axis=0, keepdims=True)
    for t in range(3):
        rows = pl.ds(t * 256, 256)
        total = dot_nt(R.right[1], R.w_up[rows, 0:WIDE])
        for j in range(1, 4):
            total += dot_nt(R.right[1 + j], R.w_up[rows, j * WIDE : (j + 1) * WIDE])
        R.hidden[:, rows] = total
    gain = jnp.zeros((1, D), F32)
    for m in range(MICRO):
        rows = pl.ds(m * SLOT, SLOT)
        d_entry = R.hidden[rows, :]
        normed = R.normed2[rows, :]
        gain += jnp.sum(d_entry * normed, axis=0, keepdims=True)
        d_hidden = R.right[0, rows, :].astype(F32) + normal_back(
            d_entry * R.gain_b[...], normed, R.inv2[rows, 0:1]
        )
        R.hidden[rows, :] = d_hidden
        R.right[5, rows, :] = d_hidden.astype(BF16)
    R.vec[1:2, :] = gain


def backward_attention(R, m):
    rows = pl.ds(pl.multiple_of(m * SLOT, SLOT), SLOT)
    R.d_mixed[rows, :] = dot_nt(R.right[5, rows, :], R.w_out[...]).astype(BF16)
    cosine, sine = R.cos[m], -R.sin[m]
    for p in range(PAIRS):
        lanes = pl.ds(p * LANES, LANES)
        dm2 = head_masked(R.d_mixed[rows, lanes])
        q2 = head_masked(R.q[rows, lanes])
        k2 = head_masked(R.k[rows, lanes])
        probs = R.probs[m * PAIRS + p]
        d_probs = dot_nt(dm2, R.v[rows, lanes])
        d_scores = (
            probs * (d_probs - jnp.sum(probs * d_probs, axis=-1, keepdims=True))
        ).astype(BF16)
        d_values = dot_tn(probs.astype(BF16), dm2)
        side = jnp.concatenate([d_scores[:SLOT], d_scores[SLOT:]], axis=1)
        d_query = dot(side, k2) * SCALE
        d_keys = dot_tn(d_scores, q2) * SCALE
        R.right[6, rows, lanes] = rotate_pair(d_query, cosine, sine).astype(BF16)
        R.right[7, rows, lanes] = rotate_pair(d_keys, cosine, sine).astype(BF16)
        R.right[8, rows, lanes] = d_values.astype(BF16)
    d_entry = jnp.zeros((SLOT, D), F32)
    for t in range(3):
        d_entry += dot_nt(R.right[6 + t, rows, :], R.w_qkv[:, t * WIDE : (t + 1) * WIDE])
    normed = R.normed[rows, :]
    R.vec[0:1, :] = R.vec[0:1, :] + jnp.sum(d_entry * normed, axis=0, keepdims=True)
    R.d_state[rows, :] = (
        R.hidden[rows, :] + normal_back(d_entry * R.gain_a[...], normed, R.inv[rows, 0:1])
    ).astype(BF16)


def turn_lefts(R, core):
    def place(kind, owner_core, chip, block):
        x, z = chip % 2, chip // 2

        @pl.when(core == owner_core)
        def _():
            R.left[kind, x * 4 + z] = block

        @pl.when(core != owner_core)
        def _():
            R.left_out[kind, x * 4 + z] = block

    for kind, factor in ((4, R.entry2), (5, R.mixed), (6, R.entry)):
        turned = factor[...].T
        for d in range(16):
            place(kind, d % 2, d // 2, turned[d * PART : (d + 1) * PART, :])
    for d4 in range(4):
        turned = R.act[:, d4 * 768 : (d4 + 1) * 768].T
        for e in range(4):
            d = d4 * 4 + e
            for i in range(4):
                at = e * 192 + i * PART
                place(i, d % 2, d // 2, turned[at : at + PART, :])


def passed_along(block, axis, distance):
    devices = range(lax.axis_size(axis))
    route = [(i - distance, i) for i in devices if i - distance in devices]
    return lax.ppermute(block, axis, route)


def row_tables(lengths_row):
    steps_all = jnp.arange(SEQ_TOK, dtype=jnp.int32)
    bounds = jnp.cumsum(lengths_row)
    passed = (steps_all[:, None] >= bounds[None, :]).astype(jnp.int32)
    document = jnp.sum(passed, axis=1)
    offset = jnp.sum(passed * lengths_row[None, :], axis=1)
    position = steps_all - offset
    inside = document < SEGS - 1
    document_rows = jnp.concatenate([document, document])
    position_rows = jnp.concatenate([position, position])
    inside_rows = jnp.concatenate([inside, inside])
    copies = jnp.concatenate([jnp.zeros((SEQ_TOK,), jnp.int32), jnp.ones((SEQ_TOK,), jnp.int32)])
    blocks = position_rows // BLOCK
    query_block = blocks[:, None]
    key_block = blocks[None, :]
    noisy_query = (copies == 0)[:, None]
    noisy_key = (copies == 0)[None, :]
    ruling = jnp.where(
        noisy_query,
        jnp.where(noisy_key, key_block == query_block, key_block < query_block),
        jnp.logical_and(jnp.logical_not(noisy_key), key_block <= query_block),
    )
    same_doc = (
        (document_rows[:, None] == document_rows[None, :])
        & inside_rows[:, None]
        & inside_rows[None, :]
    )
    indices = jnp.arange(2 * SEQ_TOK, dtype=jnp.int32)
    allowed = same_doc & ruling | (indices[:, None] == indices[None, :])
    frequency = jnp.exp(
        jnp.arange(HEAD_DIM // 2).astype(jnp.float32) * (-2.0 * math.log(10000.0) / HEAD_DIM)
    )
    angles = position_rows.astype(jnp.float32)[:, None] * frequency[None, :]
    return (allowed, jnp.cos(angles), jnp.sin(angles))


def rotate(tensor, cosine, sine):
    halfway = tensor.shape[-1] // 2
    upper_part = tensor[..., :halfway]
    lower_part = tensor[..., halfway:]
    cos_rows = cosine[:, None, :]
    sin_rows = sine[:, None, :]
    return jnp.concatenate(
        [
            upper_part * cos_rows - lower_part * sin_rows,
            upper_part * sin_rows + lower_part * cos_rows,
        ],
        axis=-1,
    )


def unrotate(gradient, cosine, sine):
    halfway = gradient.shape[-1] // 2
    upper_part = gradient[..., :halfway]
    lower_part = gradient[..., halfway:]
    cos_rows = cosine[:, None, :]
    sin_rows = sine[:, None, :]
    return jnp.concatenate(
        [
            upper_part * cos_rows + lower_part * sin_rows,
            lower_part * cos_rows - upper_part * sin_rows,
        ],
        axis=-1,
    )


def plain_normalize(values):
    centred = values - jnp.mean(values, axis=-1, keepdims=True)
    inverse = lax.rsqrt(jnp.mean(centred * centred, axis=-1, keepdims=True) + EPSILON)
    return (centred * inverse, inverse)


def plain_normal_back(d_normed, normed, inverse):
    return inverse * (
        d_normed
        - jnp.mean(d_normed, axis=-1, keepdims=True)
        - normed * jnp.mean(d_normed * normed, axis=-1, keepdims=True)
    )


def scores_of(query, keyset, allowed):
    raw = jnp.einsum(
        "qhd,khd->hqk", query, keyset, preferred_element_type=jnp.float32
    ) * HEAD_DIM ** (-0.5)
    return jnp.where(allowed[None], raw, -1e30)


def forward_pass(state, lengths_row, weights):
    gain_a, w_qkv, w_out, gain_b, w_up, b_up, w_down, b_down = weights
    allowed, cosine, sine = row_tables(lengths_row)
    count = state.shape[0]
    widened = state.astype(jnp.float32)
    normed, inverse = plain_normalize(widened)
    entry = (normed * gain_a).astype(jnp.bfloat16)
    joined = jnp.dot(entry, w_qkv, preferred_element_type=jnp.float32)
    query = rotate(joined[:, :D].reshape(count, HEADS, HEAD_DIM), cosine, sine).astype(jnp.bfloat16)
    keyset = rotate(joined[:, D : 2 * D].reshape(count, HEADS, HEAD_DIM), cosine, sine).astype(
        jnp.bfloat16
    )
    valueset = joined[:, 2 * D :].reshape(count, HEADS, HEAD_DIM).astype(jnp.bfloat16)
    scores = scores_of(query, keyset, allowed)
    highest = jnp.max(scores, axis=-1, keepdims=True)
    exponent = jnp.exp(scores - highest)
    totals = jnp.sum(exponent, axis=-1, keepdims=True)
    soft_low = (exponent / totals).astype(jnp.bfloat16)
    log_total = highest + jnp.log(totals)
    mixed = (
        jnp.einsum("hqk,khd->qhd", soft_low, valueset, preferred_element_type=jnp.float32)
        .reshape(count, D)
        .astype(jnp.bfloat16)
    )
    hidden = widened + jnp.dot(mixed, w_out, preferred_element_type=jnp.float32)
    normed_two, inverse_two = plain_normalize(hidden)
    entry_two = (normed_two * gain_b).astype(jnp.bfloat16)
    inner = jnp.dot(entry_two, w_up, preferred_element_type=jnp.float32) + b_up
    activated = jax.nn.gelu(inner, approximate=True).astype(jnp.bfloat16)
    result = (
        hidden + jnp.dot(activated, w_down, preferred_element_type=jnp.float32) + b_down
    ).astype(jnp.bfloat16)
    saved = (
        normed,
        inverse,
        entry,
        query,
        keyset,
        valueset,
        log_total,
        mixed,
        normed_two,
        inverse_two,
        entry_two,
        inner,
        activated,
    )
    return (result, saved)


def forward_blank(state, lengths_row, weights):
    count = state.shape[0]
    rows_f = jnp.zeros((count, D), jnp.float32)
    rows_b = jnp.zeros((count, D), jnp.bfloat16)
    column = jnp.zeros((count, 1), jnp.float32)
    heads_b = jnp.zeros((count, HEADS, HEAD_DIM), jnp.bfloat16)
    saved = (
        rows_f,
        column,
        rows_b,
        heads_b,
        heads_b,
        heads_b,
        jnp.zeros((HEADS, count, 1), jnp.float32),
        rows_b,
        rows_f,
        column,
        rows_b,
        jnp.zeros((count, FF), jnp.float32),
        jnp.zeros((count, FF), jnp.bfloat16),
    )
    return (jnp.zeros_like(state), saved)


def settle_plain(index, group):
    return group


def backward_core(saved, incoming, lengths_row, weights, settle):
    gain_a, w_qkv, w_out, gain_b, w_up, b_up, w_down, b_down = weights
    (
        normed,
        inverse,
        entry,
        query,
        keyset,
        valueset,
        log_total,
        mixed,
        normed_two,
        inverse_two,
        entry_two,
        inner,
        activated,
    ) = saved
    allowed, cosine, sine = row_tables(lengths_row)
    count = incoming.shape[0]
    upper = incoming.astype(jnp.float32)
    grad_down = jnp.einsum("rf,rd->fd", activated, incoming, preferred_element_type=jnp.float32)
    grad_bias_down = jnp.sum(upper, axis=0)
    d_activated = jnp.einsum("rd,fd->rf", incoming, w_down, preferred_element_type=jnp.float32)
    _, gelu_pull = jax.vjp(partial(jax.nn.gelu, approximate=True), inner)
    d_inner = gelu_pull(d_activated)[0].astype(jnp.bfloat16)
    grad_up = jnp.einsum("rd,rf->df", entry_two, d_inner, preferred_element_type=jnp.float32)
    grad_bias_up = jnp.sum(d_inner, axis=0, dtype=jnp.float32)
    d_entry_two = jnp.einsum("rf,df->rd", d_inner, w_up, preferred_element_type=jnp.float32)
    grad_gain_b = jnp.sum(d_entry_two * normed_two, axis=0)
    feed_group = settle(0, (grad_gain_b, grad_up, grad_bias_up, grad_down, grad_bias_down))
    d_hidden = upper + plain_normal_back(d_entry_two * gain_b, normed_two, inverse_two)
    d_branch = d_hidden.astype(jnp.bfloat16)
    grad_out = jnp.einsum("rd,re->de", mixed, d_branch, preferred_element_type=jnp.float32)
    d_mixed = (
        jnp.einsum("re,de->rd", d_branch, w_out, preferred_element_type=jnp.float32)
        .astype(jnp.bfloat16)
        .reshape(count, HEADS, HEAD_DIM)
    )
    scores = scores_of(query, keyset, allowed)
    probs = jnp.exp(scores - log_total)
    d_probs = jnp.einsum("qhd,khd->hqk", d_mixed, valueset, preferred_element_type=jnp.float32)
    d_scores = (probs * (d_probs - jnp.sum(probs * d_probs, axis=-1, keepdims=True))).astype(
        jnp.bfloat16
    )
    d_values = jnp.einsum(
        "hqk,qhd->khd", probs.astype(jnp.bfloat16), d_mixed, preferred_element_type=jnp.float32
    )
    scaling = HEAD_DIM ** (-0.5)
    d_query = (
        jnp.einsum("hqk,khd->qhd", d_scores, keyset, preferred_element_type=jnp.float32) * scaling
    )
    d_keys = (
        jnp.einsum("hqk,qhd->khd", d_scores, query, preferred_element_type=jnp.float32) * scaling
    )
    d_joined = jnp.concatenate(
        [
            unrotate(d_query, cosine, sine).reshape(count, D),
            unrotate(d_keys, cosine, sine).reshape(count, D),
            d_values.reshape(count, D),
        ],
        axis=1,
    ).astype(jnp.bfloat16)
    grad_qkv = jnp.einsum("rd,re->de", entry, d_joined, preferred_element_type=jnp.float32)
    d_entry = jnp.einsum("re,de->rd", d_joined, w_qkv, preferred_element_type=jnp.float32)
    grad_gain_a = jnp.sum(d_entry * normed, axis=0)
    attn_group = settle(1, (grad_gain_a, grad_qkv, grad_out))
    d_state = (d_hidden + plain_normal_back(d_entry * gain_a, normed, inverse)).astype(jnp.bfloat16)
    return (d_state, tuple(attn_group) + tuple(feed_group))


def backward_pass(saved, incoming, lengths_row, weights):
    return backward_core(saved, incoming, lengths_row, weights, settle_plain)


def backward_blank(saved, incoming, lengths_row, weights):
    return (
        jnp.zeros_like(incoming),
        tuple((jnp.zeros(item.shape, jnp.float32) for item in weights)),
    )


def keep_at(place, active, stack, leaf):
    current = lax.dynamic_index_in_dim(stack, place, 0, keepdims=False)
    return lax.dynamic_update_index_in_dim(stack, jnp.where(active, leaf, current), place, 0)


def reduce_total(grads):
    (
        grad_gain_a,
        grad_qkv,
        grad_out,
        grad_gain_b,
        grad_up,
        grad_bias_up,
        grad_down,
        grad_bias_down,
    ) = grads
    return (
        lax.psum_scatter(grad_gain_a[None], "dp", scatter_dimension=1, tiled=True),
        lax.psum_scatter(grad_qkv[None], "dp", scatter_dimension=1, tiled=True),
        lax.psum_scatter(grad_out[None], "dp", scatter_dimension=1, tiled=True),
        lax.psum_scatter(grad_gain_b[None], "dp", scatter_dimension=1, tiled=True),
        lax.psum_scatter(grad_up[None], "dp", scatter_dimension=1, tiled=True),
        lax.psum_scatter(grad_bias_up[None], "dp", scatter_dimension=1, tiled=True),
        lax.psum_scatter(grad_down[None], "dp", scatter_dimension=1, tiled=True),
        lax.psum_scatter(grad_bias_down[None], "dp", scatter_dimension=1, tiled=True),
    )


def plain_device(
    inputs, cotangent, lengths, gain_one, w_qkv, w_out, gain_two, w_up, b_up, w_down, b_down
):
    section = lax.axis_index("section")
    micro = inputs.shape[0]
    weights = (gain_one[0], w_qkv[0], w_out[0], gain_two[0], w_up[0], b_up[0], w_down[0], b_down[0])
    slot_lengths = lengths[:, 0]
    arrived = jnp.zeros(inputs.shape[1:], jnp.bfloat16)
    results = jnp.zeros(inputs.shape, jnp.bfloat16)
    stored = ()
    for tick in range(micro + 1):
        number = tick - section
        active = jnp.logical_and(number >= 0, number < micro)
        place = jnp.clip(number, 0, micro - 1)
        layer_in = jnp.where(section == 0, inputs[min(tick, micro - 1)], arrived)
        lengths_row = lax.dynamic_index_in_dim(slot_lengths, place, 0, keepdims=False)
        result, saved = lax.cond(
            active, forward_pass, forward_blank, layer_in, lengths_row, weights
        )
        if tick == 0:
            stored = jax.tree.map(lambda leaf: jnp.zeros((micro,) + leaf.shape, leaf.dtype), saved)
        stored = jax.tree.map(partial(keep_at, place, active), stored, saved)
        results = keep_at(place, active, results, result)
        if tick < micro:
            arrived = passed_along(result, "section", 1)
    back_arrived = jnp.zeros(inputs.shape[1:], jnp.bfloat16)
    grads_in = jnp.zeros(inputs.shape, jnp.bfloat16)
    totals = tuple((jnp.zeros(item.shape, jnp.float32) for item in weights))
    reduced_sums = ()
    for tick in range(micro + 1):
        number = tick - (1 - section)
        active = jnp.logical_and(number >= 0, number < micro)
        place = jnp.clip(number, 0, micro - 1)
        incoming = jnp.where(section == 1, cotangent[min(tick, micro - 1)], back_arrived)
        saved = jax.tree.map(
            lambda stack: lax.dynamic_index_in_dim(stack, place, 0, keepdims=False), stored
        )
        lengths_row = lax.dynamic_index_in_dim(slot_lengths, place, 0, keepdims=False)
        d_state, grads = lax.cond(
            active, backward_pass, backward_blank, saved, incoming, lengths_row, weights
        )
        totals = tuple((earlier + later for earlier, later in zip(totals, grads)))
        grads_in = keep_at(place, active, grads_in, d_state)
        if tick < micro:
            back_arrived = passed_along(d_state, "section", -1)
    reduced_sums = reduce_total(totals)
    sum_gain_a, sum_qkv, sum_out, sum_gain_b, sum_up, sum_bias_up, sum_down, sum_bias_down = (
        reduced_sums
    )
    return (
        results[None],
        grads_in[None],
        sum_gain_a,
        sum_qkv,
        sum_out,
        sum_gain_b,
        sum_up,
        sum_bias_up,
        sum_down,
        sum_bias_down,
    )


VMEM = pl.BlockSpec(memory_space=pltpu.VMEM)
SMEM = pl.BlockSpec(memory_space=pltpu.SMEM)
ANY = pl.BlockSpec(memory_space=pl.ANY)
IN = dict(
    inputs=ANY, cotangent=ANY, lengths=SMEM, gain_a=VMEM, w_qkv_in=ANY, w_out_in=ANY,
    gain_b=VMEM, w_up_in=ANY, b_up=VMEM, w_down_in=ANY, b_down=VMEM,
)
OUT = dict(
    y=((ROWS, D), BF16),
    d_state=((ROWS, D), BF16),
    sum_qkv=((PART, 3 * D), F32),
    sum_out=((PART, D), F32),
    sum_up=((PART, FF), F32),
    sum_down=((4 * PART, D), F32),
    vec_sum=((8, WIDE), F32),
)
EVERY, INNER, OUTER = range(3)
DEPTH = 2
A_UNITS = UNITS - SUM_Z_FIRST

SCRATCH = dict(
    w_qkv=((D, 3 * D), BF16),
    w_out=((D, D), BF16),
    w_up=((D, FF), BF16),
    w_down=((FF, D), BF16),
    x=((ROWS, D), BF16),
    cos=((MICRO, SLOT, LANES), F32),
    sin=((MICRO, SLOT, LANES), F32),
    mask=((MICRO, SLOT, SLOT), F32),
    normed=((ROWS, D), F32),
    inv=((ROWS, LANES), F32),
    entry=((ROWS, D), BF16),
    q=((ROWS, D), BF16),
    k=((ROWS, D), BF16),
    v=((ROWS, D), BF16),
    probs=((MICRO * PAIRS, 2 * SLOT, SLOT), F32),
    mixed=((ROWS, D), BF16),
    hidden=((ROWS, D), F32),
    normed2=((ROWS, D), F32),
    inv2=((ROWS, LANES), F32),
    entry2=((ROWS, D), BF16),
    act=((ROWS, FF), BF16),
    slope=((ROWS, FF), F32),
    d_mixed=((ROWS, D), BF16),
    d_entry=((ROWS, D), F32),
    right=((RIGHTS, ROWS, WIDE), BF16),
    right_in=((RIGHTS, ROWS, WIDE), BF16),
    left=((LEFTS, 8, PART, ROWS), BF16),
    left_out=((LEFTS, 8, PART, ROWS), BF16),
    left_in=((LEFTS, 8, PART, ROWS), BF16),
    grad=((UNITS, 2, 4, PART, WIDE), BF16),
    ax=((A_UNITS, 4, PART, WIDE), BF16),
    az=((A_UNITS, 5, PART, WIDE), BF16),
    bz=((SUM_Z_FIRST, 5, 2, PART, WIDE), BF16),
    bs=((SUM_Z_FIRST, PART, WIDE), BF16),
    bx=((SUM_Z_FIRST, PART, WIDE), BF16),
    vec=((8, WIDE), F32),
    vec_in=((5, 8, WIDE), F32),
    vec_part=((3, 8, WIDE), F32),
)
SEMS = dict(
    load=(5,), ys=(4,), yr=(4,), ls=(4,), lr=(4,), rs=(4,), rr=(4,),
    axs=(A_UNITS,), axr=(A_UNITS,), azs=(A_UNITS, 5), azr=(A_UNITS, 5),
    bzs=(SUM_Z_FIRST, 5), bzr=(SUM_Z_FIRST, 5), bxs=(SUM_Z_FIRST,), bxr=(SUM_Z_FIRST,),
    vs=(5,), vr=(5,),
)
LEFT_GROUPS = ((0, 4), (4, 1), (5, 1), (6, 1))
RIGHT_GROUPS = ((0, 1), (1, 4), (5, 1), (6, 3))


def kernel(*refs):
    names = (*IN, *OUT, *SCRATCH, *SEMS)
    R = SimpleNamespace(**dict(zip(names, refs)))
    place, section = lax.axis_index("dp"), lax.axis_index("section")
    core, x, z = place % 2, (place // 2) % 2, place // 4
    half = z // 2
    outer = (z == 0) | (z == 3)
    inner = (z == 1) | (z == 2)

    def dp_of(z_, x_, core_):
        return (z_ * 4 + x_ * 2 + core_, section)

    near_core = dp_of(z, x, 1 - core)
    near_x = dp_of(z, 1 - x, core)
    near_y = (place, 1 - section)
    near_side = dp_of(half * 2 + 1 - z % 2, x, core)
    near_mid = dp_of(3 - z, x, core)

    owners = [j + half * (3 - 2 * j) for j in range(4)]

    def owner(j):
        return owners[j]

    def copy(src, dst, send, recv, device):
        return pltpu.make_async_remote_copy(
            src_ref=src, dst_ref=dst, send_sem=send, recv_sem=recv,
            device_id=device, device_id_type=MESH,
        )

    weights_in = (R.w_qkv_in, R.w_out_in, R.w_up_in, R.w_down_in)
    weights = (R.w_qkv, R.w_out, R.w_up, R.w_down)
    loads = [
        pltpu.make_async_copy(src, dst, R.load.at[i])
        for i, (src, dst) in enumerate(zip(weights_in, weights))
    ]
    for load in loads:
        load.start()

    def take(index, src, dst):
        @pl.when(section == index)
        def _():
            pltpu.make_async_copy(src, dst, R.load.at[4]).start()

    def taken(index, src, dst):
        @pl.when(section == index)
        def _():
            pltpu.make_async_copy(src, dst, R.load.at[4]).wait()

    take(0, R.inputs, R.x)
    take(1, R.cotangent, R.right.at[0])

    barrier = pltpu.get_barrier_semaphore()
    for device in (near_core, near_x, near_y, near_side):
        pl.semaphore_signal(barrier, inc=1, device_id=device, device_id_type=MESH)

    @pl.when(inner)
    def _():
        pl.semaphore_signal(barrier, inc=1, device_id=near_mid, device_id_type=MESH)

    build_tables(R.lengths, R.cos, R.sin, R.mask)

    @pl.when(inner)
    def _():
        pl.semaphore_wait(barrier, 5)

    @pl.when(outer)
    def _():
        pl.semaphore_wait(barrier, 4)

    def x_copy(m):
        rows = pl.ds(m * SLOT, SLOT)
        return copy(R.y.at[rows], R.x.at[rows], R.ys.at[m], R.yr.at[m], near_y)

    def g_copy(m):
        rows = pl.ds(m * SLOT, SLOT)
        return copy(
            R.d_state.at[rows], R.right.at[0, rows], R.ys.at[2 + m], R.yr.at[2 + m], near_y
        )

    taken(0, R.inputs, R.x)
    for m in range(MICRO):

        @pl.when(section == 1)
        def _():
            x_copy(m).wait_recv()

        forward(R, m, lambda n: loads[n].wait() if m == 0 else None)

        @pl.when(section == 0)
        def _():
            x_copy(m).start()

    def left_copy(i):
        a, n = LEFT_GROUPS[i]
        rows = pl.ds(a, n)
        return copy(
            R.left_out.at[rows], R.left_in.at[rows], R.ls.at[i], R.lr.at[i], near_core
        )

    def right_copy(i):
        a, n = RIGHT_GROUPS[i]
        rows = pl.ds(a, n)
        return copy(
            R.right.at[rows], R.right_in.at[rows], R.rs.at[i], R.rr.at[i], near_core
        )

    def send_lefts():
        turn_lefts(R, core)
        for i in range(4):
            left_copy(i).start()

    @pl.when(section == 0)
    def _():
        send_lefts()
        for m in range(MICRO):
            g_copy(m).wait_recv()

    taken(1, R.cotangent, R.right.at[0])

    def weight_unit(u):
        left, right = UNIT_LEFT[u], UNIT_RIGHT[u]
        own = R.left[left].reshape(8 * PART, ROWS)
        other = R.left_in[left].reshape(8 * PART, ROWS)
        total = dot(own, R.right[right]) + dot(other, R.right_in[right])
        R.grad[u] = total.astype(BF16).reshape(2, 4, PART, WIDE)

    def finish(u, total):
        if u < 4:
            R.sum_down[u * PART : (u + 1) * PART, :] = total
        elif u < 8:
            R.sum_up[:, (u - 4) * WIDE : (u - 3) * WIDE] = total
        elif u == 8:
            R.sum_out[...] = total
        else:
            R.sum_qkv[:, (u - 9) * WIDE : (u - 8) * WIDE] = total

    started = {}

    def start(condition, make, *operands):
        started[(condition, make) + operands[:1] + operands[-2:-1]] = (condition, make, operands)
        make(*operands).start()

    def ax_copy(i):
        u = i + SUM_Z_FIRST
        return copy(R.grad.at[u, 1 - x], R.ax.at[i], R.axs.at[i], R.axr.at[i], near_x)

    def az_copy(i, src, at, slot, device):
        return copy(
            src.at[at], R.az.at[i, slot], R.azs.at[i, slot], R.azr.at[i, slot], device
        )

    def a0(i):
        start(EVERY, ax_copy, i)

    def a1(i):
        ax_copy(i).wait_recv()
        for j in range(4):
            R.ax[i, j] = R.ax[i, j] + R.grad[i + SUM_Z_FIRST, x, j]

        @pl.when(outer)
        def _():
            for j in (3, 2, 1):
                start(OUTER, az_copy, i, R.ax, (i, owner(j)), j - 1, near_side)

    def a2(i):
        @pl.when(inner)
        def _():
            for j in (3, 2):
                az_copy(i, R.az, (i, j - 1), j - 1, near_side).wait_recv()
                R.az[i, j - 1] = R.az[i, j - 1] + R.ax[i, owner(j)]
                start(INNER, az_copy, i, R.az, (i, j - 1), 6 - j, near_mid)

    def a3(i):
        @pl.when(inner)
        def _():
            az_copy(i, R.az, (i, 3), 3, near_mid).wait_recv()
            R.az[i, 3] = R.az[i, 3] + R.ax[i, owner(0)]
            start(INNER, az_copy, i, R.az, (i, 3), 0, near_side)

    def a4(i):
        u = i + SUM_Z_FIRST

        @pl.when(inner)
        def _():
            az_copy(i, R.az, (i, 0), 0, near_side).wait_recv()
            az_copy(i, R.az, (i, 4), 4, near_mid).wait_recv()
            finish(
                u,
                R.ax[i, owner(1)].astype(F32)
                + R.az[i, 0].astype(F32)
                + R.az[i, 4].astype(F32),
            )

        @pl.when(outer)
        def _():
            az_copy(i, R.az, (i, 0), 0, near_side).wait_recv()
            finish(u, R.ax[i, owner(0)].astype(F32) + R.az[i, 0].astype(F32))

    def bz_copy(i, src, at, slot, device):
        return copy(
            src.at[at], R.bz.at[i, slot], R.bzs.at[i, slot], R.bzr.at[i, slot], device
        )

    def bx_copy(i):
        return copy(R.bs.at[i], R.bx.at[i], R.bxs.at[i], R.bxr.at[i], near_x)

    def b0(i):
        @pl.when(outer)
        def _():
            for j in (3, 2, 1):
                start(OUTER, bz_copy, i, R.grad, (i, slice(None), owner(j)), j - 1, near_side)

    def b1(i):
        @pl.when(inner)
        def _():
            for j in (3, 2):
                bz_copy(i, R.bz, (i, j - 1), j - 1, near_side).wait_recv()
                for a in range(2):
                    R.bz[i, j - 1, a] = R.bz[i, j - 1, a] + R.grad[i, a, owner(j)]
                start(INNER, bz_copy, i, R.bz, (i, j - 1), 6 - j, near_mid)

    def b2(i):
        @pl.when(inner)
        def _():
            bz_copy(i, R.bz, (i, 3), 3, near_mid).wait_recv()
            for a in range(2):
                R.bz[i, 3, a] = R.bz[i, 3, a] + R.grad[i, a, owner(0)]
            start(INNER, bz_copy, i, R.bz, (i, 3), 0, near_side)

    def b_total(i, a):
        own = R.grad[i, a, z].astype(F32) + R.bz[i, 0, a].astype(F32)
        return own

    def b3(i):
        @pl.when(inner)
        def _():
            bz_copy(i, R.bz, (i, 0), 0, near_side).wait_recv()
            bz_copy(i, R.bz, (i, 4), 4, near_mid).wait_recv()
            R.bs[i] = (b_total(i, 1 - x) + R.bz[i, 4, 1 - x].astype(F32)).astype(BF16)

        @pl.when(outer)
        def _():
            bz_copy(i, R.bz, (i, 0), 0, near_side).wait_recv()
            R.bs[i] = b_total(i, 1 - x).astype(BF16)

        start(EVERY, bx_copy, i)

    def b4(i):
        bx_copy(i).wait_recv()

        @pl.when(inner)
        def _():
            finish(i, b_total(i, x) + R.bz[i, 4, x].astype(F32) + R.bx[i].astype(F32))

        @pl.when(outer)
        def _():
            finish(i, b_total(i, x) + R.bx[i].astype(F32))

    def v_copy(stage, src, at, device):
        return copy(src.at[at] if at is not None else src, R.vec_in.at[stage], R.vs.at[stage], R.vr.at[stage], device)

    def v0():
        start(EVERY, v_copy, 0, R.vec, None, near_core)

    def v1():
        v_copy(0, R.vec, None, near_core).wait_recv()
        R.vec_part[0] = R.vec[...] + R.vec_in[0]
        start(EVERY, v_copy, 1, R.vec_part, 0, near_x)

    def v2():
        v_copy(1, R.vec_part, 0, near_x).wait_recv()
        R.vec_part[1] = R.vec_part[0] + R.vec_in[1]

        @pl.when(outer)
        def _():
            start(OUTER, v_copy, 2, R.vec_part, 1, near_side)

    def v3():
        @pl.when(inner)
        def _():
            v_copy(2, R.vec_part, 1, near_side).wait_recv()
            R.vec_part[2] = R.vec_part[1] + R.vec_in[2]
            start(INNER, v_copy, 3, R.vec_part, 2, near_mid)

    def v4():
        @pl.when(inner)
        def _():
            v_copy(3, R.vec_part, 2, near_mid).wait_recv()
            R.vec_sum[...] = R.vec_part[2] + R.vec_in[3]
            start(INNER, v_copy, 4, R.vec_sum, None, near_side)

    def v5():
        @pl.when(outer)
        def _():
            v_copy(4, R.vec_part, 2, near_side).wait_recv()
            R.vec_sum[...] = R.vec_in[4]

    def first_units():
        left_copy(0).wait_recv()
        right_copy(0).wait_recv()
        for u, send, i in ((0, b0, 0), (2, a0, 0), (1, b0, 1), (3, a0, 1)):
            weight_unit(u)
            send(i)

    right_copy(0).start()
    R.vec[...] = jnp.zeros((8, WIDE), F32)
    pl.when(section == 0)(first_units)
    backward_feed(R)
    right_copy(1).start()
    right_copy(2).start()
    for m in range(MICRO):
        backward_attention(R, m)

        @pl.when(section == 1)
        def _():
            g_copy(m).start()

    right_copy(3).start()

    @pl.when(section == 1)
    def _():
        send_lefts()
        first_units()

    for i in range(1, 4):
        left_copy(i).wait_recv()
        right_copy(i).wait_recv()

    events = []
    for u in range(4, UNITS):
        i = u - SUM_Z_FIRST
        events += [(0.0, weight_unit, u)]
        if i < DEPTH:
            events += [(0.0, a0, i)]
    for i, t in enumerate((7.0, 16.0)):
        events += [(t, b1, i), (t + 4, b2, i), (t + 8, b3, i), (t + 12, b4, i)]
    for i in range(A_UNITS):
        t1 = 6.4 * (i + 1)
        t2 = max(t1 + 6.0, 20.0 + 4.7 * (i + 1))
        events += [(t1, a1, i), (t2, a2, i), (t2 + 3.5, a3, i), (t2 + 7.0, a4, i)]
        if i + DEPTH < A_UNITS:
            events += [(t1, a0, i + DEPTH)]
    for i, step in enumerate((v0, v1, v2, v3, v4, v5)):
        events += [(20.0 + 4.0 * i, step, None)]
    for _, step, index in sorted(events, key=lambda e: e[0]):
        step() if index is None else step(index)

    for i in range(4):
        left_copy(i).wait_send()
        right_copy(i).wait_send()

    def wait_sent(name):
        for condition, make, operands in started.values():
            if condition == name:
                make(*operands).wait_send()

    wait_sent(EVERY)
    pl.when(inner)(lambda: wait_sent(INNER))
    pl.when(outer)(lambda: wait_sent(OUTER))

    for m in range(MICRO):

        @pl.when(section == 0)
        def _():
            x_copy(m).wait_send()

        @pl.when(section == 1)
        def _():
            g_copy(m).wait_send()


def settle(vec, *refs):
    arrays, narrow, wide, sems = refs[:6], refs[6:10], refs[10:16], refs[16]
    copies = [pltpu.make_async_copy(a, w, sems.at[i]) for i, (a, w) in enumerate(zip(arrays, wide))]
    for item in copies:
        item.start()
    place = lax.axis_index("dp")
    near = pltpu.roll(vec[...], (16 - place) % 16 * PART, 1)
    for i in range(3):
        narrow[i][...] = near[i : i + 1, :PART]
    far = pltpu.roll(vec[...], (4 - place % 4) % 4 * (4 * PART), 1)
    row = lax.broadcasted_iota(jnp.int32, far.shape, 0)
    mine = jnp.sum(jnp.where(row == 3 + place // 4, far, 0.0), axis=0, keepdims=True)
    narrow[3][...] = mine[:, : 4 * PART]
    for item in copies:
        item.wait()


def layer_device(
    inputs, cotangent, lengths, gain_one, w_qkv, w_out, gain_two, w_up, b_up, w_down, b_down
):
    y, d_state, qkv, out, up, down, vec = pl.pallas_call(
        kernel,
        out_shape=[jax.ShapeDtypeStruct(s, d) for s, d in OUT.values()],
        in_specs=list(IN.values()),
        out_specs=[VMEM] * len(OUT),
        scratch_shapes=[pltpu.VMEM(s, d) for s, d in SCRATCH.values()]
        + [pltpu.SemaphoreType.DMA(s) for s in SEMS.values()],
        compiler_params=pltpu.CompilerParams(
            collective_id=0, has_side_effects=True, vmem_limit_bytes=60 * 2**20
        ),
        name="layers",
    )(
        inputs.reshape(ROWS, D), cotangent.reshape(ROWS, D), lengths[:, 0], gain_one, w_qkv[0],
        w_out[0], gain_two, w_up[0], b_up, w_down[0], b_down,
    )
    totals = pl.pallas_call(
        settle,
        out_shape=[
            jax.ShapeDtypeStruct((1, PART), F32),
            jax.ShapeDtypeStruct((1, PART), F32),
            jax.ShapeDtypeStruct((1, PART), F32),
            jax.ShapeDtypeStruct((1, 4 * PART), F32),
        ]
        + [jax.ShapeDtypeStruct(s, d) for s, d in list(OUT.values())[:6]],
        in_specs=[VMEM] * 7,
        out_specs=[VMEM] * 4 + [ANY] * 6,
        scratch_shapes=[pltpu.SemaphoreType.DMA((6,))],
        name="settle",
    )(vec, y, d_state, qkv, out, up, down)
    gain_a, gain_b, bias_down, bias_up, y, d_state, qkv, out, up, down = totals
    return (
        y.reshape(1, MICRO, SLOT, D),
        d_state.reshape(1, MICRO, SLOT, D),
        gain_a,
        qkv[None],
        out[None],
        gain_b,
        up[None],
        bias_up,
        down[None],
        bias_down,
    )


def solution(mesh):
    placed = (
        P(None, "dp", None),
        P(None, "dp", None),
        P(None, "dp", None),
        P("section", None),
        P("section", None, None),
        P("section", None, None),
        P("section", None),
        P("section", None, None),
        P("section", None),
        P("section", None, None),
        P("section", None),
    )
    return jax.shard_map(
        layer_device if mesh.shape["dp"] == 16 else plain_device,
        mesh=mesh,
        in_specs=placed,
        out_specs=(
            P("section", None, "dp", None),
            P("section", None, "dp", None),
            P("section", "dp"),
            P("section", "dp", None),
            P("section", "dp", None),
            P("section", "dp"),
            P("section", "dp", None),
            P("section", "dp"),
            P("section", "dp", None),
            P("section", "dp"),
        ),
        check_vma=False,
    )
```

```python
from functools import partial
import math

from types import SimpleNamespace

import jax
import jax.numpy as jnp
from jax import lax
from jax.experimental import pallas as pl
from jax.experimental.pallas import tpu as pltpu
from jax.sharding import PartitionSpec as P

D = 768
FF = 3072
HEADS = 12
HEAD_DIM = 64
BLOCK = 16
SEGS = 3
SEQ_TOK = 64
EPSILON = 1e-05

F32 = jnp.float32
BF16 = jnp.bfloat16
MESH = pl.DeviceIdType.MESH
MICRO = 2
SLOT = 2 * SEQ_TOK
ROWS = MICRO * SLOT
PAIRS = HEADS // 2
LANES = 128
PART = 48
UNITS = 12
WIDE = 768
SCALE = HEAD_DIM ** (-0.5)

UNIT_LEFT = (0, 1, 2, 3, 4, 4, 4, 4, 5, 6, 6, 6)
UNIT_RIGHT = (0, 0, 0, 0, 1, 2, 3, 4, 5, 6, 7, 8)
LEFTS = 7
RIGHTS = 9


def dot(a, b):
    return jnp.dot(a, b, preferred_element_type=F32)


def dot_nt(a, b):
    return lax.dot_general(a, b, (((1,), (1,)), ((), ())), preferred_element_type=F32)


def dot_tn(a, b):
    return lax.dot_general(a, b, (((0,), (0,)), ((), ())), preferred_element_type=F32)


def normalize(values):
    centred = values - jnp.mean(values, axis=-1, keepdims=True)
    inverse = lax.rsqrt(jnp.mean(centred * centred, axis=-1, keepdims=True) + EPSILON)
    return centred * inverse, inverse


def normal_back(d_normed, normed, inverse):
    return inverse * (
        d_normed
        - jnp.mean(d_normed, axis=-1, keepdims=True)
        - normed * jnp.mean(d_normed * normed, axis=-1, keepdims=True)
    )


def token_tables(token, first, second):
    one = (token >= first).astype(jnp.int32)
    two = (token >= first + second).astype(jnp.int32)
    return one + two, token - one * first - two * second


def swap_halves(values):
    lane = lax.broadcasted_iota(jnp.int32, values.shape, 1)
    low = (lane % HEAD_DIM) < HEAD_DIM // 2
    up = pltpu.roll(values, LANES - HEAD_DIM // 2, 1)
    down = pltpu.roll(values, HEAD_DIM // 2, 1)
    return jnp.where(low, up, down)


def head_masked(pair):
    lane = lax.broadcasted_iota(jnp.int32, pair.shape, 1)
    zero = jnp.zeros_like(pair)
    return jnp.concatenate(
        [jnp.where(lane < HEAD_DIM, pair, zero), jnp.where(lane < HEAD_DIM, zero, pair)], axis=0
    )


def build_tables(lengths, cos_t, sin_t, mask_t):
    for m in range(MICRO):
        first, second = lengths[m, 0], lengths[m, 1]
        row = lax.broadcasted_iota(jnp.int32, (SLOT, LANES), 0)
        col = lax.broadcasted_iota(jnp.int32, (SLOT, LANES), 1)
        doc_r, pos_r = token_tables(row % SEQ_TOK, first, second)
        doc_c, pos_c = token_tables(col % SEQ_TOK, first, second)
        block_r, block_c = pos_r // BLOCK, pos_c // BLOCK
        noisy_r, noisy_c = row < SEQ_TOK, col < SEQ_TOK
        same = (doc_r == doc_c) & (doc_r < SEGS - 1)
        ruling = (noisy_r & noisy_c & (block_r == block_c)) | (
            jnp.logical_not(noisy_c)
            & (
                (noisy_r & (block_c < block_r))
                | (jnp.logical_not(noisy_r) & (block_c <= block_r))
            )
        )
        allowed = (same & ruling) | (row == col)
        mask_t[m] = jnp.where(allowed, 1.0, 0.0)
        half = HEAD_DIM // 2
        frequency = jnp.exp((col % half).astype(F32) * (-2.0 * math.log(10000.0) / HEAD_DIM))
        angle = pos_r.astype(F32) * frequency
        sign = jnp.where((col % HEAD_DIM) < half, -1.0, 1.0)
        cos_t[m] = jnp.cos(angle)
        sin_t[m] = jnp.sin(angle) * sign


def rotate_pair(values, cosine, sine):
    return values * cosine + swap_halves(values) * sine


def gelu_both(v):
    c = math.sqrt(2.0 / math.pi)
    square = v * v
    t = jnp.tanh(c * (v + 0.044715 * (v * square)))
    half = 0.5 * (1.0 + t)
    slope = half + (0.5 * c) * v * (1.0 - t * t) * (1.0 + (3.0 * 0.044715) * square)
    return v * half, slope


def forward(R, m, waits):
    rows = pl.ds(pl.multiple_of(m * SLOT, SLOT), SLOT)
    lane = lax.broadcasted_iota(jnp.int32, (SLOT, LANES), 1)
    normed, inverse = normalize(R.x[rows, :].astype(F32))
    R.normed[rows, :] = normed
    R.inv[rows, :] = jnp.broadcast_to(inverse, (SLOT, LANES))
    entry = (normed * R.gain_a[...]).astype(BF16)
    R.entry[rows, :] = entry
    waits(0)
    cosine, sine = R.cos[m], R.sin[m]
    for t in range(9):
        joined = dot(entry, R.w_qkv[:, t * 256 : (t + 1) * 256])
        kept = (R.q, R.k, R.v)[t // 3]
        for j in range(2):
            at = (t * 256 + j * LANES) % D
            piece = joined[:, j * LANES : (j + 1) * LANES]
            if t < 6:
                piece = rotate_pair(piece, cosine, sine)
            kept[rows, at : at + LANES] = piece.astype(BF16)
    keep = jnp.concatenate([R.mask[m], R.mask[m]], axis=0) > 0.5
    for p in range(PAIRS):
        lanes = pl.ds(p * LANES, LANES)
        q2 = head_masked(R.q[rows, lanes])
        raw = dot_nt(q2, R.k[rows, lanes]) * SCALE
        scores = jnp.where(keep, raw, -1e30)
        exponent = jnp.exp(scores - jnp.max(scores, axis=-1, keepdims=True))
        probs = exponent / jnp.sum(exponent, axis=-1, keepdims=True)
        R.probs[m * PAIRS + p] = probs
        pv = dot(probs.astype(BF16), R.v[rows, lanes])
        R.mixed[rows, lanes] = jnp.where(lane < HEAD_DIM, pv[:SLOT], pv[SLOT:]).astype(BF16)
    waits(1)
    hidden = R.x[rows, :].astype(F32) + dot(R.mixed[rows, :], R.w_out[...])
    R.hidden[rows, :] = hidden
    normed, inverse = normalize(hidden)
    R.normed2[rows, :] = normed
    R.inv2[rows, :] = jnp.broadcast_to(inverse, (SLOT, LANES))
    entry2 = (normed * R.gain_b[...]).astype(BF16)
    R.entry2[rows, :] = entry2
    waits(2)
    for t in range(FF // 256):
        cols = pl.ds(t * 256, 256)
        inner = dot(entry2, R.w_up[:, cols]) + R.b_up[:, cols]
        act, slope = gelu_both(inner)
        R.act[rows, cols] = act.astype(BF16)
        R.slope[rows, cols] = slope * R.slope[rows, cols]
    waits(3)
    R.y[rows, :] = (
        R.hidden[rows, :] + dot(R.act[rows, :], R.w_down[...]) + R.b_down[...]
    ).astype(BF16)


def feed_inner_matmul(R, t):
    g = R.right[0]
    for j in range(3):
        cols = pl.ds(t * WIDE + j * 256, 256)
        R.slope[:, cols] = R.slope[:, cols] * dot_nt(g, R.w_down[cols, :])


def feed_inner(R, t):
    for j in range(3):
        d_inner = R.slope[:, t * WIDE + j * 256 : t * WIDE + (j + 1) * 256].astype(BF16)
        R.right[1 + t, :, j * 256 : (j + 1) * 256] = d_inner
        R.vec[3 + t : 4 + t, j * 256 : (j + 1) * 256] = jnp.sum(
            d_inner.astype(F32), axis=0, keepdims=True
        )


def feed_entry(R, t):
    rows = pl.ds(t * 256, 256)
    total = dot_nt(R.right[1], R.w_up[rows, 0:WIDE])
    for j in range(1, 4):
        total += dot_nt(R.right[1 + j], R.w_up[rows, j * WIDE : (j + 1) * WIDE])
    R.hidden[:, rows] = total


def feed_norm(R):
    R.vec[2:3, :] = jnp.sum(R.right[0].astype(F32), axis=0, keepdims=True)
    gain = jnp.zeros((1, D), F32)
    for m in range(MICRO):
        rows = pl.ds(m * SLOT, SLOT)
        d_entry = R.hidden[rows, :]
        normed = R.normed2[rows, :]
        gain += jnp.sum(d_entry * normed, axis=0, keepdims=True)
        d_hidden = R.right[0, rows, :].astype(F32) + normal_back(
            d_entry * R.gain_b[...], normed, R.inv2[rows, 0:1]
        )
        R.hidden[rows, :] = d_hidden
        R.right[5, rows, :] = d_hidden.astype(BF16)
    R.vec[1:2, :] = gain


def attention_mixed(R):
    R.d_mixed[...] = dot_nt(R.right[5], R.w_out[...]).astype(BF16)


def attention_pairs(R, m, t):
    rows = pl.ds(m * SLOT, SLOT)
    cosine, sine = R.cos[m], -R.sin[m]
    for p in (2 * t, 2 * t + 1):
        lanes = pl.ds(p * LANES, LANES)
        dm2 = head_masked(R.d_mixed[rows, lanes])
        q2 = head_masked(R.q[rows, lanes])
        k2 = head_masked(R.k[rows, lanes])
        probs = R.probs[m * PAIRS + p]
        d_probs = dot_nt(dm2, R.v[rows, lanes])
        d_scores = (
            probs * (d_probs - jnp.sum(probs * d_probs, axis=-1, keepdims=True))
        ).astype(BF16)
        d_values = dot_tn(probs.astype(BF16), dm2)
        side = jnp.concatenate([d_scores[:SLOT], d_scores[SLOT:]], axis=1)
        d_query = dot(side, k2) * SCALE
        d_keys = dot_tn(d_scores, q2) * SCALE
        R.right[6, rows, lanes] = rotate_pair(d_query, cosine, sine).astype(BF16)
        R.right[7, rows, lanes] = rotate_pair(d_keys, cosine, sine).astype(BF16)
        R.right[8, rows, lanes] = d_values.astype(BF16)


def attention_entry(R, m):
    rows = pl.ds(m * SLOT, SLOT)
    d_entry = jnp.zeros((SLOT, D), F32)
    for t in range(3):
        d_entry += dot_nt(R.right[6 + t, rows, :], R.w_qkv[:, t * WIDE : (t + 1) * WIDE])
    normed = R.normed[rows, :]
    R.vec[0:1, :] = R.vec[0:1, :] + jnp.sum(d_entry * normed, axis=0, keepdims=True)
    R.d_state[rows, :] = (
        R.hidden[rows, :] + normal_back(d_entry * R.gain_a[...], normed, R.inv[rows, 0:1])
    ).astype(BF16)


def turn_lefts(R, core):
    def place(kind, owner_core, chip, block):
        x, z = chip % 2, chip // 2

        @pl.when(core == owner_core)
        def _():
            R.left[kind, x * 4 + z] = block

        @pl.when(core != owner_core)
        def _():
            R.left_out[kind, x * 4 + z] = block

    for kind, factor in ((4, R.entry2), (5, R.mixed), (6, R.entry)):
        turned = factor[...].T
        for d in range(16):
            place(kind, d % 2, d // 2, turned[d * PART : (d + 1) * PART, :])
    for d4 in range(4):
        turned = R.act[:, d4 * 768 : (d4 + 1) * 768].T
        for e in range(4):
            d = d4 * 4 + e
            for i in range(4):
                at = e * 192 + i * PART
                place(i, d % 2, d // 2, turned[at : at + PART, :])


def passed_along(block, axis, distance):
    devices = range(lax.axis_size(axis))
    route = [(i - distance, i) for i in devices if i - distance in devices]
    return lax.ppermute(block, axis, route)


def row_tables(lengths_row):
    steps_all = jnp.arange(SEQ_TOK, dtype=jnp.int32)
    bounds = jnp.cumsum(lengths_row)
    passed = (steps_all[:, None] >= bounds[None, :]).astype(jnp.int32)
    document = jnp.sum(passed, axis=1)
    offset = jnp.sum(passed * lengths_row[None, :], axis=1)
    position = steps_all - offset
    inside = document < SEGS - 1
    document_rows = jnp.concatenate([document, document])
    position_rows = jnp.concatenate([position, position])
    inside_rows = jnp.concatenate([inside, inside])
    copies = jnp.concatenate([jnp.zeros((SEQ_TOK,), jnp.int32), jnp.ones((SEQ_TOK,), jnp.int32)])
    blocks = position_rows // BLOCK
    query_block = blocks[:, None]
    key_block = blocks[None, :]
    noisy_query = (copies == 0)[:, None]
    noisy_key = (copies == 0)[None, :]
    ruling = jnp.where(
        noisy_query,
        jnp.where(noisy_key, key_block == query_block, key_block < query_block),
        jnp.logical_and(jnp.logical_not(noisy_key), key_block <= query_block),
    )
    same_doc = (
        (document_rows[:, None] == document_rows[None, :])
        & inside_rows[:, None]
        & inside_rows[None, :]
    )
    indices = jnp.arange(2 * SEQ_TOK, dtype=jnp.int32)
    allowed = same_doc & ruling | (indices[:, None] == indices[None, :])
    frequency = jnp.exp(
        jnp.arange(HEAD_DIM // 2).astype(jnp.float32) * (-2.0 * math.log(10000.0) / HEAD_DIM)
    )
    angles = position_rows.astype(jnp.float32)[:, None] * frequency[None, :]
    return (allowed, jnp.cos(angles), jnp.sin(angles))


def rotate(tensor, cosine, sine):
    halfway = tensor.shape[-1] // 2
    upper_part = tensor[..., :halfway]
    lower_part = tensor[..., halfway:]
    cos_rows = cosine[:, None, :]
    sin_rows = sine[:, None, :]
    return jnp.concatenate(
        [
            upper_part * cos_rows - lower_part * sin_rows,
            upper_part * sin_rows + lower_part * cos_rows,
        ],
        axis=-1,
    )


def unrotate(gradient, cosine, sine):
    halfway = gradient.shape[-1] // 2
    upper_part = gradient[..., :halfway]
    lower_part = gradient[..., halfway:]
    cos_rows = cosine[:, None, :]
    sin_rows = sine[:, None, :]
    return jnp.concatenate(
        [
            upper_part * cos_rows + lower_part * sin_rows,
            lower_part * cos_rows - upper_part * sin_rows,
        ],
        axis=-1,
    )


def plain_normalize(values):
    centred = values - jnp.mean(values, axis=-1, keepdims=True)
    inverse = lax.rsqrt(jnp.mean(centred * centred, axis=-1, keepdims=True) + EPSILON)
    return (centred * inverse, inverse)


def plain_normal_back(d_normed, normed, inverse):
    return inverse * (
        d_normed
        - jnp.mean(d_normed, axis=-1, keepdims=True)
        - normed * jnp.mean(d_normed * normed, axis=-1, keepdims=True)
    )


def scores_of(query, keyset, allowed):
    raw = jnp.einsum(
        "qhd,khd->hqk", query, keyset, preferred_element_type=jnp.float32
    ) * HEAD_DIM ** (-0.5)
    return jnp.where(allowed[None], raw, -1e30)


def forward_pass(state, lengths_row, weights):
    gain_a, w_qkv, w_out, gain_b, w_up, b_up, w_down, b_down = weights
    allowed, cosine, sine = row_tables(lengths_row)
    count = state.shape[0]
    widened = state.astype(jnp.float32)
    normed, inverse = plain_normalize(widened)
    entry = (normed * gain_a).astype(jnp.bfloat16)
    joined = jnp.dot(entry, w_qkv, preferred_element_type=jnp.float32)
    query = rotate(joined[:, :D].reshape(count, HEADS, HEAD_DIM), cosine, sine).astype(jnp.bfloat16)
    keyset = rotate(joined[:, D : 2 * D].reshape(count, HEADS, HEAD_DIM), cosine, sine).astype(
        jnp.bfloat16
    )
    valueset = joined[:, 2 * D :].reshape(count, HEADS, HEAD_DIM).astype(jnp.bfloat16)
    scores = scores_of(query, keyset, allowed)
    highest = jnp.max(scores, axis=-1, keepdims=True)
    exponent = jnp.exp(scores - highest)
    totals = jnp.sum(exponent, axis=-1, keepdims=True)
    soft_low = (exponent / totals).astype(jnp.bfloat16)
    log_total = highest + jnp.log(totals)
    mixed = (
        jnp.einsum("hqk,khd->qhd", soft_low, valueset, preferred_element_type=jnp.float32)
        .reshape(count, D)
        .astype(jnp.bfloat16)
    )
    hidden = widened + jnp.dot(mixed, w_out, preferred_element_type=jnp.float32)
    normed_two, inverse_two = plain_normalize(hidden)
    entry_two = (normed_two * gain_b).astype(jnp.bfloat16)
    inner = jnp.dot(entry_two, w_up, preferred_element_type=jnp.float32) + b_up
    activated = jax.nn.gelu(inner, approximate=True).astype(jnp.bfloat16)
    result = (
        hidden + jnp.dot(activated, w_down, preferred_element_type=jnp.float32) + b_down
    ).astype(jnp.bfloat16)
    saved = (
        normed,
        inverse,
        entry,
        query,
        keyset,
        valueset,
        log_total,
        mixed,
        normed_two,
        inverse_two,
        entry_two,
        inner,
        activated,
    )
    return (result, saved)


def forward_blank(state, lengths_row, weights):
    count = state.shape[0]
    rows_f = jnp.zeros((count, D), jnp.float32)
    rows_b = jnp.zeros((count, D), jnp.bfloat16)
    column = jnp.zeros((count, 1), jnp.float32)
    heads_b = jnp.zeros((count, HEADS, HEAD_DIM), jnp.bfloat16)
    saved = (
        rows_f,
        column,
        rows_b,
        heads_b,
        heads_b,
        heads_b,
        jnp.zeros((HEADS, count, 1), jnp.float32),
        rows_b,
        rows_f,
        column,
        rows_b,
        jnp.zeros((count, FF), jnp.float32),
        jnp.zeros((count, FF), jnp.bfloat16),
    )
    return (jnp.zeros_like(state), saved)


def settle_plain(index, group):
    return group


def backward_core(saved, incoming, lengths_row, weights, settle):
    gain_a, w_qkv, w_out, gain_b, w_up, b_up, w_down, b_down = weights
    (
        normed,
        inverse,
        entry,
        query,
        keyset,
        valueset,
        log_total,
        mixed,
        normed_two,
        inverse_two,
        entry_two,
        inner,
        activated,
    ) = saved
    allowed, cosine, sine = row_tables(lengths_row)
    count = incoming.shape[0]
    upper = incoming.astype(jnp.float32)
    grad_down = jnp.einsum("rf,rd->fd", activated, incoming, preferred_element_type=jnp.float32)
    grad_bias_down = jnp.sum(upper, axis=0)
    d_activated = jnp.einsum("rd,fd->rf", incoming, w_down, preferred_element_type=jnp.float32)
    _, gelu_pull = jax.vjp(partial(jax.nn.gelu, approximate=True), inner)
    d_inner = gelu_pull(d_activated)[0].astype(jnp.bfloat16)
    grad_up = jnp.einsum("rd,rf->df", entry_two, d_inner, preferred_element_type=jnp.float32)
    grad_bias_up = jnp.sum(d_inner, axis=0, dtype=jnp.float32)
    d_entry_two = jnp.einsum("rf,df->rd", d_inner, w_up, preferred_element_type=jnp.float32)
    grad_gain_b = jnp.sum(d_entry_two * normed_two, axis=0)
    feed_group = settle(0, (grad_gain_b, grad_up, grad_bias_up, grad_down, grad_bias_down))
    d_hidden = upper + plain_normal_back(d_entry_two * gain_b, normed_two, inverse_two)
    d_branch = d_hidden.astype(jnp.bfloat16)
    grad_out = jnp.einsum("rd,re->de", mixed, d_branch, preferred_element_type=jnp.float32)
    d_mixed = (
        jnp.einsum("re,de->rd", d_branch, w_out, preferred_element_type=jnp.float32)
        .astype(jnp.bfloat16)
        .reshape(count, HEADS, HEAD_DIM)
    )
    scores = scores_of(query, keyset, allowed)
    probs = jnp.exp(scores - log_total)
    d_probs = jnp.einsum("qhd,khd->hqk", d_mixed, valueset, preferred_element_type=jnp.float32)
    d_scores = (probs * (d_probs - jnp.sum(probs * d_probs, axis=-1, keepdims=True))).astype(
        jnp.bfloat16
    )
    d_values = jnp.einsum(
        "hqk,qhd->khd", probs.astype(jnp.bfloat16), d_mixed, preferred_element_type=jnp.float32
    )
    scaling = HEAD_DIM ** (-0.5)
    d_query = (
        jnp.einsum("hqk,khd->qhd", d_scores, keyset, preferred_element_type=jnp.float32) * scaling
    )
    d_keys = (
        jnp.einsum("hqk,qhd->khd", d_scores, query, preferred_element_type=jnp.float32) * scaling
    )
    d_joined = jnp.concatenate(
        [
            unrotate(d_query, cosine, sine).reshape(count, D),
            unrotate(d_keys, cosine, sine).reshape(count, D),
            d_values.reshape(count, D),
        ],
        axis=1,
    ).astype(jnp.bfloat16)
    grad_qkv = jnp.einsum("rd,re->de", entry, d_joined, preferred_element_type=jnp.float32)
    d_entry = jnp.einsum("re,de->rd", d_joined, w_qkv, preferred_element_type=jnp.float32)
    grad_gain_a = jnp.sum(d_entry * normed, axis=0)
    attn_group = settle(1, (grad_gain_a, grad_qkv, grad_out))
    d_state = (d_hidden + plain_normal_back(d_entry * gain_a, normed, inverse)).astype(jnp.bfloat16)
    return (d_state, tuple(attn_group) + tuple(feed_group))


def backward_pass(saved, incoming, lengths_row, weights):
    return backward_core(saved, incoming, lengths_row, weights, settle_plain)


def backward_blank(saved, incoming, lengths_row, weights):
    return (
        jnp.zeros_like(incoming),
        tuple((jnp.zeros(item.shape, jnp.float32) for item in weights)),
    )


def keep_at(place, active, stack, leaf):
    current = lax.dynamic_index_in_dim(stack, place, 0, keepdims=False)
    return lax.dynamic_update_index_in_dim(stack, jnp.where(active, leaf, current), place, 0)


def reduce_total(grads):
    (
        grad_gain_a,
        grad_qkv,
        grad_out,
        grad_gain_b,
        grad_up,
        grad_bias_up,
        grad_down,
        grad_bias_down,
    ) = grads
    return (
        lax.psum_scatter(grad_gain_a[None], "dp", scatter_dimension=1, tiled=True),
        lax.psum_scatter(grad_qkv[None], "dp", scatter_dimension=1, tiled=True),
        lax.psum_scatter(grad_out[None], "dp", scatter_dimension=1, tiled=True),
        lax.psum_scatter(grad_gain_b[None], "dp", scatter_dimension=1, tiled=True),
        lax.psum_scatter(grad_up[None], "dp", scatter_dimension=1, tiled=True),
        lax.psum_scatter(grad_bias_up[None], "dp", scatter_dimension=1, tiled=True),
        lax.psum_scatter(grad_down[None], "dp", scatter_dimension=1, tiled=True),
        lax.psum_scatter(grad_bias_down[None], "dp", scatter_dimension=1, tiled=True),
    )


def plain_device(
    inputs, cotangent, lengths, gain_one, w_qkv, w_out, gain_two, w_up, b_up, w_down, b_down
):
    section = lax.axis_index("section")
    micro = inputs.shape[0]
    weights = (gain_one[0], w_qkv[0], w_out[0], gain_two[0], w_up[0], b_up[0], w_down[0], b_down[0])
    slot_lengths = lengths[:, 0]
    arrived = jnp.zeros(inputs.shape[1:], jnp.bfloat16)
    results = jnp.zeros(inputs.shape, jnp.bfloat16)
    stored = ()
    for tick in range(micro + 1):
        number = tick - section
        active = jnp.logical_and(number >= 0, number < micro)
        place = jnp.clip(number, 0, micro - 1)
        layer_in = jnp.where(section == 0, inputs[min(tick, micro - 1)], arrived)
        lengths_row = lax.dynamic_index_in_dim(slot_lengths, place, 0, keepdims=False)
        result, saved = lax.cond(
            active, forward_pass, forward_blank, layer_in, lengths_row, weights
        )
        if tick == 0:
            stored = jax.tree.map(lambda leaf: jnp.zeros((micro,) + leaf.shape, leaf.dtype), saved)
        stored = jax.tree.map(partial(keep_at, place, active), stored, saved)
        results = keep_at(place, active, results, result)
        if tick < micro:
            arrived = passed_along(result, "section", 1)
    back_arrived = jnp.zeros(inputs.shape[1:], jnp.bfloat16)
    grads_in = jnp.zeros(inputs.shape, jnp.bfloat16)
    totals = tuple((jnp.zeros(item.shape, jnp.float32) for item in weights))
    reduced_sums = ()
    for tick in range(micro + 1):
        number = tick - (1 - section)
        active = jnp.logical_and(number >= 0, number < micro)
        place = jnp.clip(number, 0, micro - 1)
        incoming = jnp.where(section == 1, cotangent[min(tick, micro - 1)], back_arrived)
        saved = jax.tree.map(
            lambda stack: lax.dynamic_index_in_dim(stack, place, 0, keepdims=False), stored
        )
        lengths_row = lax.dynamic_index_in_dim(slot_lengths, place, 0, keepdims=False)
        d_state, grads = lax.cond(
            active, backward_pass, backward_blank, saved, incoming, lengths_row, weights
        )
        totals = tuple((earlier + later for earlier, later in zip(totals, grads)))
        grads_in = keep_at(place, active, grads_in, d_state)
        if tick < micro:
            back_arrived = passed_along(d_state, "section", -1)
    reduced_sums = reduce_total(totals)
    sum_gain_a, sum_qkv, sum_out, sum_gain_b, sum_up, sum_bias_up, sum_down, sum_bias_down = (
        reduced_sums
    )
    return (
        results[None],
        grads_in[None],
        sum_gain_a,
        sum_qkv,
        sum_out,
        sum_gain_b,
        sum_up,
        sum_bias_up,
        sum_down,
        sum_bias_down,
    )


VMEM = pl.BlockSpec(memory_space=pltpu.VMEM)
SMEM = pl.BlockSpec(memory_space=pltpu.SMEM)
ANY = pl.BlockSpec(memory_space=pl.ANY)
IN = dict(
    inputs=ANY, cotangent=ANY, lengths=SMEM, gain_a=VMEM, w_qkv_in=ANY, w_out_in=ANY,
    gain_b=VMEM, w_up_in=ANY, b_up=VMEM, w_down_in=ANY, b_down=VMEM,
)
OUT = dict(
    y=((ROWS, D), BF16),
    d_state=((ROWS, D), BF16),
    sum_qkv=((PART, 3 * D), F32),
    sum_out=((PART, D), F32),
    sum_up=((PART, FF), F32),
    sum_down=((4 * PART, D), F32),
    vec_sum=((8, WIDE), F32),
)
SHARED = 4
Z_UNITS = UNITS - 1
X_UNITS = UNITS - SHARED
ORDER = (
  (
    (
        (),
        (303, 302, 301,),
        (),
        (),
        (),
        (),
        (),
        (),
        (),
        (),
        (19, 18, 17, 16,),
        (23, 22, 21, 20,),
        (27, 26, 25, 24,),
        (),
        (),
        (),
        (),
        (),
        (),
        (107, 106, 105,),
        (111, 110, 109,),
        (115, 114, 113,),
        (),
        (),
        (),
        (600,),
        (),
        (),
        (),
        (601, 119, 602, 31, 118, 30, 117, 29, 28, 123, 122, 121, 35, 127, 126, 125, 34, 33, 32, 39, 38, 37, 36, 400, 204, 605, 131, 43, 208, 130, 42, 212, 129, 41, 40, 135, 47, 134, 133, 139, 138, 137, 46, 45, 44, 216, 500, 143, 142, 141, 147, 146, 145, 220, 224, 228, 232, 236, 240, 244,),
    ),
    (
        (),
        (),
        (),
        (),
        (),
        (),
        (),
        (),
        (),
        (),
        (19, 18, 16, 17,),
        (23, 22, 20, 21,),
        (27, 26, 24, 25,),
        (),
        (),
        (),
        (),
        (),
        (),
        (),
        (),
        (),
        (),
        (),
        (),
        (600,),
        (),
        (),
        (),
        (303, 601, 302, 602, 31, 30, 28, 29, 107, 35, 34, 603, 32, 33, 106, 39, 38, 36, 37, 300, 400, 111, 604, 110, 104, 205, 115, 114, 108, 209, 112, 213, 43, 42, 119, 118, 40, 123, 122, 127, 126, 41, 131, 47, 46, 116, 44, 130, 45, 500, 217, 135, 120, 221, 124, 225, 128, 229, 132, 134, 139, 138, 143, 233, 142, 136, 237, 140, 147, 146, 241, 144, 245,),
    ),
  ),
  (
    (
        (),
        (600, 303, 302, 301,),
        (19, 18, 17, 16,),
        (),
        (),
        (),
        (601,),
        (),
        (),
        (),
        (107, 106, 105,),
        (602, 111, 110, 109,),
        (115, 114, 113, 23, 119, 22, 21, 20, 118, 117, 605, 27, 123, 26, 25, 24, 122, 121, 400, 31, 127, 30, 126, 29, 28, 125, 500, 204, 35, 131, 34, 130, 33, 32, 129, 39, 135, 208, 212, 216, 220, 38, 134, 37, 36, 133, 43, 139, 224, 228, 42, 138, 232, 41, 40, 137, 47, 143, 46, 142, 236, 45, 141, 44, 147, 146, 145, 240, 244,),
    ),
    (
        (),
        (600,),
        (19, 18, 16, 17,),
        (),
        (),
        (),
        (),
        (601,),
        (),
        (),
        (),
        (),
        (602, 603, 604, 23, 22, 20, 21, 303, 302, 107, 106, 27, 26, 24, 25, 300, 111, 110, 115, 114, 400, 119, 118, 123, 122, 31, 104, 30, 28, 29, 500, 205, 127, 108, 209, 126, 112, 213, 35, 34, 32, 33, 116, 217, 131, 120, 221, 124, 225, 130, 128, 39, 135, 38, 36, 37, 229, 43, 132, 134, 139, 42, 233, 40, 41, 47, 138, 136, 237, 143, 46, 142, 44, 45, 140, 241, 147, 146, 144, 245,),
    ),
  ),
)

SCRATCH = dict(
    w_qkv=((D, 3 * D), BF16),
    w_out=((D, D), BF16),
    w_up=((D, FF), BF16),
    w_down=((FF, D), BF16),
    x=((ROWS, D), BF16),
    cos=((MICRO, SLOT, LANES), F32),
    sin=((MICRO, SLOT, LANES), F32),
    mask=((MICRO, SLOT, SLOT), F32),
    normed=((ROWS, D), F32),
    inv=((ROWS, LANES), F32),
    entry=((ROWS, D), BF16),
    q=((ROWS, D), BF16),
    k=((ROWS, D), BF16),
    v=((ROWS, D), BF16),
    probs=((MICRO * PAIRS, 2 * SLOT, SLOT), F32),
    mixed=((ROWS, D), BF16),
    hidden=((ROWS, D), F32),
    normed2=((ROWS, D), F32),
    inv2=((ROWS, LANES), F32),
    entry2=((ROWS, D), BF16),
    act=((ROWS, FF), BF16),
    slope=((ROWS, FF), F32),
    d_mixed=((ROWS, D), BF16),
    d_entry=((ROWS, D), F32),
    right=((RIGHTS, ROWS, WIDE), BF16),
    right_in=((RIGHTS, ROWS, WIDE), BF16),
    left_x=((2, SHARED - 1, 4, PART, ROWS), BF16),
    right_x=((2, ROWS, WIDE), BF16),
    left=((LEFTS, 8, PART, ROWS), BF16),
    left_out=((LEFTS, 8, PART, ROWS), BF16),
    left_in=((LEFTS, 8, PART, ROWS), BF16),
    grad=((UNITS, 2, 4, PART, WIDE), BF16),
    ax=((X_UNITS, 4, PART, WIDE), BF16),
    az=((Z_UNITS, 5, PART, WIDE), BF16),
    bz=((5, 2, PART, WIDE), BF16),
    bs=((PART, WIDE), BF16),
    bx=((PART, WIDE), BF16),
    vec=((8, WIDE), F32),
    vec_in=((5, 8, WIDE), F32),
    vec_part=((5, 8, WIDE), F32),
)
SEMS = dict(
    load=(5,), ys=(4,), yr=(4,), ls=(4,), lr=(4,), rs=(7,), rr=(7,),
    axs=(X_UNITS, 4), axr=(X_UNITS, 4), azs=(Z_UNITS, 5), azr=(Z_UNITS, 5),
    bzs=(5,), bzr=(5,), bxs=(1,), bxr=(1,), gs=(3, 2), gr=(3, 2), lxs=(2,), lxr=(2,),
    vs=(5,), vr=(5,),
)
LEFT_GROUPS = ((0, 4), (4, 1), (5, 1), (6, 1))
RIGHT_GROUPS = (None, (1, 1), (2, 1), (3, 1), (4, 1), (5, 1), (6, 3))


def kernel(*refs):
    names = (*IN, *OUT, *SCRATCH, *SEMS)
    R = SimpleNamespace(**dict(zip(names, refs)))
    place, section = lax.axis_index("dp"), lax.axis_index("section")
    core, x, z = place % 2, (place // 2) % 2, place // 4
    half = z // 2
    outer = (z == 0) | (z == 3)
    inner = (z == 1) | (z == 2)

    def dp_of(z_, x_, core_):
        return (z_ * 4 + x_ * 2 + core_, section)

    near_core = dp_of(z, x, 1 - core)
    near_x = dp_of(z, 1 - x, core)
    diagonal = dp_of(z, 1 - x, 1 - core)
    near_y = (place, 1 - section)
    near_side = dp_of(half * 2 + 1 - z % 2, x, core)
    near_mid = dp_of(3 - z, x, core)

    owners = [j + half * (3 - 2 * j) for j in range(4)]

    def owner(j):
        return owners[j]

    def copy(src, dst, send, recv, device):
        return pltpu.make_async_remote_copy(
            src_ref=src, dst_ref=dst, send_sem=send, recv_sem=recv,
            device_id=device, device_id_type=MESH,
        )

    weights_in = (R.w_qkv_in, R.w_out_in, R.w_up_in, R.w_down_in)
    weights = (R.w_qkv, R.w_out, R.w_up, R.w_down)
    loads = [
        pltpu.make_async_copy(src, dst, R.load.at[i])
        for i, (src, dst) in enumerate(zip(weights_in, weights))
    ]
    loads[0].start()

    def take(index, src, dst):
        @pl.when(section == index)
        def _():
            pltpu.make_async_copy(src, dst, R.load.at[4]).start()

    def taken(index, src, dst):
        @pl.when(section == index)
        def _():
            pltpu.make_async_copy(src, dst, R.load.at[4]).wait()

    take(0, R.inputs, R.x)
    take(1, R.cotangent, R.right.at[0])

    barrier = pltpu.get_barrier_semaphore()
    for device in (near_core, near_x, diagonal, near_y, near_side):
        pl.semaphore_signal(barrier, inc=1, device_id=device, device_id_type=MESH)

    @pl.when(inner)
    def _():
        pl.semaphore_signal(barrier, inc=1, device_id=near_mid, device_id_type=MESH)

    def all_here():
        pl.when(inner)(lambda: pl.semaphore_wait(barrier, 6))
        pl.when(outer)(lambda: pl.semaphore_wait(barrier, 5))

    build_tables(R.lengths, R.cos, R.sin, R.mask)
    for load in loads[1:]:
        load.start()

    def share(kind, m):
        rows = pl.ds(m * SLOT, SLOT)
        src, dst, device = (
            (R.right.at[0, rows], R.right_in.at[0, rows], near_core),
            (R.right.at[0, rows], R.right_x.at[0, rows], near_x),
            (R.right_x.at[0, rows], R.right_x.at[1, rows], near_core),
        )[kind]
        return copy(src, dst, R.gs.at[kind, m], R.gr.at[kind, m], device)

    def left_x_copy(kind):
        src, device = ((R.left, near_x), (R.left_out, diagonal))[kind]
        src = src.at[pl.ds(1, SHARED - 1), pl.ds((1 - x) * 4, 4)]
        return copy(src, R.left_x.at[kind], R.lxs.at[kind], R.lxr.at[kind], device)

    @pl.when(section == 1)
    def _():
        all_here()
        pltpu.make_async_copy(R.cotangent, R.right.at[0], R.load.at[4]).wait()
        for m in range(MICRO):
            share(0, m).start()
            share(1, m).start()

    def x_copy(m):
        rows = pl.ds(m * SLOT, SLOT)
        return copy(R.y.at[rows], R.x.at[rows], R.ys.at[m], R.yr.at[m], near_y)

    def g_copy(m):
        rows = pl.ds(m * SLOT, SLOT)
        return copy(
            R.d_state.at[rows], R.right.at[0, rows], R.ys.at[2 + m], R.yr.at[2 + m], near_y
        )

    taken(0, R.inputs, R.x)
    @pl.when(section == 0)
    def _():
        R.slope[...] = jnp.ones((ROWS, FF), F32)

    @pl.when(section == 1)
    def _():
        loads[3].wait()
        for t in range(FF // 256):
            cols = pl.ds(t * 256, 256)
            R.slope[:, cols] = dot_nt(R.right[0], R.w_down[cols, :])

    for m in range(MICRO):

        @pl.when(section == 1)
        def _():
            x_copy(m).wait_recv()

        def arrives(n):
            if m == 0 and n < 3:
                loads[n].wait()
            elif m == 0:
                pl.when(section == 0)(lambda: loads[3].wait())

        forward(R, m, arrives)

        @pl.when(section == 0)
        def _():
            if m == 0:
                all_here()
            x_copy(m).start()

    def left_copy(i):
        a, n = LEFT_GROUPS[i]
        rows = pl.ds(a, n)
        return copy(
            R.left_out.at[rows], R.left_in.at[rows], R.ls.at[i], R.lr.at[i], near_core
        )

    def right_copy(i):
        a, n = RIGHT_GROUPS[i]
        rows = pl.ds(a, n)
        return copy(
            R.right.at[rows], R.right_in.at[rows], R.rs.at[i], R.rr.at[i], near_core
        )

    def send_lefts():
        turn_lefts(R, core)
        for i in range(4):
            left_copy(i).start()
        for kind in range(2):
            left_x_copy(kind).start()

    @pl.when(section == 0)
    def _():
        send_lefts()
        for m in range(MICRO):
            g_copy(m).wait_recv()
            share(0, m).start()
            share(1, m).start()


    def weight_unit(u):
        left, right = UNIT_LEFT[u], UNIT_RIGHT[u]
        own = R.left[left].reshape(8 * PART, ROWS)
        other = R.left_in[left].reshape(8 * PART, ROWS)
        total = dot(own, R.right[right]) + dot(other, R.right_in[right])
        R.grad[u] = total.astype(BF16).reshape(2, 4, PART, WIDE)

    def shared_unit(u):
        mine = pl.ds(x * 4, 4)
        factors = (
            (R.left[u, mine], R.right[0]),
            (R.left_in[u, mine], R.right_in[0]),
            (R.left_x[0, u - 1], R.right_x[0]),
            (R.left_x[1, u - 1], R.right_x[1]),
        )
        total = sum(dot(a.reshape(4 * PART, ROWS), b) for a, b in factors)
        R.grad[u, x] = total.astype(BF16).reshape(4, PART, WIDE)

    def place_of(u):
        if u < SHARED:
            return R.sum_down, u * PART, slice(None)
        if u < 8:
            return R.sum_up, 0, slice((u - 4) * WIDE, (u - 3) * WIDE)
        if u == 8:
            return R.sum_out, 0, slice(None)
        return R.sum_qkv, 0, slice((u - 9) * WIDE, (u - 8) * WIDE)

    def add_up(terms, ref, at, first=0, columns=slice(None)):
        def some_rows(r, _):
            rows = pl.ds(pl.multiple_of(r * 16, 16), 16)
            total = sum(array[(*index, rows)].astype(F32) for array, index in terms)
            to = pl.ds(pl.multiple_of(first + r * 16, 16), 16)
            ref[(*at, to, columns)] = total.astype(ref.dtype)
            return 0

        lax.fori_loop(0, PART // 16, some_rows, 0)

    def finish(u, terms):
        ref, first, columns = place_of(u)
        add_up(terms, ref, (), first, columns)

    def start(make, *operands):
        make(*operands).start()

    def ax_copy(u, j):
        i = u - SHARED
        return copy(
            R.grad.at[u, 1 - x, owner(j)], R.ax.at[i, j], R.axs.at[i, j], R.axr.at[i, j], near_x
        )

    def az_copy(u, src, at, slot, device):
        i = u - 1
        return copy(src.at[at], R.az.at[i, slot], R.azs.at[i, slot], R.azr.at[i, slot], device)

    def x_sum(u, j):
        own = (R.grad, (u, x, owner(j)))
        if u < SHARED:
            return [own]
        ax_copy(u, j).wait_recv()
        return [own, (R.ax, (u - SHARED, j))]

    def x_send(is_outer, u, j):
        start(ax_copy, u, j)

    def z_send(is_outer, u, j):
        if is_outer and u < SHARED:
            start(az_copy, u, R.grad, (u, x, owner(j)), j - 1, near_side)
            return
        total = x_sum(u, j)
        if is_outer:
            add_up(total, R.ax, (u - SHARED, j))
            start(az_copy, u, R.ax, (u - SHARED, j), j - 1, near_side)
            return
        slot, device = (j - 1, near_side) if j else (3, near_mid)
        at = (u - 1, slot)
        az_copy(u, R.az, at, slot, device).wait_recv()
        add_up(total + [(R.az, at)], R.az, at)
        if j:
            start(az_copy, u, R.az, at, 6 - j, near_mid)
        else:
            start(az_copy, u, R.az, at, 0, near_side)

    def z_last(is_outer, u, j):
        total = x_sum(u, j)
        for slot, device in ((0, near_side),) if is_outer else ((0, near_side), (4, near_mid)):
            az_copy(u, R.az, (u - 1, slot), slot, device).wait_recv()
            total.append((R.az, (u - 1, slot)))
        finish(u, total)

    def bz_copy(src, at, slot, device):
        return copy(src.at[at], R.bz.at[slot], R.bzs.at[slot], R.bzr.at[slot], device)

    def bx_copy():
        return copy(R.bs, R.bx, R.bxs.at[0], R.bxr.at[0], near_x)

    def bz_send(is_outer, u, j):
        if is_outer:
            start(bz_copy, R.grad, (0, slice(None), owner(j)), j - 1, near_side)
            return
        slot, device = (j - 1, near_side) if j else (3, near_mid)
        bz_copy(R.bz, slot, slot, device).wait_recv()
        for a in range(2):
            add_up([(R.bz, (slot, a)), (R.grad, (0, a, owner(j)))], R.bz, (slot, a))
        if j:
            start(bz_copy, R.bz, slot, 6 - j, near_mid)
        else:
            start(bz_copy, R.bz, slot, 0, near_side)

    def b_total(is_outer, a):
        terms = [(R.grad, (0, a, z)), (R.bz, (0, a)), (R.bz, (4, a))]
        return terms[:2] if is_outer else terms

    def bx_send(is_outer, u, j):
        bz_copy(R.bz, 0, 0, near_side).wait_recv()
        if not is_outer:
            bz_copy(R.bz, 4, 4, near_mid).wait_recv()
        add_up(b_total(is_outer, 1 - x), R.bs, ())
        start(bx_copy)

    def bx_last(is_outer, u, j):
        bx_copy().wait_recv()
        finish(0, b_total(is_outer, x) + [(R.bx, ())])

    def v_copy(stage, src, at, device):
        return copy(src.at[at] if at is not None else src, R.vec_in.at[stage], R.vs.at[stage], R.vr.at[stage], device)

    def v_step(is_outer, high, low):
        stage = 4 * high + low
        if stage == 0:
            R.vec_part[3] = R.vec[...]
            start(v_copy, 0, R.vec_part, 3, near_core)
        elif stage == 1:
            v_copy(0, R.vec_part, 3, near_core).wait_recv()
            R.vec_part[0] = R.vec[...] + R.vec_in[0]
            start(v_copy, 1, R.vec_part, 0, near_x)
        elif stage == 2:
            v_copy(1, R.vec_part, 0, near_x).wait_recv()
            R.vec_part[1] = R.vec_part[0] + R.vec_in[1]
            if is_outer:
                start(v_copy, 2, R.vec_part, 1, near_side)
        elif stage == 3:
            v_copy(2, R.vec_part, 1, near_side).wait_recv()
            R.vec_part[2] = R.vec_part[1] + R.vec_in[2]
            start(v_copy, 3, R.vec_part, 2, near_mid)
        elif stage == 4:
            v_copy(3, R.vec_part, 2, near_mid).wait_recv()
            R.vec_part[4] = R.vec_part[2] + R.vec_in[3]
            R.vec_sum[...] = R.vec_part[4]
            start(v_copy, 4, R.vec_part, 4, near_side)
        else:
            v_copy(4, R.vec_part, 3, near_side).wait_recv()
            R.vec_sum[...] = R.vec_in[4]

    steps = (x_send, z_send, z_last, bz_send, bx_send, bx_last, v_step)

    def serve(which, step):
        def run(is_outer, codes):
            for code in codes:
                kind, rest = divmod(code, 100)
                steps[kind](is_outer, rest // 4, rest % 4)

        codes_outer, codes_inner = (order[step] for order in ORDER[which])
        if codes_outer:
            pl.when(outer)(lambda: run(True, codes_outer))
        if codes_inner:
            pl.when(inner)(lambda: run(False, codes_inner))

    done = [0]

    def between(*more):
        @pl.when(section == 0)
        def _():
            for item in more or (None,):
                serve(0, done[0])
                done[0] += 1
                if item is not None:
                    item()

    def unit(u):
        return lambda: weight_unit(u)

    def shared_arrives(m):
        share(1, m).wait_recv()
        share(2, m).start()

    @pl.when(section == 1)
    def _():
        for m in range(MICRO):
            shared_arrives(m)

    R.vec[...] = jnp.zeros((8, WIDE), F32)

    @pl.when(section == 0)
    def _():
        left_copy(0).wait_recv()
        for m in range(MICRO):
            share(0, m).wait_recv()
        shared_arrives(0)

    def unit_up(i):
        def run():
            if i == 0:
                left_copy(1).wait_recv()
            right_copy(1 + i).wait_recv()
            weight_unit(SHARED + i)

        return run

    between(unit(0))
    for t in range(4):
        between()
        pl.when(section == 0)(lambda: feed_inner_matmul(R, t))
        feed_inner(R, t)
        right_copy(1 + t).start()
    for t in range(3):
        between()
        feed_entry(R, t)
    between()
    feed_norm(R)
    right_copy(5).start()
    between(*[unit_up(i) for i in range(4)])
    between()
    attention_mixed(R)

    def shared_units():
        for kind in range(2):
            left_x_copy(kind).wait_recv()
        for m in range(MICRO):
            share(2, m).wait_recv()

    for m in range(MICRO):
        for t in range(3):
            between()
            attention_pairs(R, m, t)
            if m == 0 and t == 0:
                pl.when(section == 0)(lambda: shared_arrives(1))
        between()
        attention_entry(R, m)
        if m == 0:
            pl.when(section == 0)(shared_units)
            between(*[lambda u=u: shared_unit(u) for u in range(1, SHARED)])

        @pl.when(section == 1)
        def _():
            g_copy(m).start()

    right_copy(6).start()

    @pl.when(section == 0)
    def _():
        for i in (2, 3):
            left_copy(i).wait_recv()
            right_copy(3 + i).wait_recv()

    between(*[unit(u) for u in range(8, UNITS)])
    pl.when(section == 0)(lambda: serve(0, done[0]))

    @pl.when(section == 1)
    def _():
        send_lefts()
        left_copy(0).wait_recv()
        for m in range(MICRO):
            share(0, m).wait_recv()
        for i in range(1, 4):
            left_copy(i).wait_recv()
        for i in range(1, 7):
            right_copy(i).wait_recv()
        for step, u in enumerate((0,) + tuple(range(4, UNITS)) + (1, 2, 3)):
            serve(1, step)
            if u == 1:
                shared_units()
            if 0 < u < SHARED:
                shared_unit(u)
            else:
                weight_unit(u)
        serve(1, UNITS)

    for i in range(4):
        left_copy(i).wait_send()
    for i in range(1, 7):
        right_copy(i).wait_send()
    for kind in range(2):
        left_x_copy(kind).wait_send()
    for kind in range(3):
        for m in range(MICRO):
            share(kind, m).wait_send()

    def every_sent(is_outer):
        for u in range(SHARED, UNITS):
            for j in range(4):
                ax_copy(u, j).wait_send()
        for slot in (0, 1, 2) if is_outer else (3, 4, 0):
            for u in range(1, UNITS):
                az_copy(u, R.az, (u - 1, slot), slot, near_side).wait_send()
            bz_copy(R.bz, slot, slot, near_side).wait_send()
        bx_copy().wait_send()
        for stage in (0, 1, 2) if is_outer else (0, 1, 3, 4):
            v_copy(stage, R.vec_part, 0, near_side).wait_send()

    pl.when(outer)(lambda: every_sent(True))
    pl.when(inner)(lambda: every_sent(False))

    for m in range(MICRO):

        @pl.when(section == 0)
        def _():
            x_copy(m).wait_send()

        @pl.when(section == 1)
        def _():
            g_copy(m).wait_send()


def settle(vec, *refs):
    arrays, narrow, wide, sems = refs[:6], refs[6:10], refs[10:16], refs[16]
    copies = [pltpu.make_async_copy(a, w, sems.at[i]) for i, (a, w) in enumerate(zip(arrays, wide))]
    for item in copies:
        item.start()
    place = lax.axis_index("dp")
    near = pltpu.roll(vec[...], (16 - place) % 16 * PART, 1)
    for i in range(3):
        narrow[i][...] = near[i : i + 1, :PART]
    far = pltpu.roll(vec[...], (4 - place % 4) % 4 * (4 * PART), 1)
    row = lax.broadcasted_iota(jnp.int32, far.shape, 0)
    mine = jnp.sum(jnp.where(row == 3 + place // 4, far, 0.0), axis=0, keepdims=True)
    narrow[3][...] = mine[:, : 4 * PART]
    for item in copies:
        item.wait()


def layer_device(
    inputs, cotangent, lengths, gain_one, w_qkv, w_out, gain_two, w_up, b_up, w_down, b_down
):
    y, d_state, qkv, out, up, down, vec = pl.pallas_call(
        kernel,
        out_shape=[jax.ShapeDtypeStruct(s, d) for s, d in OUT.values()],
        in_specs=list(IN.values()),
        out_specs=[VMEM] * len(OUT),
        scratch_shapes=[pltpu.VMEM(s, d) for s, d in SCRATCH.values()]
        + [pltpu.SemaphoreType.DMA(s) for s in SEMS.values()],
        compiler_params=pltpu.CompilerParams(
            collective_id=0, has_side_effects=True, vmem_limit_bytes=60 * 2**20
        ),
        name="layers",
    )(
        inputs.reshape(ROWS, D), cotangent.reshape(ROWS, D), lengths[:, 0], gain_one, w_qkv[0],
        w_out[0], gain_two, w_up[0], b_up, w_down[0], b_down,
    )
    totals = pl.pallas_call(
        settle,
        out_shape=[
            jax.ShapeDtypeStruct((1, PART), F32),
            jax.ShapeDtypeStruct((1, PART), F32),
            jax.ShapeDtypeStruct((1, PART), F32),
            jax.ShapeDtypeStruct((1, 4 * PART), F32),
        ]
        + [jax.ShapeDtypeStruct(s, d) for s, d in list(OUT.values())[:6]],
        in_specs=[VMEM] * 7,
        out_specs=[VMEM] * 4 + [ANY] * 6,
        scratch_shapes=[pltpu.SemaphoreType.DMA((6,))],
        name="settle",
    )(vec, y, d_state, qkv, out, up, down)
    gain_a, gain_b, bias_down, bias_up, y, d_state, qkv, out, up, down = totals
    return (
        y.reshape(1, MICRO, SLOT, D),
        d_state.reshape(1, MICRO, SLOT, D),
        gain_a,
        qkv[None],
        out[None],
        gain_b,
        up[None],
        bias_up,
        down[None],
        bias_down,
    )


def solution(mesh):
    placed = (
        P(None, "dp", None),
        P(None, "dp", None),
        P(None, "dp", None),
        P("section", None),
        P("section", None, None),
        P("section", None, None),
        P("section", None),
        P("section", None, None),
        P("section", None),
        P("section", None, None),
        P("section", None),
    )
    return jax.shard_map(
        layer_device if mesh.shape["dp"] == 16 else plain_device,
        mesh=mesh,
        in_specs=placed,
        out_specs=(
            P("section", None, "dp", None),
            P("section", None, "dp", None),
            P("section", "dp"),
            P("section", "dp", None),
            P("section", "dp", None),
            P("section", "dp"),
            P("section", "dp", None),
            P("section", "dp"),
            P("section", "dp", None),
            P("section", "dp"),
        ),
        check_vma=False,
    )
```

```python
from functools import partial
import math

from types import SimpleNamespace

import jax
import jax.numpy as jnp
from jax import lax
from jax.experimental import pallas as pl
from jax.experimental.pallas import tpu as pltpu
from jax.sharding import PartitionSpec as P

D = 768
FF = 3072
HEADS = 12
HEAD_DIM = 64
BLOCK = 16
SEGS = 3
SEQ_TOK = 64
EPSILON = 1e-05

F32 = jnp.float32
BF16 = jnp.bfloat16
MESH = pl.DeviceIdType.MESH
MICRO = 2
BLOCK_BITS = BLOCK.bit_length() - 1
SLOT = 2 * SEQ_TOK
ROWS = MICRO * SLOT
PAIRS = HEADS // 2
LANES = 128
PART = 48
UNITS = 12
WIDE = 768
SCALE = HEAD_DIM ** (-0.5)

UNIT_LEFT = (0, 1, 2, 3, 4, 4, 4, 4, 5, 6, 6, 6)
UNIT_RIGHT = (0, 0, 0, 0, 1, 2, 3, 4, 5, 6, 7, 8)
LEFTS = 7
RIGHTS = 9


def dot(a, b):
    return jnp.dot(a, b, preferred_element_type=F32)


def dot_nt(a, b):
    return lax.dot_general(a, b, (((1,), (1,)), ((), ())), preferred_element_type=F32)


def dot_tn(a, b):
    return lax.dot_general(a, b, (((0,), (0,)), ((), ())), preferred_element_type=F32)


def normalize(values):
    centred = values - jnp.mean(values, axis=-1, keepdims=True)
    inverse = lax.rsqrt(jnp.mean(centred * centred, axis=-1, keepdims=True) + EPSILON)
    return centred * inverse, inverse


def normal_back(d_normed, normed, inverse):
    return inverse * (
        d_normed
        - jnp.mean(d_normed, axis=-1, keepdims=True)
        - normed * jnp.mean(d_normed * normed, axis=-1, keepdims=True)
    )


def token_tables(token, first, second):
    one = (token >= first).astype(jnp.int32)
    two = (token >= first + second).astype(jnp.int32)
    return one + two, token - one * first - two * second


def swap_halves(values):
    lane = lax.broadcasted_iota(jnp.int32, values.shape, 1)
    low = (lane % HEAD_DIM) < HEAD_DIM // 2
    up = pltpu.roll(values, LANES - HEAD_DIM // 2, 1)
    down = pltpu.roll(values, HEAD_DIM // 2, 1)
    return jnp.where(low, up, down)


def head_masked(pair):
    lane = lax.broadcasted_iota(jnp.int32, pair.shape, 1)
    zero = jnp.zeros_like(pair)
    return jnp.concatenate(
        [jnp.where(lane < HEAD_DIM, pair, zero), jnp.where(lane < HEAD_DIM, zero, pair)], axis=0
    )


def build_tables(lengths, cos_t, sin_t, mask_t):
    half = HEAD_DIM // 2
    for m in range(MICRO):
        first, second = lengths[m, 0], lengths[m, 1]
        row = lax.broadcasted_iota(jnp.int32, (SEQ_TOK, LANES), 0)
        col = lax.broadcasted_iota(jnp.int32, (SEQ_TOK, LANES), 1)
        _, position = token_tables(row, first, second)
        frequency = jnp.exp((col & (half - 1)).astype(F32) * (-2.0 * math.log(10000.0) / HEAD_DIM))
        angle = position.astype(F32) * frequency
        both = jnp.sin(jnp.where(col < HEAD_DIM, angle + math.pi / 2, angle))
        other = pltpu.roll(both, HEAD_DIM, 1)
        cosine = jnp.where(col < HEAD_DIM, both, other)
        sine = jnp.where(col < HEAD_DIM, other, both)
        sine = jnp.where((col & (HEAD_DIM - 1)) < half, -sine, sine)
        cos_t[m] = jnp.concatenate([cosine, cosine], axis=0)
        sin_t[m] = jnp.concatenate([sine, sine], axis=0)
        row = lax.broadcasted_iota(jnp.int32, (SLOT, LANES), 0)
        col = lax.broadcasted_iota(jnp.int32, (SLOT, LANES), 1)
        doc_r, pos_r = token_tables(row & (SEQ_TOK - 1), first, second)
        doc_c, pos_c = token_tables(col & (SEQ_TOK - 1), first, second)
        block_r, block_c = pos_r >> BLOCK_BITS, pos_c >> BLOCK_BITS
        noisy_r, noisy_c = row < SEQ_TOK, col < SEQ_TOK
        same = (doc_r == doc_c) & (doc_r < SEGS - 1)
        ruling = (noisy_r & noisy_c & (block_r == block_c)) | (
            jnp.logical_not(noisy_c)
            & (
                (noisy_r & (block_c < block_r))
                | (jnp.logical_not(noisy_r) & (block_c <= block_r))
            )
        )
        allowed = (same & ruling) | (row == col)
        mask_t[m] = jnp.where(allowed, 1.0, 0.0)


def rotate_pair(values, cosine, sine):
    return values * cosine + swap_halves(values) * sine


def gelu_both(v):
    c = math.sqrt(2.0 / math.pi)
    square = v * v
    t = jnp.tanh(c * (v + 0.044715 * (v * square)))
    half = 0.5 * (1.0 + t)
    slope = half + (0.5 * c) * v * (1.0 - t * t) * (1.0 + (3.0 * 0.044715) * square)
    return v * half, slope


def forward(R, m, waits):
    rows = pl.ds(pl.multiple_of(m * SLOT, SLOT), SLOT)
    lane = lax.broadcasted_iota(jnp.int32, (SLOT, LANES), 1)
    normed, inverse = normalize(R.x[rows, :].astype(F32))
    R.normed[rows, :] = normed
    R.inv[rows, :] = jnp.broadcast_to(inverse, (SLOT, LANES))
    entry = (normed * R.gain_a[...]).astype(BF16)
    R.entry[rows, :] = entry
    waits(0)
    cosine, sine = R.cos[m], R.sin[m]
    for t in range(9):
        joined = dot(entry, R.w_qkv[:, t * 256 : (t + 1) * 256])
        kept = (R.q, R.k, R.v)[t // 3]
        for j in range(2):
            at = (t * 256 + j * LANES) % D
            piece = joined[:, j * LANES : (j + 1) * LANES]
            if t < 6:
                piece = rotate_pair(piece, cosine, sine)
            kept[rows, at : at + LANES] = piece.astype(BF16)
    keep = jnp.concatenate([R.mask[m], R.mask[m]], axis=0) > 0.5
    for p in range(PAIRS):
        lanes = pl.ds(p * LANES, LANES)
        q2 = head_masked(R.q[rows, lanes])
        raw = dot_nt(q2, R.k[rows, lanes]) * SCALE
        scores = jnp.where(keep, raw, -1e30)
        exponent = jnp.exp(scores - jnp.max(scores, axis=-1, keepdims=True))
        probs = exponent / jnp.sum(exponent, axis=-1, keepdims=True)
        R.probs[m * PAIRS + p] = probs
        pv = dot(probs.astype(BF16), R.v[rows, lanes])
        R.mixed[rows, lanes] = jnp.where(lane < HEAD_DIM, pv[:SLOT], pv[SLOT:]).astype(BF16)
    waits(1)
    hidden = R.x[rows, :].astype(F32) + dot(R.mixed[rows, :], R.w_out[...])
    R.hidden[rows, :] = hidden
    normed, inverse = normalize(hidden)
    R.normed2[rows, :] = normed
    R.inv2[rows, :] = jnp.broadcast_to(inverse, (SLOT, LANES))
    entry2 = (normed * R.gain_b[...]).astype(BF16)
    R.entry2[rows, :] = entry2
    waits(2)
    for t in range(FF // 256):
        cols = pl.ds(t * 256, 256)
        inner = dot(entry2, R.w_up[:, cols]) + R.b_up[:, cols]
        act, slope = gelu_both(inner)
        R.act[rows, cols] = act.astype(BF16)
        R.slope[rows, cols] = slope * R.slope[rows, cols]
    waits(3)
    R.y[rows, :] = (
        R.hidden[rows, :] + dot(R.act[rows, :], R.w_down[...]) + R.b_down[...]
    ).astype(BF16)


def feed_inner_matmul(R, t):
    g = R.right[0]
    for j in range(3):
        cols = pl.ds(t * WIDE + j * 256, 256)
        R.slope[:, cols] = R.slope[:, cols] * dot_nt(g, R.w_down[cols, :])


def feed_inner(R, t):
    for j in range(3):
        d_inner = R.slope[:, t * WIDE + j * 256 : t * WIDE + (j + 1) * 256].astype(BF16)
        R.right[1 + t, :, j * 256 : (j + 1) * 256] = d_inner
        R.vec[3 + t : 4 + t, j * 256 : (j + 1) * 256] = jnp.sum(
            d_inner.astype(F32), axis=0, keepdims=True
        )


def feed_entry(R, t):
    rows = pl.ds(t * 256, 256)
    total = dot_nt(R.right[1], R.w_up[rows, 0:WIDE])
    for j in range(1, 4):
        total += dot_nt(R.right[1 + j], R.w_up[rows, j * WIDE : (j + 1) * WIDE])
    R.hidden[:, rows] = total


def feed_norm(R):
    R.vec[2:3, :] = jnp.sum(R.right[0].astype(F32), axis=0, keepdims=True)
    gain = jnp.zeros((1, D), F32)
    for m in range(MICRO):
        rows = pl.ds(m * SLOT, SLOT)
        d_entry = R.hidden[rows, :]
        normed = R.normed2[rows, :]
        gain += jnp.sum(d_entry * normed, axis=0, keepdims=True)
        d_hidden = R.right[0, rows, :].astype(F32) + normal_back(
            d_entry * R.gain_b[...], normed, R.inv2[rows, 0:1]
        )
        R.hidden[rows, :] = d_hidden
        R.right[5, rows, :] = d_hidden.astype(BF16)
    R.vec[1:2, :] = gain


def attention_mixed(R):
    R.d_mixed[...] = dot_nt(R.right[5], R.w_out[...]).astype(BF16)


def attention_pairs(R, m, t):
    rows = pl.ds(m * SLOT, SLOT)
    cosine, sine = R.cos[m], -R.sin[m]
    for p in (2 * t, 2 * t + 1):
        lanes = pl.ds(p * LANES, LANES)
        dm2 = head_masked(R.d_mixed[rows, lanes])
        q2 = head_masked(R.q[rows, lanes])
        k2 = head_masked(R.k[rows, lanes])
        probs = R.probs[m * PAIRS + p]
        d_probs = dot_nt(dm2, R.v[rows, lanes])
        d_scores = (
            probs * (d_probs - jnp.sum(probs * d_probs, axis=-1, keepdims=True))
        ).astype(BF16)
        d_values = dot_tn(probs.astype(BF16), dm2)
        side = jnp.concatenate([d_scores[:SLOT], d_scores[SLOT:]], axis=1)
        d_query = dot(side, k2) * SCALE
        d_keys = dot_tn(d_scores, q2) * SCALE
        R.right[6, rows, lanes] = rotate_pair(d_query, cosine, sine).astype(BF16)
        R.right[7, rows, lanes] = rotate_pair(d_keys, cosine, sine).astype(BF16)
        R.right[8, rows, lanes] = d_values.astype(BF16)


def attention_entry(R, m):
    rows = pl.ds(m * SLOT, SLOT)
    d_entry = jnp.zeros((SLOT, D), F32)
    for t in range(3):
        d_entry += dot_nt(R.right[6 + t, rows, :], R.w_qkv[:, t * WIDE : (t + 1) * WIDE])
    normed = R.normed[rows, :]
    R.vec[0:1, :] = R.vec[0:1, :] + jnp.sum(d_entry * normed, axis=0, keepdims=True)
    R.d_state[rows, :] = (
        R.hidden[rows, :] + normal_back(d_entry * R.gain_a[...], normed, R.inv[rows, 0:1])
    ).astype(BF16)


def turn_lefts(R, core, group):
    def place(kind, owner_core, chip, block):
        x, z = chip % 2, chip // 2

        @pl.when(core == owner_core)
        def _():
            R.left[kind, x * 4 + z] = block

        @pl.when(core != owner_core)
        def _():
            R.left_out[kind, x * 4 + z] = block

    if group:
        turned = (R.entry2, R.mixed, R.entry)[group - 1][...].T
        for d in range(16):
            place(3 + group, d % 2, d // 2, turned[d * PART : (d + 1) * PART, :])
        return
    for d4 in range(4):
        turned = R.act[:, d4 * 768 : (d4 + 1) * 768].T
        for e in range(4):
            d = d4 * 4 + e
            for i in range(4):
                at = e * 192 + i * PART
                place(i, d % 2, d // 2, turned[at : at + PART, :])


def passed_along(block, axis, distance):
    devices = range(lax.axis_size(axis))
    route = [(i - distance, i) for i in devices if i - distance in devices]
    return lax.ppermute(block, axis, route)


def row_tables(lengths_row):
    steps_all = jnp.arange(SEQ_TOK, dtype=jnp.int32)
    bounds = jnp.cumsum(lengths_row)
    passed = (steps_all[:, None] >= bounds[None, :]).astype(jnp.int32)
    document = jnp.sum(passed, axis=1)
    offset = jnp.sum(passed * lengths_row[None, :], axis=1)
    position = steps_all - offset
    inside = document < SEGS - 1
    document_rows = jnp.concatenate([document, document])
    position_rows = jnp.concatenate([position, position])
    inside_rows = jnp.concatenate([inside, inside])
    copies = jnp.concatenate([jnp.zeros((SEQ_TOK,), jnp.int32), jnp.ones((SEQ_TOK,), jnp.int32)])
    blocks = position_rows // BLOCK
    query_block = blocks[:, None]
    key_block = blocks[None, :]
    noisy_query = (copies == 0)[:, None]
    noisy_key = (copies == 0)[None, :]
    ruling = jnp.where(
        noisy_query,
        jnp.where(noisy_key, key_block == query_block, key_block < query_block),
        jnp.logical_and(jnp.logical_not(noisy_key), key_block <= query_block),
    )
    same_doc = (
        (document_rows[:, None] == document_rows[None, :])
        & inside_rows[:, None]
        & inside_rows[None, :]
    )
    indices = jnp.arange(2 * SEQ_TOK, dtype=jnp.int32)
    allowed = same_doc & ruling | (indices[:, None] == indices[None, :])
    frequency = jnp.exp(
        jnp.arange(HEAD_DIM // 2).astype(jnp.float32) * (-2.0 * math.log(10000.0) / HEAD_DIM)
    )
    angles = position_rows.astype(jnp.float32)[:, None] * frequency[None, :]
    return (allowed, jnp.cos(angles), jnp.sin(angles))


def rotate(tensor, cosine, sine):
    halfway = tensor.shape[-1] // 2
    upper_part = tensor[..., :halfway]
    lower_part = tensor[..., halfway:]
    cos_rows = cosine[:, None, :]
    sin_rows = sine[:, None, :]
    return jnp.concatenate(
        [
            upper_part * cos_rows - lower_part * sin_rows,
            upper_part * sin_rows + lower_part * cos_rows,
        ],
        axis=-1,
    )


def unrotate(gradient, cosine, sine):
    halfway = gradient.shape[-1] // 2
    upper_part = gradient[..., :halfway]
    lower_part = gradient[..., halfway:]
    cos_rows = cosine[:, None, :]
    sin_rows = sine[:, None, :]
    return jnp.concatenate(
        [
            upper_part * cos_rows + lower_part * sin_rows,
            lower_part * cos_rows - upper_part * sin_rows,
        ],
        axis=-1,
    )


def plain_normalize(values):
    centred = values - jnp.mean(values, axis=-1, keepdims=True)
    inverse = lax.rsqrt(jnp.mean(centred * centred, axis=-1, keepdims=True) + EPSILON)
    return (centred * inverse, inverse)


def plain_normal_back(d_normed, normed, inverse):
    return inverse * (
        d_normed
        - jnp.mean(d_normed, axis=-1, keepdims=True)
        - normed * jnp.mean(d_normed * normed, axis=-1, keepdims=True)
    )


def scores_of(query, keyset, allowed):
    raw = jnp.einsum(
        "qhd,khd->hqk", query, keyset, preferred_element_type=jnp.float32
    ) * HEAD_DIM ** (-0.5)
    return jnp.where(allowed[None], raw, -1e30)


def forward_pass(state, lengths_row, weights):
    gain_a, w_qkv, w_out, gain_b, w_up, b_up, w_down, b_down = weights
    allowed, cosine, sine = row_tables(lengths_row)
    count = state.shape[0]
    widened = state.astype(jnp.float32)
    normed, inverse = plain_normalize(widened)
    entry = (normed * gain_a).astype(jnp.bfloat16)
    joined = jnp.dot(entry, w_qkv, preferred_element_type=jnp.float32)
    query = rotate(joined[:, :D].reshape(count, HEADS, HEAD_DIM), cosine, sine).astype(jnp.bfloat16)
    keyset = rotate(joined[:, D : 2 * D].reshape(count, HEADS, HEAD_DIM), cosine, sine).astype(
        jnp.bfloat16
    )
    valueset = joined[:, 2 * D :].reshape(count, HEADS, HEAD_DIM).astype(jnp.bfloat16)
    scores = scores_of(query, keyset, allowed)
    highest = jnp.max(scores, axis=-1, keepdims=True)
    exponent = jnp.exp(scores - highest)
    totals = jnp.sum(exponent, axis=-1, keepdims=True)
    soft_low = (exponent / totals).astype(jnp.bfloat16)
    log_total = highest + jnp.log(totals)
    mixed = (
        jnp.einsum("hqk,khd->qhd", soft_low, valueset, preferred_element_type=jnp.float32)
        .reshape(count, D)
        .astype(jnp.bfloat16)
    )
    hidden = widened + jnp.dot(mixed, w_out, preferred_element_type=jnp.float32)
    normed_two, inverse_two = plain_normalize(hidden)
    entry_two = (normed_two * gain_b).astype(jnp.bfloat16)
    inner = jnp.dot(entry_two, w_up, preferred_element_type=jnp.float32) + b_up
    activated = jax.nn.gelu(inner, approximate=True).astype(jnp.bfloat16)
    result = (
        hidden + jnp.dot(activated, w_down, preferred_element_type=jnp.float32) + b_down
    ).astype(jnp.bfloat16)
    saved = (
        normed,
        inverse,
        entry,
        query,
        keyset,
        valueset,
        log_total,
        mixed,
        normed_two,
        inverse_two,
        entry_two,
        inner,
        activated,
    )
    return (result, saved)


def forward_blank(state, lengths_row, weights):
    count = state.shape[0]
    rows_f = jnp.zeros((count, D), jnp.float32)
    rows_b = jnp.zeros((count, D), jnp.bfloat16)
    column = jnp.zeros((count, 1), jnp.float32)
    heads_b = jnp.zeros((count, HEADS, HEAD_DIM), jnp.bfloat16)
    saved = (
        rows_f,
        column,
        rows_b,
        heads_b,
        heads_b,
        heads_b,
        jnp.zeros((HEADS, count, 1), jnp.float32),
        rows_b,
        rows_f,
        column,
        rows_b,
        jnp.zeros((count, FF), jnp.float32),
        jnp.zeros((count, FF), jnp.bfloat16),
    )
    return (jnp.zeros_like(state), saved)


def settle_plain(index, group):
    return group


def backward_core(saved, incoming, lengths_row, weights, settle):
    gain_a, w_qkv, w_out, gain_b, w_up, b_up, w_down, b_down = weights
    (
        normed,
        inverse,
        entry,
        query,
        keyset,
        valueset,
        log_total,
        mixed,
        normed_two,
        inverse_two,
        entry_two,
        inner,
        activated,
    ) = saved
    allowed, cosine, sine = row_tables(lengths_row)
    count = incoming.shape[0]
    upper = incoming.astype(jnp.float32)
    grad_down = jnp.einsum("rf,rd->fd", activated, incoming, preferred_element_type=jnp.float32)
    grad_bias_down = jnp.sum(upper, axis=0)
    d_activated = jnp.einsum("rd,fd->rf", incoming, w_down, preferred_element_type=jnp.float32)
    _, gelu_pull = jax.vjp(partial(jax.nn.gelu, approximate=True), inner)
    d_inner = gelu_pull(d_activated)[0].astype(jnp.bfloat16)
    grad_up = jnp.einsum("rd,rf->df", entry_two, d_inner, preferred_element_type=jnp.float32)
    grad_bias_up = jnp.sum(d_inner, axis=0, dtype=jnp.float32)
    d_entry_two = jnp.einsum("rf,df->rd", d_inner, w_up, preferred_element_type=jnp.float32)
    grad_gain_b = jnp.sum(d_entry_two * normed_two, axis=0)
    feed_group = settle(0, (grad_gain_b, grad_up, grad_bias_up, grad_down, grad_bias_down))
    d_hidden = upper + plain_normal_back(d_entry_two * gain_b, normed_two, inverse_two)
    d_branch = d_hidden.astype(jnp.bfloat16)
    grad_out = jnp.einsum("rd,re->de", mixed, d_branch, preferred_element_type=jnp.float32)
    d_mixed = (
        jnp.einsum("re,de->rd", d_branch, w_out, preferred_element_type=jnp.float32)
        .astype(jnp.bfloat16)
        .reshape(count, HEADS, HEAD_DIM)
    )
    scores = scores_of(query, keyset, allowed)
    probs = jnp.exp(scores - log_total)
    d_probs = jnp.einsum("qhd,khd->hqk", d_mixed, valueset, preferred_element_type=jnp.float32)
    d_scores = (probs * (d_probs - jnp.sum(probs * d_probs, axis=-1, keepdims=True))).astype(
        jnp.bfloat16
    )
    d_values = jnp.einsum(
        "hqk,qhd->khd", probs.astype(jnp.bfloat16), d_mixed, preferred_element_type=jnp.float32
    )
    scaling = HEAD_DIM ** (-0.5)
    d_query = (
        jnp.einsum("hqk,khd->qhd", d_scores, keyset, preferred_element_type=jnp.float32) * scaling
    )
    d_keys = (
        jnp.einsum("hqk,qhd->khd", d_scores, query, preferred_element_type=jnp.float32) * scaling
    )
    d_joined = jnp.concatenate(
        [
            unrotate(d_query, cosine, sine).reshape(count, D),
            unrotate(d_keys, cosine, sine).reshape(count, D),
            d_values.reshape(count, D),
        ],
        axis=1,
    ).astype(jnp.bfloat16)
    grad_qkv = jnp.einsum("rd,re->de", entry, d_joined, preferred_element_type=jnp.float32)
    d_entry = jnp.einsum("re,de->rd", d_joined, w_qkv, preferred_element_type=jnp.float32)
    grad_gain_a = jnp.sum(d_entry * normed, axis=0)
    attn_group = settle(1, (grad_gain_a, grad_qkv, grad_out))
    d_state = (d_hidden + plain_normal_back(d_entry * gain_a, normed, inverse)).astype(jnp.bfloat16)
    return (d_state, tuple(attn_group) + tuple(feed_group))


def backward_pass(saved, incoming, lengths_row, weights):
    return backward_core(saved, incoming, lengths_row, weights, settle_plain)


def backward_blank(saved, incoming, lengths_row, weights):
    return (
        jnp.zeros_like(incoming),
        tuple((jnp.zeros(item.shape, jnp.float32) for item in weights)),
    )


def keep_at(place, active, stack, leaf):
    current = lax.dynamic_index_in_dim(stack, place, 0, keepdims=False)
    return lax.dynamic_update_index_in_dim(stack, jnp.where(active, leaf, current), place, 0)


def reduce_total(grads):
    (
        grad_gain_a,
        grad_qkv,
        grad_out,
        grad_gain_b,
        grad_up,
        grad_bias_up,
        grad_down,
        grad_bias_down,
    ) = grads
    return (
        lax.psum_scatter(grad_gain_a[None], "dp", scatter_dimension=1, tiled=True),
        lax.psum_scatter(grad_qkv[None], "dp", scatter_dimension=1, tiled=True),
        lax.psum_scatter(grad_out[None], "dp", scatter_dimension=1, tiled=True),
        lax.psum_scatter(grad_gain_b[None], "dp", scatter_dimension=1, tiled=True),
        lax.psum_scatter(grad_up[None], "dp", scatter_dimension=1, tiled=True),
        lax.psum_scatter(grad_bias_up[None], "dp", scatter_dimension=1, tiled=True),
        lax.psum_scatter(grad_down[None], "dp", scatter_dimension=1, tiled=True),
        lax.psum_scatter(grad_bias_down[None], "dp", scatter_dimension=1, tiled=True),
    )


def plain_device(
    inputs, cotangent, lengths, gain_one, w_qkv, w_out, gain_two, w_up, b_up, w_down, b_down
):
    section = lax.axis_index("section")
    micro = inputs.shape[0]
    weights = (gain_one[0], w_qkv[0], w_out[0], gain_two[0], w_up[0], b_up[0], w_down[0], b_down[0])
    slot_lengths = lengths[:, 0]
    arrived = jnp.zeros(inputs.shape[1:], jnp.bfloat16)
    results = jnp.zeros(inputs.shape, jnp.bfloat16)
    stored = ()
    for tick in range(micro + 1):
        number = tick - section
        active = jnp.logical_and(number >= 0, number < micro)
        place = jnp.clip(number, 0, micro - 1)
        layer_in = jnp.where(section == 0, inputs[min(tick, micro - 1)], arrived)
        lengths_row = lax.dynamic_index_in_dim(slot_lengths, place, 0, keepdims=False)
        result, saved = lax.cond(
            active, forward_pass, forward_blank, layer_in, lengths_row, weights
        )
        if tick == 0:
            stored = jax.tree.map(lambda leaf: jnp.zeros((micro,) + leaf.shape, leaf.dtype), saved)
        stored = jax.tree.map(partial(keep_at, place, active), stored, saved)
        results = keep_at(place, active, results, result)
        if tick < micro:
            arrived = passed_along(result, "section", 1)
    back_arrived = jnp.zeros(inputs.shape[1:], jnp.bfloat16)
    grads_in = jnp.zeros(inputs.shape, jnp.bfloat16)
    totals = tuple((jnp.zeros(item.shape, jnp.float32) for item in weights))
    reduced_sums = ()
    for tick in range(micro + 1):
        number = tick - (1 - section)
        active = jnp.logical_and(number >= 0, number < micro)
        place = jnp.clip(number, 0, micro - 1)
        incoming = jnp.where(section == 1, cotangent[min(tick, micro - 1)], back_arrived)
        saved = jax.tree.map(
            lambda stack: lax.dynamic_index_in_dim(stack, place, 0, keepdims=False), stored
        )
        lengths_row = lax.dynamic_index_in_dim(slot_lengths, place, 0, keepdims=False)
        d_state, grads = lax.cond(
            active, backward_pass, backward_blank, saved, incoming, lengths_row, weights
        )
        totals = tuple((earlier + later for earlier, later in zip(totals, grads)))
        grads_in = keep_at(place, active, grads_in, d_state)
        if tick < micro:
            back_arrived = passed_along(d_state, "section", -1)
    reduced_sums = reduce_total(totals)
    sum_gain_a, sum_qkv, sum_out, sum_gain_b, sum_up, sum_bias_up, sum_down, sum_bias_down = (
        reduced_sums
    )
    return (
        results[None],
        grads_in[None],
        sum_gain_a,
        sum_qkv,
        sum_out,
        sum_gain_b,
        sum_up,
        sum_bias_up,
        sum_down,
        sum_bias_down,
    )


VMEM = pl.BlockSpec(memory_space=pltpu.VMEM)
SMEM = pl.BlockSpec(memory_space=pltpu.SMEM)
ANY = pl.BlockSpec(memory_space=pl.ANY)
IN = dict(
    inputs=ANY, cotangent=ANY, lengths=SMEM, gain_a=VMEM, w_qkv_in=ANY, w_out_in=ANY,
    gain_b=VMEM, w_up_in=ANY, b_up=VMEM, w_down_in=ANY, b_down=VMEM,
)
OUT = dict(
    y_out=((ROWS, D), BF16),
    d_state_out=((ROWS, D), BF16),
    sum_qkv=((PART, 3 * D), F32),
    sum_out=((PART, D), F32),
    sum_up=((PART, FF), F32),
    sum_down=((4 * PART, D), F32),
    vec_sum=((8, WIDE), F32),
)
SHARED = 4
Z_UNITS = UNITS - 1
X_UNITS = UNITS - SHARED
ORDER = (
  (
    (
        (),
        (303, 302, 301,),
        (),
        (),
        (),
        (),
        (),
        (),
        (),
        (),
        (19, 18, 17, 16,),
        (23, 22, 21, 20,),
        (27, 26, 25, 24,),
        (),
        (),
        (),
        (),
        (),
        (),
        (107, 106, 105,),
        (111, 110, 109,),
        (115, 114, 113,),
        (),
        (),
        (),
        (600,),
        (),
        (),
        (),
        (601, 119, 602, 31, 118, 30, 117, 29, 28, 123, 122, 121, 35, 127, 126, 125, 34, 33, 32, 39, 38, 37, 36, 400, 204, 605, 131, 43, 208, 130, 42, 212, 129, 41, 40, 135, 47, 134, 133, 139, 138, 137, 46, 45, 44, 216, 500, 143, 142, 141, 147, 146, 145, 220, 224, 228, 232, 236, 240, 244,),
    ),
    (
        (),
        (),
        (),
        (),
        (),
        (),
        (),
        (),
        (),
        (),
        (19, 18, 16, 17,),
        (23, 22, 20, 21,),
        (27, 26, 24, 25,),
        (),
        (),
        (),
        (),
        (),
        (),
        (),
        (),
        (),
        (),
        (),
        (),
        (600,),
        (),
        (),
        (),
        (303, 601, 302, 602, 31, 30, 28, 29, 107, 35, 34, 603, 32, 33, 106, 39, 38, 36, 37, 300, 400, 111, 604, 110, 104, 205, 115, 114, 108, 209, 112, 213, 43, 42, 119, 118, 40, 123, 122, 127, 126, 41, 131, 47, 46, 116, 44, 130, 45, 500, 217, 135, 120, 221, 124, 225, 128, 229, 132, 134, 139, 138, 143, 233, 142, 136, 237, 140, 147, 146, 241, 144, 245,),
    ),
  ),
  (
    (
        (),
        (600, 303, 302, 301,),
        (19, 18, 17, 16,),
        (),
        (),
        (),
        (601,),
        (),
        (),
        (),
        (107, 106, 105,),
        (602, 111, 110, 109,),
        (115, 114, 113, 23, 119, 22, 21, 20, 118, 117, 605, 27, 123, 26, 25, 24, 122, 121, 400, 31, 127, 30, 126, 29, 28, 125, 500, 204, 35, 131, 34, 130, 33, 32, 129, 39, 135, 208, 212, 216, 220, 38, 134, 37, 36, 133, 43, 139, 224, 228, 42, 138, 232, 41, 40, 137, 47, 143, 46, 142, 236, 45, 141, 44, 147, 146, 145, 240, 244,),
    ),
    (
        (),
        (600,),
        (19, 18, 16, 17,),
        (),
        (),
        (),
        (),
        (601,),
        (),
        (),
        (),
        (),
        (602, 603, 604, 23, 22, 20, 21, 303, 302, 107, 106, 27, 26, 24, 25, 300, 111, 110, 115, 114, 400, 119, 118, 123, 122, 31, 104, 30, 28, 29, 500, 205, 127, 108, 209, 126, 112, 213, 35, 34, 32, 33, 116, 217, 131, 120, 221, 124, 225, 130, 128, 39, 135, 38, 36, 37, 229, 43, 132, 134, 139, 42, 233, 40, 41, 47, 138, 136, 237, 143, 46, 142, 44, 45, 140, 241, 147, 146, 144, 245,),
    ),
  ),
)

SCRATCH = dict(
    w_qkv=((D, 3 * D), BF16),
    w_out=((D, D), BF16),
    w_up=((D, FF), BF16),
    w_down=((FF, D), BF16),
    x=((ROWS, D), BF16),
    y=((ROWS, D), BF16),
    d_state=((ROWS, D), BF16),
    cos=((MICRO, SLOT, LANES), F32),
    sin=((MICRO, SLOT, LANES), F32),
    mask=((MICRO, SLOT, SLOT), F32),
    normed=((ROWS, D), F32),
    inv=((ROWS, LANES), F32),
    entry=((ROWS, D), BF16),
    q=((ROWS, D), BF16),
    k=((ROWS, D), BF16),
    v=((ROWS, D), BF16),
    probs=((MICRO * PAIRS, 2 * SLOT, SLOT), F32),
    mixed=((ROWS, D), BF16),
    hidden=((ROWS, D), F32),
    normed2=((ROWS, D), F32),
    inv2=((ROWS, LANES), F32),
    entry2=((ROWS, D), BF16),
    act=((ROWS, FF), BF16),
    slope=((ROWS, FF), F32),
    d_mixed=((ROWS, D), BF16),
    d_entry=((ROWS, D), F32),
    right=((RIGHTS, ROWS, WIDE), BF16),
    right_in=((RIGHTS, ROWS, WIDE), BF16),
    left_x=((2, SHARED - 1, 4, PART, ROWS), BF16),
    right_x=((2, ROWS, WIDE), BF16),
    left=((LEFTS, 8, PART, ROWS), BF16),
    left_out=((LEFTS, 8, PART, ROWS), BF16),
    left_in=((LEFTS, 8, PART, ROWS), BF16),
    grad=((UNITS, 2, 4, PART, WIDE), BF16),
    ax=((X_UNITS, 4, PART, WIDE), BF16),
    az=((Z_UNITS, 5, PART, WIDE), BF16),
    bz=((5, 2, PART, WIDE), BF16),
    bs=((PART, WIDE), BF16),
    bx=((PART, WIDE), BF16),
    vec=((8, WIDE), F32),
    vec_in=((5, 8, WIDE), F32),
    vec_part=((5, 8, WIDE), F32),
)
SEMS = dict(
    load=(7,), ys=(4,), yr=(4,), ls=(4,), lr=(4,), rs=(7,), rr=(7,),
    axs=(X_UNITS, 4), axr=(X_UNITS, 4), azs=(Z_UNITS, 5), azr=(Z_UNITS, 5),
    bzs=(5,), bzr=(5,), bxs=(1,), bxr=(1,), gs=(3, 2), gr=(3, 2), lxs=(2,), lxr=(2,),
    vs=(5,), vr=(5,),
)
LEFT_GROUPS = ((0, 4), (4, 1), (5, 1), (6, 1))
RIGHT_GROUPS = (None, (1, 1), (2, 1), (3, 1), (4, 1), (5, 1), (6, 3))


def kernel(*refs):
    names = (*IN, *OUT, *SCRATCH, *SEMS)
    R = SimpleNamespace(**dict(zip(names, refs)))
    place, section = lax.axis_index("dp"), lax.axis_index("section")
    core, x, z = place % 2, (place // 2) % 2, place // 4
    half = z // 2
    outer = (z == 0) | (z == 3)
    inner = (z == 1) | (z == 2)

    def dp_of(z_, x_, core_):
        return (z_ * 4 + x_ * 2 + core_, section)

    near_core = dp_of(z, x, 1 - core)
    near_x = dp_of(z, 1 - x, core)
    diagonal = dp_of(z, 1 - x, 1 - core)
    near_y = (place, 1 - section)
    near_side = dp_of(half * 2 + 1 - z % 2, x, core)
    near_mid = dp_of(3 - z, x, core)

    owners = [j + half * (3 - 2 * j) for j in range(4)]

    def owner(j):
        return owners[j]

    def copy(src, dst, send, recv, device):
        return pltpu.make_async_remote_copy(
            src_ref=src, dst_ref=dst, send_sem=send, recv_sem=recv,
            device_id=device, device_id_type=MESH,
        )

    weights_in = (R.w_qkv_in, R.w_out_in, R.w_up_in, R.w_down_in)
    weights = (R.w_qkv, R.w_out, R.w_up, R.w_down)
    loads = [
        pltpu.make_async_copy(src, dst, R.load.at[i])
        for i, (src, dst) in enumerate(zip(weights_in, weights))
    ]
    loads[0].start()

    def take(index, src, dst):
        @pl.when(section == index)
        def _():
            pltpu.make_async_copy(src, dst, R.load.at[4]).start()

    def taken(index, src, dst):
        @pl.when(section == index)
        def _():
            pltpu.make_async_copy(src, dst, R.load.at[4]).wait()

    take(0, R.inputs, R.x)
    take(1, R.cotangent, R.right.at[0])

    barrier = pltpu.get_barrier_semaphore()
    for device in (near_core, near_x, diagonal, near_y, near_side):
        pl.semaphore_signal(barrier, inc=1, device_id=device, device_id_type=MESH)

    @pl.when(inner)
    def _():
        pl.semaphore_signal(barrier, inc=1, device_id=near_mid, device_id_type=MESH)

    def all_here():
        pl.when(inner)(lambda: pl.semaphore_wait(barrier, 6))
        pl.when(outer)(lambda: pl.semaphore_wait(barrier, 5))

    build_tables(R.lengths, R.cos, R.sin, R.mask)
    for load in loads[1:]:
        load.start()

    def share(kind, m):
        rows = pl.ds(m * SLOT, SLOT)
        src, dst, device = (
            (R.right.at[0, rows], R.right_in.at[0, rows], near_core),
            (R.right.at[0, rows], R.right_x.at[0, rows], near_x),
            (R.right_x.at[0, rows], R.right_x.at[1, rows], near_core),
        )[kind]
        return copy(src, dst, R.gs.at[kind, m], R.gr.at[kind, m], device)

    def left_x_copy(kind):
        src, device = ((R.left, near_x), (R.left_out, diagonal))[kind]
        src = src.at[pl.ds(1, SHARED - 1), pl.ds((1 - x) * 4, 4)]
        return copy(src, R.left_x.at[kind], R.lxs.at[kind], R.lxr.at[kind], device)

    @pl.when(section == 1)
    def _():
        all_here()
        pltpu.make_async_copy(R.cotangent, R.right.at[0], R.load.at[4]).wait()
        for m in range(MICRO):
            share(0, m).start()
            share(1, m).start()

    def x_copy(m):
        rows = pl.ds(m * SLOT, SLOT)
        return copy(R.y.at[rows], R.x.at[rows], R.ys.at[m], R.yr.at[m], near_y)

    def g_copy(m):
        rows = pl.ds(m * SLOT, SLOT)
        return copy(
            R.d_state.at[rows], R.right.at[0, rows], R.ys.at[2 + m], R.yr.at[2 + m], near_y
        )

    taken(0, R.inputs, R.x)
    @pl.when(section == 0)
    def _():
        R.slope[...] = jnp.ones((ROWS, FF), F32)

    @pl.when(section == 1)
    def _():
        loads[3].wait()
        for t in range(FF // 256):
            cols = pl.ds(t * 256, 256)
            R.slope[:, cols] = dot_nt(R.right[0], R.w_down[cols, :])

    for m in range(MICRO):

        @pl.when(section == 1)
        def _():
            x_copy(m).wait_recv()

        def arrives(n):
            if m == 0 and n < 3:
                loads[n].wait()
            elif m == 0:
                pl.when(section == 0)(lambda: loads[3].wait())

        forward(R, m, arrives)

        @pl.when(section == 0)
        def _():
            if m == 0:
                all_here()
            x_copy(m).start()

    leaves = (
        pltpu.make_async_copy(R.y, R.y_out, R.load.at[5]),
        pltpu.make_async_copy(R.d_state, R.d_state_out, R.load.at[6]),
    )
    leaves[0].start()

    def left_copy(i):
        a, n = LEFT_GROUPS[i]
        rows = pl.ds(a, n)
        return copy(
            R.left_out.at[rows], R.left_in.at[rows], R.ls.at[i], R.lr.at[i], near_core
        )

    def right_copy(i):
        a, n = RIGHT_GROUPS[i]
        rows = pl.ds(a, n)
        return copy(
            R.right.at[rows], R.right_in.at[rows], R.rs.at[i], R.rr.at[i], near_core
        )

    def send_lefts(groups):
        for group in groups:
            turn_lefts(R, core, group)
            left_copy(group).start()
        if 1 in groups:
            for kind in range(2):
                left_x_copy(kind).start()

    @pl.when(section == 0)
    def _():
        send_lefts(range(4))
        for m in range(MICRO):
            g_copy(m).wait_recv()
            share(0, m).start()
            share(1, m).start()


    def weight_unit(u):
        left, right = UNIT_LEFT[u], UNIT_RIGHT[u]
        own = R.left[left].reshape(8 * PART, ROWS)
        other = R.left_in[left].reshape(8 * PART, ROWS)
        total = dot(own, R.right[right]) + dot(other, R.right_in[right])
        R.grad[u] = total.astype(BF16).reshape(2, 4, PART, WIDE)

    def shared_unit(u):
        mine = pl.ds(x * 4, 4)
        factors = (
            (R.left[u, mine], R.right[0]),
            (R.left_in[u, mine], R.right_in[0]),
            (R.left_x[0, u - 1], R.right_x[0]),
            (R.left_x[1, u - 1], R.right_x[1]),
        )
        total = sum(dot(a.reshape(4 * PART, ROWS), b) for a, b in factors)
        R.grad[u, x] = total.astype(BF16).reshape(4, PART, WIDE)

    def place_of(u):
        if u < SHARED:
            return R.sum_down, u * PART, slice(None)
        if u < 8:
            return R.sum_up, 0, slice((u - 4) * WIDE, (u - 3) * WIDE)
        if u == 8:
            return R.sum_out, 0, slice(None)
        return R.sum_qkv, 0, slice((u - 9) * WIDE, (u - 8) * WIDE)

    def add_up(terms, ref, at, first=0, columns=slice(None)):
        def some_rows(r, _):
            rows = pl.ds(pl.multiple_of(r * 16, 16), 16)
            total = sum(array[(*index, rows)].astype(F32) for array, index in terms)
            to = pl.ds(pl.multiple_of(first + r * 16, 16), 16)
            ref[(*at, to, columns)] = total.astype(ref.dtype)
            return 0

        lax.fori_loop(0, PART // 16, some_rows, 0)

    def finish(u, terms):
        ref, first, columns = place_of(u)
        add_up(terms, ref, (), first, columns)

    def start(make, *operands):
        make(*operands).start()

    def ax_copy(u, j):
        i = u - SHARED
        return copy(
            R.grad.at[u, 1 - x, owner(j)], R.ax.at[i, j], R.axs.at[i, j], R.axr.at[i, j], near_x
        )

    def az_copy(u, src, at, slot, device):
        i = u - 1
        return copy(src.at[at], R.az.at[i, slot], R.azs.at[i, slot], R.azr.at[i, slot], device)

    def x_sum(u, j):
        own = (R.grad, (u, x, owner(j)))
        if u < SHARED:
            return [own]
        ax_copy(u, j).wait_recv()
        return [own, (R.ax, (u - SHARED, j))]

    def x_send(is_outer, u, j):
        start(ax_copy, u, j)

    def z_send(is_outer, u, j):
        if is_outer and u < SHARED:
            start(az_copy, u, R.grad, (u, x, owner(j)), j - 1, near_side)
            return
        total = x_sum(u, j)
        if is_outer:
            add_up(total, R.ax, (u - SHARED, j))
            start(az_copy, u, R.ax, (u - SHARED, j), j - 1, near_side)
            return
        slot, device = (j - 1, near_side) if j else (3, near_mid)
        at = (u - 1, slot)
        az_copy(u, R.az, at, slot, device).wait_recv()
        add_up(total + [(R.az, at)], R.az, at)
        if j:
            start(az_copy, u, R.az, at, 6 - j, near_mid)
        else:
            start(az_copy, u, R.az, at, 0, near_side)

    def z_last(is_outer, u, j):
        total = x_sum(u, j)
        for slot, device in ((0, near_side),) if is_outer else ((0, near_side), (4, near_mid)):
            az_copy(u, R.az, (u - 1, slot), slot, device).wait_recv()
            total.append((R.az, (u - 1, slot)))
        finish(u, total)

    def bz_copy(src, at, slot, device):
        return copy(src.at[at], R.bz.at[slot], R.bzs.at[slot], R.bzr.at[slot], device)

    def bx_copy():
        return copy(R.bs, R.bx, R.bxs.at[0], R.bxr.at[0], near_x)

    def bz_send(is_outer, u, j):
        if is_outer:
            start(bz_copy, R.grad, (0, slice(None), owner(j)), j - 1, near_side)
            return
        slot, device = (j - 1, near_side) if j else (3, near_mid)
        bz_copy(R.bz, slot, slot, device).wait_recv()
        for a in range(2):
            add_up([(R.bz, (slot, a)), (R.grad, (0, a, owner(j)))], R.bz, (slot, a))
        if j:
            start(bz_copy, R.bz, slot, 6 - j, near_mid)
        else:
            start(bz_copy, R.bz, slot, 0, near_side)

    def b_total(is_outer, a):
        terms = [(R.grad, (0, a, z)), (R.bz, (0, a)), (R.bz, (4, a))]
        return terms[:2] if is_outer else terms

    def bx_send(is_outer, u, j):
        bz_copy(R.bz, 0, 0, near_side).wait_recv()
        if not is_outer:
            bz_copy(R.bz, 4, 4, near_mid).wait_recv()
        add_up(b_total(is_outer, 1 - x), R.bs, ())
        start(bx_copy)

    def bx_last(is_outer, u, j):
        bx_copy().wait_recv()
        finish(0, b_total(is_outer, x) + [(R.bx, ())])

    def v_copy(stage, src, at, device):
        return copy(src.at[at] if at is not None else src, R.vec_in.at[stage], R.vs.at[stage], R.vr.at[stage], device)

    def v_step(is_outer, high, low):
        stage = 4 * high + low
        if stage == 0:
            R.vec_part[3] = R.vec[...]
            start(v_copy, 0, R.vec_part, 3, near_core)
        elif stage == 1:
            v_copy(0, R.vec_part, 3, near_core).wait_recv()
            R.vec_part[0] = R.vec[...] + R.vec_in[0]
            start(v_copy, 1, R.vec_part, 0, near_x)
        elif stage == 2:
            v_copy(1, R.vec_part, 0, near_x).wait_recv()
            R.vec_part[1] = R.vec_part[0] + R.vec_in[1]
            if is_outer:
                start(v_copy, 2, R.vec_part, 1, near_side)
        elif stage == 3:
            v_copy(2, R.vec_part, 1, near_side).wait_recv()
            R.vec_part[2] = R.vec_part[1] + R.vec_in[2]
            start(v_copy, 3, R.vec_part, 2, near_mid)
        elif stage == 4:
            v_copy(3, R.vec_part, 2, near_mid).wait_recv()
            R.vec_part[4] = R.vec_part[2] + R.vec_in[3]
            R.vec_sum[...] = R.vec_part[4]
            start(v_copy, 4, R.vec_part, 4, near_side)
        else:
            v_copy(4, R.vec_part, 3, near_side).wait_recv()
            R.vec_sum[...] = R.vec_in[4]

    steps = (x_send, z_send, z_last, bz_send, bx_send, bx_last, v_step)

    def serve(which, step):
        def run(is_outer, codes):
            for code in codes:
                kind, rest = divmod(code, 100)
                steps[kind](is_outer, rest // 4, rest % 4)

        codes_outer, codes_inner = (order[step] for order in ORDER[which])
        if codes_outer:
            pl.when(outer)(lambda: run(True, codes_outer))
        if codes_inner:
            pl.when(inner)(lambda: run(False, codes_inner))

    done = [0]

    def between(*more):
        @pl.when(section == 0)
        def _():
            for item in more or (None,):
                serve(0, done[0])
                done[0] += 1
                if item is not None:
                    item()

    def unit(u):
        return lambda: weight_unit(u)

    def shared_arrives(m):
        share(1, m).wait_recv()
        share(2, m).start()

    @pl.when(section == 1)
    def _():
        for m in range(MICRO):
            shared_arrives(m)

    R.vec[...] = jnp.zeros((8, WIDE), F32)

    @pl.when(section == 0)
    def _():
        left_copy(0).wait_recv()
        for m in range(MICRO):
            share(0, m).wait_recv()
        shared_arrives(0)

    def unit_up(i):
        def run():
            if i == 0:
                left_copy(1).wait_recv()
            right_copy(1 + i).wait_recv()
            weight_unit(SHARED + i)

        return run

    between(unit(0))
    for t in range(4):
        between()
        pl.when(section == 0)(lambda: feed_inner_matmul(R, t))
        feed_inner(R, t)
        right_copy(1 + t).start()
    for t in range(3):
        between()
        feed_entry(R, t)
    between()
    feed_norm(R)
    right_copy(5).start()
    between(*[unit_up(i) for i in range(4)])
    between()
    attention_mixed(R)

    def shared_units():
        for kind in range(2):
            left_x_copy(kind).wait_recv()
        for m in range(MICRO):
            share(2, m).wait_recv()

    for m in range(MICRO):
        for t in range(3):
            between()
            attention_pairs(R, m, t)
            if m == 0 and t == 0:
                pl.when(section == 0)(lambda: shared_arrives(1))
        between()
        attention_entry(R, m)
        if m == 0:
            pl.when(section == 0)(shared_units)
            between(*[lambda u=u: shared_unit(u) for u in range(1, SHARED)])

        @pl.when(section == 1)
        def _():
            g_copy(m).start()

    right_copy(6).start()
    leaves[1].start()

    @pl.when(section == 0)
    def _():
        for i in (2, 3):
            left_copy(i).wait_recv()
            right_copy(3 + i).wait_recv()

    between(*[unit(u) for u in range(8, UNITS)])
    pl.when(section == 0)(lambda: serve(0, done[0]))

    @pl.when(section == 1)
    def _():
        send_lefts(range(2))
        left_copy(0).wait_recv()
        for m in range(MICRO):
            share(0, m).wait_recv()
        for step, u in enumerate((0,) + tuple(range(4, UNITS)) + (1, 2, 3)):
            serve(1, step)
            if step == 1:
                send_lefts(range(2, 4))
                for i in range(1, 4):
                    left_copy(i).wait_recv()
                for i in range(1, 7):
                    right_copy(i).wait_recv()
            if u == 1:
                shared_units()
            if 0 < u < SHARED:
                shared_unit(u)
            else:
                weight_unit(u)
        serve(1, UNITS)

    for leave in leaves:
        leave.wait()
    for i in range(4):
        left_copy(i).wait_send()
    for i in range(1, 7):
        right_copy(i).wait_send()
    for kind in range(2):
        left_x_copy(kind).wait_send()
    for kind in range(3):
        for m in range(MICRO):
            share(kind, m).wait_send()

    def every_sent(is_outer):
        for u in range(SHARED, UNITS):
            for j in range(4):
                ax_copy(u, j).wait_send()
        for slot in (0, 1, 2) if is_outer else (3, 4, 0):
            for u in range(1, UNITS):
                az_copy(u, R.az, (u - 1, slot), slot, near_side).wait_send()
            bz_copy(R.bz, slot, slot, near_side).wait_send()
        bx_copy().wait_send()
        for stage in (0, 1, 2) if is_outer else (0, 1, 3, 4):
            v_copy(stage, R.vec_part, 0, near_side).wait_send()

    pl.when(outer)(lambda: every_sent(True))
    pl.when(inner)(lambda: every_sent(False))

    for m in range(MICRO):

        @pl.when(section == 0)
        def _():
            x_copy(m).wait_send()

        @pl.when(section == 1)
        def _():
            g_copy(m).wait_send()


def settle(vec, *refs):
    arrays, narrow, wide, held, sems = refs[:6], refs[6:10], refs[10:16], refs[16:22], refs[22]
    inward = [pltpu.make_async_copy(a, h, sems.at[0, i]) for i, (a, h) in enumerate(zip(arrays, held))]
    copies = [pltpu.make_async_copy(h, w, sems.at[1, i]) for i, (h, w) in enumerate(zip(held, wide))]
    for item in inward:
        item.start()
    for there, item in zip(inward, copies):
        there.wait()
        item.start()
    place = lax.axis_index("dp")
    near = pltpu.roll(vec[...], (16 - place) % 16 * PART, 1)
    for i in range(3):
        narrow[i][...] = near[i : i + 1, :PART]
    far = pltpu.roll(vec[...], (4 - place % 4) % 4 * (4 * PART), 1)
    row = lax.broadcasted_iota(jnp.int32, far.shape, 0)
    mine = jnp.sum(jnp.where(row == 3 + place // 4, far, 0.0), axis=0, keepdims=True)
    narrow[3][...] = mine[:, : 4 * PART]
    for item in copies:
        item.wait()


def layer_device(
    inputs, cotangent, lengths, gain_one, w_qkv, w_out, gain_two, w_up, b_up, w_down, b_down
):
    y, d_state, qkv, out, up, down, vec = pl.pallas_call(
        kernel,
        out_shape=[jax.ShapeDtypeStruct(s, d) for s, d in OUT.values()],
        in_specs=list(IN.values()),
        out_specs=[ANY] * 2 + [VMEM] * (len(OUT) - 2),
        scratch_shapes=[pltpu.VMEM(s, d) for s, d in SCRATCH.values()]
        + [pltpu.SemaphoreType.DMA(s) for s in SEMS.values()],
        compiler_params=pltpu.CompilerParams(
            collective_id=0, has_side_effects=True, vmem_limit_bytes=60 * 2**20
        ),
        name="layers",
    )(
        inputs.reshape(ROWS, D), cotangent.reshape(ROWS, D), lengths[:, 0], gain_one, w_qkv[0],
        w_out[0], gain_two, w_up[0], b_up, w_down[0], b_down,
    )
    totals = pl.pallas_call(
        settle,
        out_shape=[
            jax.ShapeDtypeStruct((1, PART), F32),
            jax.ShapeDtypeStruct((1, PART), F32),
            jax.ShapeDtypeStruct((1, PART), F32),
            jax.ShapeDtypeStruct((1, 4 * PART), F32),
        ]
        + [jax.ShapeDtypeStruct(s, d) for s, d in list(OUT.values())[:6]],
        in_specs=[VMEM] + [ANY] * 6,
        out_specs=[VMEM] * 4 + [ANY] * 6,
        scratch_shapes=[pltpu.VMEM(s, d) for s, d in list(OUT.values())[:6]]
        + [pltpu.SemaphoreType.DMA((2, 6))],
        name="settle",
    )(vec, y, d_state, qkv, out, up, down)
    gain_a, gain_b, bias_down, bias_up, y, d_state, qkv, out, up, down = totals
    return (
        y.reshape(1, MICRO, SLOT, D),
        d_state.reshape(1, MICRO, SLOT, D),
        gain_a,
        qkv[None],
        out[None],
        gain_b,
        up[None],
        bias_up,
        down[None],
        bias_down,
    )


def solution(mesh):
    placed = (
        P(None, "dp", None),
        P(None, "dp", None),
        P(None, "dp", None),
        P("section", None),
        P("section", None, None),
        P("section", None, None),
        P("section", None),
        P("section", None, None),
        P("section", None),
        P("section", None, None),
        P("section", None),
    )
    return jax.shard_map(
        layer_device if mesh.shape["dp"] == 16 else plain_device,
        mesh=mesh,
        in_specs=placed,
        out_specs=(
            P("section", None, "dp", None),
            P("section", None, "dp", None),
            P("section", "dp"),
            P("section", "dp", None),
            P("section", "dp", None),
            P("section", "dp"),
            P("section", "dp", None),
            P("section", "dp"),
            P("section", "dp", None),
            P("section", "dp"),
        ),
        check_vma=False,
    )
```

```python
from functools import partial
import math

from types import SimpleNamespace

import jax
import jax.numpy as jnp
from jax import lax
from jax.experimental import pallas as pl
from jax.experimental.pallas import tpu as pltpu
from jax.sharding import PartitionSpec as P

D = 768
FF = 3072
HEADS = 12
HEAD_DIM = 64
BLOCK = 16
SEGS = 3
SEQ_TOK = 64
EPSILON = 1e-05

F32 = jnp.float32
BF16 = jnp.bfloat16
MESH = pl.DeviceIdType.MESH
MICRO = 2
BLOCK_BITS = BLOCK.bit_length() - 1
SLOT = 2 * SEQ_TOK
ROWS = MICRO * SLOT
PAIRS = HEADS // 2
LANES = 128
PART = 48
UNITS = 12
WIDE = 768
SCALE = HEAD_DIM ** (-0.5)

UNIT_LEFT = (0, 1, 2, 3, 4, 4, 4, 4, 5, 6, 6, 6)
UNIT_RIGHT = (0, 0, 0, 0, 1, 2, 3, 4, 5, 6, 7, 8)
LEFTS = 7
RIGHTS = 9


def dot(a, b):
    return jnp.dot(a, b, preferred_element_type=F32)


def dot_nt(a, b):
    return lax.dot_general(a, b, (((1,), (1,)), ((), ())), preferred_element_type=F32)


def dot_tn(a, b):
    return lax.dot_general(a, b, (((0,), (0,)), ((), ())), preferred_element_type=F32)


def normalize(values):
    centred = values - jnp.mean(values, axis=-1, keepdims=True)
    inverse = lax.rsqrt(jnp.mean(centred * centred, axis=-1, keepdims=True) + EPSILON)
    return centred * inverse, inverse


def normal_back(d_normed, normed, inverse):
    return inverse * (
        d_normed
        - jnp.mean(d_normed, axis=-1, keepdims=True)
        - normed * jnp.mean(d_normed * normed, axis=-1, keepdims=True)
    )


def token_tables(token, first, second):
    one = (token >= first).astype(jnp.int32)
    two = (token >= first + second).astype(jnp.int32)
    return one + two, token - one * first - two * second


def swap_halves(values):
    lane = lax.broadcasted_iota(jnp.int32, values.shape, 1)
    low = (lane % HEAD_DIM) < HEAD_DIM // 2
    up = pltpu.roll(values, LANES - HEAD_DIM // 2, 1)
    down = pltpu.roll(values, HEAD_DIM // 2, 1)
    return jnp.where(low, up, down)


def head_masked(pair):
    lane = lax.broadcasted_iota(jnp.int32, pair.shape, 1)
    zero = jnp.zeros_like(pair)
    return jnp.concatenate(
        [jnp.where(lane < HEAD_DIM, pair, zero), jnp.where(lane < HEAD_DIM, zero, pair)], axis=0
    )


def build_tables(lengths, cos_t, sin_t, mask_t):
    half = HEAD_DIM // 2
    for m in range(MICRO):
        first, second = lengths[m, 0], lengths[m, 1]
        row = lax.broadcasted_iota(jnp.int32, (SEQ_TOK, LANES), 0)
        col = lax.broadcasted_iota(jnp.int32, (SEQ_TOK, LANES), 1)
        _, position = token_tables(row, first, second)
        frequency = jnp.exp((col & (half - 1)).astype(F32) * (-2.0 * math.log(10000.0) / HEAD_DIM))
        angle = position.astype(F32) * frequency
        both = jnp.sin(jnp.where(col < HEAD_DIM, angle + math.pi / 2, angle))
        other = pltpu.roll(both, HEAD_DIM, 1)
        cosine = jnp.where(col < HEAD_DIM, both, other)
        sine = jnp.where(col < HEAD_DIM, other, both)
        sine = jnp.where((col & (HEAD_DIM - 1)) < half, -sine, sine)
        cos_t[m] = jnp.concatenate([cosine, cosine], axis=0)
        sin_t[m] = jnp.concatenate([sine, sine], axis=0)
        row = lax.broadcasted_iota(jnp.int32, (SLOT, LANES), 0)
        col = lax.broadcasted_iota(jnp.int32, (SLOT, LANES), 1)
        doc_r, pos_r = token_tables(row & (SEQ_TOK - 1), first, second)
        doc_c, pos_c = token_tables(col & (SEQ_TOK - 1), first, second)
        block_r, block_c = pos_r >> BLOCK_BITS, pos_c >> BLOCK_BITS
        noisy_r, noisy_c = row < SEQ_TOK, col < SEQ_TOK
        same = (doc_r == doc_c) & (doc_r < SEGS - 1)
        ruling = (noisy_r & noisy_c & (block_r == block_c)) | (
            jnp.logical_not(noisy_c)
            & (
                (noisy_r & (block_c < block_r))
                | (jnp.logical_not(noisy_r) & (block_c <= block_r))
            )
        )
        allowed = (same & ruling) | (row == col)
        mask_t[m] = jnp.where(allowed, 1.0, 0.0)


def rotate_pair(values, cosine, sine):
    return values * cosine + swap_halves(values) * sine


def gelu_both(v):
    c = math.sqrt(2.0 / math.pi)
    square = v * v
    t = jnp.tanh(c * (v + 0.044715 * (v * square)))
    half = 0.5 * (1.0 + t)
    slope = half + (0.5 * c) * v * (1.0 - t * t) * (1.0 + (3.0 * 0.044715) * square)
    return v * half, slope


def forward(R, m, waits):
    rows = pl.ds(pl.multiple_of(m * SLOT, SLOT), SLOT)
    lane = lax.broadcasted_iota(jnp.int32, (SLOT, LANES), 1)
    normed, inverse = normalize(R.x[rows, :].astype(F32))
    R.normed[rows, :] = normed
    R.inv[rows, :] = jnp.broadcast_to(inverse, (SLOT, LANES))
    entry = (normed * R.gain_a[...]).astype(BF16)
    R.entry[rows, :] = entry
    waits(0)
    cosine, sine = R.cos[m], R.sin[m]
    for t in range(9):
        joined = dot(entry, R.w_qkv[:, t * 256 : (t + 1) * 256])
        kept = (R.q, R.k, R.v)[t // 3]
        for j in range(2):
            at = (t * 256 + j * LANES) % D
            piece = joined[:, j * LANES : (j + 1) * LANES]
            if t < 6:
                piece = rotate_pair(piece, cosine, sine)
            kept[rows, at : at + LANES] = piece.astype(BF16)
    keep = jnp.concatenate([R.mask[m], R.mask[m]], axis=0) > 0.5
    for p in range(PAIRS):
        lanes = pl.ds(p * LANES, LANES)
        q2 = head_masked(R.q[rows, lanes])
        raw = dot_nt(q2, R.k[rows, lanes]) * SCALE
        scores = jnp.where(keep, raw, -1e30)
        exponent = jnp.exp(scores - jnp.max(scores, axis=-1, keepdims=True))
        probs = exponent / jnp.sum(exponent, axis=-1, keepdims=True)
        R.probs[m * PAIRS + p] = probs
        pv = dot(probs.astype(BF16), R.v[rows, lanes])
        R.mixed[rows, lanes] = jnp.where(lane < HEAD_DIM, pv[:SLOT], pv[SLOT:]).astype(BF16)
    waits(1)
    hidden = R.x[rows, :].astype(F32) + dot(R.mixed[rows, :], R.w_out[...])
    R.hidden[rows, :] = hidden
    normed, inverse = normalize(hidden)
    R.normed2[rows, :] = normed
    R.inv2[rows, :] = jnp.broadcast_to(inverse, (SLOT, LANES))
    entry2 = (normed * R.gain_b[...]).astype(BF16)
    R.entry2[rows, :] = entry2
    waits(2)
    for t in range(FF // 256):
        cols = pl.ds(t * 256, 256)
        inner = dot(entry2, R.w_up[:, cols]) + R.b_up[:, cols]
        act, slope = gelu_both(inner)
        R.act[rows, cols] = act.astype(BF16)
        R.slope[rows, cols] = slope * R.slope[rows, cols]
    waits(3)
    R.y[rows, :] = (
        R.hidden[rows, :] + dot(R.act[rows, :], R.w_down[...]) + R.b_down[...]
    ).astype(BF16)


def feed_inner_matmul(R, t):
    g = R.right[0]
    for j in range(3):
        cols = pl.ds(t * WIDE + j * 256, 256)
        R.slope[:, cols] = R.slope[:, cols] * dot_nt(g, R.w_down[cols, :])


def feed_inner(R, t):
    for j in range(3):
        d_inner = R.slope[:, t * WIDE + j * 256 : t * WIDE + (j + 1) * 256].astype(BF16)
        R.right[1 + t, :, j * 256 : (j + 1) * 256] = d_inner
        R.vec[3 + t : 4 + t, j * 256 : (j + 1) * 256] = jnp.sum(
            d_inner.astype(F32), axis=0, keepdims=True
        )


def feed_entry(R, t):
    rows = pl.ds(t * 256, 256)
    total = dot_nt(R.right[1], R.w_up[rows, 0:WIDE])
    for j in range(1, 4):
        total += dot_nt(R.right[1 + j], R.w_up[rows, j * WIDE : (j + 1) * WIDE])
    R.hidden[:, rows] = total


def feed_norm(R):
    R.vec[2:3, :] = jnp.sum(R.right[0].astype(F32), axis=0, keepdims=True)
    gain = jnp.zeros((1, D), F32)
    for m in range(MICRO):
        rows = pl.ds(m * SLOT, SLOT)
        d_entry = R.hidden[rows, :]
        normed = R.normed2[rows, :]
        gain += jnp.sum(d_entry * normed, axis=0, keepdims=True)
        d_hidden = R.right[0, rows, :].astype(F32) + normal_back(
            d_entry * R.gain_b[...], normed, R.inv2[rows, 0:1]
        )
        R.hidden[rows, :] = d_hidden
        R.right[5, rows, :] = d_hidden.astype(BF16)
    R.vec[1:2, :] = gain


def attention_mixed(R):
    R.d_mixed[...] = dot_nt(R.right[5], R.w_out[...]).astype(BF16)


def attention_pairs(R, m, t):
    rows = pl.ds(m * SLOT, SLOT)
    cosine, sine = R.cos[m], -R.sin[m]
    for p in (2 * t, 2 * t + 1):
        lanes = pl.ds(p * LANES, LANES)
        dm2 = head_masked(R.d_mixed[rows, lanes])
        q2 = head_masked(R.q[rows, lanes])
        k2 = head_masked(R.k[rows, lanes])
        probs = R.probs[m * PAIRS + p]
        d_probs = dot_nt(dm2, R.v[rows, lanes])
        d_scores = (
            probs * (d_probs - jnp.sum(probs * d_probs, axis=-1, keepdims=True))
        ).astype(BF16)
        d_values = dot_tn(probs.astype(BF16), dm2)
        side = jnp.concatenate([d_scores[:SLOT], d_scores[SLOT:]], axis=1)
        d_query = dot(side, k2) * SCALE
        d_keys = dot_tn(d_scores, q2) * SCALE
        R.right[6, rows, lanes] = rotate_pair(d_query, cosine, sine).astype(BF16)
        R.right[7, rows, lanes] = rotate_pair(d_keys, cosine, sine).astype(BF16)
        R.right[8, rows, lanes] = d_values.astype(BF16)


def attention_entry(R, m):
    rows = pl.ds(m * SLOT, SLOT)
    d_entry = jnp.zeros((SLOT, D), F32)
    for t in range(3):
        d_entry += dot_nt(R.right[6 + t, rows, :], R.w_qkv[:, t * WIDE : (t + 1) * WIDE])
    normed = R.normed[rows, :]
    R.vec[0:1, :] = R.vec[0:1, :] + jnp.sum(d_entry * normed, axis=0, keepdims=True)
    R.d_state[rows, :] = (
        R.hidden[rows, :] + normal_back(d_entry * R.gain_a[...], normed, R.inv[rows, 0:1])
    ).astype(BF16)


def turn_lefts(R, core, group):
    def place(kind, owner_core, chip, block):
        x, z = chip % 2, chip // 2

        @pl.when(core == owner_core)
        def _():
            R.left[kind, x * 4 + z] = block

        @pl.when(core != owner_core)
        def _():
            R.left_out[kind, x * 4 + z] = block

    if group:
        turned = (R.entry2, R.mixed, R.entry)[group - 1][...].T
        for d in range(16):
            place(3 + group, d % 2, d // 2, turned[d * PART : (d + 1) * PART, :])
        return
    for d4 in range(4):
        turned = R.act[:, d4 * 768 : (d4 + 1) * 768].T
        for e in range(4):
            d = d4 * 4 + e
            for i in range(4):
                at = e * 192 + i * PART
                place(i, d % 2, d // 2, turned[at : at + PART, :])


def passed_along(block, axis, distance):
    devices = range(lax.axis_size(axis))
    route = [(i - distance, i) for i in devices if i - distance in devices]
    return lax.ppermute(block, axis, route)


def row_tables(lengths_row):
    steps_all = jnp.arange(SEQ_TOK, dtype=jnp.int32)
    bounds = jnp.cumsum(lengths_row)
    passed = (steps_all[:, None] >= bounds[None, :]).astype(jnp.int32)
    document = jnp.sum(passed, axis=1)
    offset = jnp.sum(passed * lengths_row[None, :], axis=1)
    position = steps_all - offset
    inside = document < SEGS - 1
    document_rows = jnp.concatenate([document, document])
    position_rows = jnp.concatenate([position, position])
    inside_rows = jnp.concatenate([inside, inside])
    copies = jnp.concatenate([jnp.zeros((SEQ_TOK,), jnp.int32), jnp.ones((SEQ_TOK,), jnp.int32)])
    blocks = position_rows // BLOCK
    query_block = blocks[:, None]
    key_block = blocks[None, :]
    noisy_query = (copies == 0)[:, None]
    noisy_key = (copies == 0)[None, :]
    ruling = jnp.where(
        noisy_query,
        jnp.where(noisy_key, key_block == query_block, key_block < query_block),
        jnp.logical_and(jnp.logical_not(noisy_key), key_block <= query_block),
    )
    same_doc = (
        (document_rows[:, None] == document_rows[None, :])
        & inside_rows[:, None]
        & inside_rows[None, :]
    )
    indices = jnp.arange(2 * SEQ_TOK, dtype=jnp.int32)
    allowed = same_doc & ruling | (indices[:, None] == indices[None, :])
    frequency = jnp.exp(
        jnp.arange(HEAD_DIM // 2).astype(jnp.float32) * (-2.0 * math.log(10000.0) / HEAD_DIM)
    )
    angles = position_rows.astype(jnp.float32)[:, None] * frequency[None, :]
    return (allowed, jnp.cos(angles), jnp.sin(angles))


def rotate(tensor, cosine, sine):
    halfway = tensor.shape[-1] // 2
    upper_part = tensor[..., :halfway]
    lower_part = tensor[..., halfway:]
    cos_rows = cosine[:, None, :]
    sin_rows = sine[:, None, :]
    return jnp.concatenate(
        [
            upper_part * cos_rows - lower_part * sin_rows,
            upper_part * sin_rows + lower_part * cos_rows,
        ],
        axis=-1,
    )


def unrotate(gradient, cosine, sine):
    halfway = gradient.shape[-1] // 2
    upper_part = gradient[..., :halfway]
    lower_part = gradient[..., halfway:]
    cos_rows = cosine[:, None, :]
    sin_rows = sine[:, None, :]
    return jnp.concatenate(
        [
            upper_part * cos_rows + lower_part * sin_rows,
            lower_part * cos_rows - upper_part * sin_rows,
        ],
        axis=-1,
    )


def plain_normalize(values):
    centred = values - jnp.mean(values, axis=-1, keepdims=True)
    inverse = lax.rsqrt(jnp.mean(centred * centred, axis=-1, keepdims=True) + EPSILON)
    return (centred * inverse, inverse)


def plain_normal_back(d_normed, normed, inverse):
    return inverse * (
        d_normed
        - jnp.mean(d_normed, axis=-1, keepdims=True)
        - normed * jnp.mean(d_normed * normed, axis=-1, keepdims=True)
    )


def scores_of(query, keyset, allowed):
    raw = jnp.einsum(
        "qhd,khd->hqk", query, keyset, preferred_element_type=jnp.float32
    ) * HEAD_DIM ** (-0.5)
    return jnp.where(allowed[None], raw, -1e30)


def forward_pass(state, lengths_row, weights):
    gain_a, w_qkv, w_out, gain_b, w_up, b_up, w_down, b_down = weights
    allowed, cosine, sine = row_tables(lengths_row)
    count = state.shape[0]
    widened = state.astype(jnp.float32)
    normed, inverse = plain_normalize(widened)
    entry = (normed * gain_a).astype(jnp.bfloat16)
    joined = jnp.dot(entry, w_qkv, preferred_element_type=jnp.float32)
    query = rotate(joined[:, :D].reshape(count, HEADS, HEAD_DIM), cosine, sine).astype(jnp.bfloat16)
    keyset = rotate(joined[:, D : 2 * D].reshape(count, HEADS, HEAD_DIM), cosine, sine).astype(
        jnp.bfloat16
    )
    valueset = joined[:, 2 * D :].reshape(count, HEADS, HEAD_DIM).astype(jnp.bfloat16)
    scores = scores_of(query, keyset, allowed)
    highest = jnp.max(scores, axis=-1, keepdims=True)
    exponent = jnp.exp(scores - highest)
    totals = jnp.sum(exponent, axis=-1, keepdims=True)
    soft_low = (exponent / totals).astype(jnp.bfloat16)
    log_total = highest + jnp.log(totals)
    mixed = (
        jnp.einsum("hqk,khd->qhd", soft_low, valueset, preferred_element_type=jnp.float32)
        .reshape(count, D)
        .astype(jnp.bfloat16)
    )
    hidden = widened + jnp.dot(mixed, w_out, preferred_element_type=jnp.float32)
    normed_two, inverse_two = plain_normalize(hidden)
    entry_two = (normed_two * gain_b).astype(jnp.bfloat16)
    inner = jnp.dot(entry_two, w_up, preferred_element_type=jnp.float32) + b_up
    activated = jax.nn.gelu(inner, approximate=True).astype(jnp.bfloat16)
    result = (
        hidden + jnp.dot(activated, w_down, preferred_element_type=jnp.float32) + b_down
    ).astype(jnp.bfloat16)
    saved = (
        normed,
        inverse,
        entry,
        query,
        keyset,
        valueset,
        log_total,
        mixed,
        normed_two,
        inverse_two,
        entry_two,
        inner,
        activated,
    )
    return (result, saved)


def forward_blank(state, lengths_row, weights):
    count = state.shape[0]
    rows_f = jnp.zeros((count, D), jnp.float32)
    rows_b = jnp.zeros((count, D), jnp.bfloat16)
    column = jnp.zeros((count, 1), jnp.float32)
    heads_b = jnp.zeros((count, HEADS, HEAD_DIM), jnp.bfloat16)
    saved = (
        rows_f,
        column,
        rows_b,
        heads_b,
        heads_b,
        heads_b,
        jnp.zeros((HEADS, count, 1), jnp.float32),
        rows_b,
        rows_f,
        column,
        rows_b,
        jnp.zeros((count, FF), jnp.float32),
        jnp.zeros((count, FF), jnp.bfloat16),
    )
    return (jnp.zeros_like(state), saved)


def settle_plain(index, group):
    return group


def backward_core(saved, incoming, lengths_row, weights, settle):
    gain_a, w_qkv, w_out, gain_b, w_up, b_up, w_down, b_down = weights
    (
        normed,
        inverse,
        entry,
        query,
        keyset,
        valueset,
        log_total,
        mixed,
        normed_two,
        inverse_two,
        entry_two,
        inner,
        activated,
    ) = saved
    allowed, cosine, sine = row_tables(lengths_row)
    count = incoming.shape[0]
    upper = incoming.astype(jnp.float32)
    grad_down = jnp.einsum("rf,rd->fd", activated, incoming, preferred_element_type=jnp.float32)
    grad_bias_down = jnp.sum(upper, axis=0)
    d_activated = jnp.einsum("rd,fd->rf", incoming, w_down, preferred_element_type=jnp.float32)
    _, gelu_pull = jax.vjp(partial(jax.nn.gelu, approximate=True), inner)
    d_inner = gelu_pull(d_activated)[0].astype(jnp.bfloat16)
    grad_up = jnp.einsum("rd,rf->df", entry_two, d_inner, preferred_element_type=jnp.float32)
    grad_bias_up = jnp.sum(d_inner, axis=0, dtype=jnp.float32)
    d_entry_two = jnp.einsum("rf,df->rd", d_inner, w_up, preferred_element_type=jnp.float32)
    grad_gain_b = jnp.sum(d_entry_two * normed_two, axis=0)
    feed_group = settle(0, (grad_gain_b, grad_up, grad_bias_up, grad_down, grad_bias_down))
    d_hidden = upper + plain_normal_back(d_entry_two * gain_b, normed_two, inverse_two)
    d_branch = d_hidden.astype(jnp.bfloat16)
    grad_out = jnp.einsum("rd,re->de", mixed, d_branch, preferred_element_type=jnp.float32)
    d_mixed = (
        jnp.einsum("re,de->rd", d_branch, w_out, preferred_element_type=jnp.float32)
        .astype(jnp.bfloat16)
        .reshape(count, HEADS, HEAD_DIM)
    )
    scores = scores_of(query, keyset, allowed)
    probs = jnp.exp(scores - log_total)
    d_probs = jnp.einsum("qhd,khd->hqk", d_mixed, valueset, preferred_element_type=jnp.float32)
    d_scores = (probs * (d_probs - jnp.sum(probs * d_probs, axis=-1, keepdims=True))).astype(
        jnp.bfloat16
    )
    d_values = jnp.einsum(
        "hqk,qhd->khd", probs.astype(jnp.bfloat16), d_mixed, preferred_element_type=jnp.float32
    )
    scaling = HEAD_DIM ** (-0.5)
    d_query = (
        jnp.einsum("hqk,khd->qhd", d_scores, keyset, preferred_element_type=jnp.float32) * scaling
    )
    d_keys = (
        jnp.einsum("hqk,qhd->khd", d_scores, query, preferred_element_type=jnp.float32) * scaling
    )
    d_joined = jnp.concatenate(
        [
            unrotate(d_query, cosine, sine).reshape(count, D),
            unrotate(d_keys, cosine, sine).reshape(count, D),
            d_values.reshape(count, D),
        ],
        axis=1,
    ).astype(jnp.bfloat16)
    grad_qkv = jnp.einsum("rd,re->de", entry, d_joined, preferred_element_type=jnp.float32)
    d_entry = jnp.einsum("re,de->rd", d_joined, w_qkv, preferred_element_type=jnp.float32)
    grad_gain_a = jnp.sum(d_entry * normed, axis=0)
    attn_group = settle(1, (grad_gain_a, grad_qkv, grad_out))
    d_state = (d_hidden + plain_normal_back(d_entry * gain_a, normed, inverse)).astype(jnp.bfloat16)
    return (d_state, tuple(attn_group) + tuple(feed_group))


def backward_pass(saved, incoming, lengths_row, weights):
    return backward_core(saved, incoming, lengths_row, weights, settle_plain)


def backward_blank(saved, incoming, lengths_row, weights):
    return (
        jnp.zeros_like(incoming),
        tuple((jnp.zeros(item.shape, jnp.float32) for item in weights)),
    )


def keep_at(place, active, stack, leaf):
    current = lax.dynamic_index_in_dim(stack, place, 0, keepdims=False)
    return lax.dynamic_update_index_in_dim(stack, jnp.where(active, leaf, current), place, 0)


def reduce_total(grads):
    (
        grad_gain_a,
        grad_qkv,
        grad_out,
        grad_gain_b,
        grad_up,
        grad_bias_up,
        grad_down,
        grad_bias_down,
    ) = grads
    return (
        lax.psum_scatter(grad_gain_a[None], "dp", scatter_dimension=1, tiled=True),
        lax.psum_scatter(grad_qkv[None], "dp", scatter_dimension=1, tiled=True),
        lax.psum_scatter(grad_out[None], "dp", scatter_dimension=1, tiled=True),
        lax.psum_scatter(grad_gain_b[None], "dp", scatter_dimension=1, tiled=True),
        lax.psum_scatter(grad_up[None], "dp", scatter_dimension=1, tiled=True),
        lax.psum_scatter(grad_bias_up[None], "dp", scatter_dimension=1, tiled=True),
        lax.psum_scatter(grad_down[None], "dp", scatter_dimension=1, tiled=True),
        lax.psum_scatter(grad_bias_down[None], "dp", scatter_dimension=1, tiled=True),
    )


def plain_device(
    inputs, cotangent, lengths, gain_one, w_qkv, w_out, gain_two, w_up, b_up, w_down, b_down
):
    section = lax.axis_index("section")
    micro = inputs.shape[0]
    weights = (gain_one[0], w_qkv[0], w_out[0], gain_two[0], w_up[0], b_up[0], w_down[0], b_down[0])
    slot_lengths = lengths[:, 0]
    arrived = jnp.zeros(inputs.shape[1:], jnp.bfloat16)
    results = jnp.zeros(inputs.shape, jnp.bfloat16)
    stored = ()
    for tick in range(micro + 1):
        number = tick - section
        active = jnp.logical_and(number >= 0, number < micro)
        place = jnp.clip(number, 0, micro - 1)
        layer_in = jnp.where(section == 0, inputs[min(tick, micro - 1)], arrived)
        lengths_row = lax.dynamic_index_in_dim(slot_lengths, place, 0, keepdims=False)
        result, saved = lax.cond(
            active, forward_pass, forward_blank, layer_in, lengths_row, weights
        )
        if tick == 0:
            stored = jax.tree.map(lambda leaf: jnp.zeros((micro,) + leaf.shape, leaf.dtype), saved)
        stored = jax.tree.map(partial(keep_at, place, active), stored, saved)
        results = keep_at(place, active, results, result)
        if tick < micro:
            arrived = passed_along(result, "section", 1)
    back_arrived = jnp.zeros(inputs.shape[1:], jnp.bfloat16)
    grads_in = jnp.zeros(inputs.shape, jnp.bfloat16)
    totals = tuple((jnp.zeros(item.shape, jnp.float32) for item in weights))
    reduced_sums = ()
    for tick in range(micro + 1):
        number = tick - (1 - section)
        active = jnp.logical_and(number >= 0, number < micro)
        place = jnp.clip(number, 0, micro - 1)
        incoming = jnp.where(section == 1, cotangent[min(tick, micro - 1)], back_arrived)
        saved = jax.tree.map(
            lambda stack: lax.dynamic_index_in_dim(stack, place, 0, keepdims=False), stored
        )
        lengths_row = lax.dynamic_index_in_dim(slot_lengths, place, 0, keepdims=False)
        d_state, grads = lax.cond(
            active, backward_pass, backward_blank, saved, incoming, lengths_row, weights
        )
        totals = tuple((earlier + later for earlier, later in zip(totals, grads)))
        grads_in = keep_at(place, active, grads_in, d_state)
        if tick < micro:
            back_arrived = passed_along(d_state, "section", -1)
    reduced_sums = reduce_total(totals)
    sum_gain_a, sum_qkv, sum_out, sum_gain_b, sum_up, sum_bias_up, sum_down, sum_bias_down = (
        reduced_sums
    )
    return (
        results[None],
        grads_in[None],
        sum_gain_a,
        sum_qkv,
        sum_out,
        sum_gain_b,
        sum_up,
        sum_bias_up,
        sum_down,
        sum_bias_down,
    )


VMEM = pl.BlockSpec(memory_space=pltpu.VMEM)
SMEM = pl.BlockSpec(memory_space=pltpu.SMEM)
ANY = pl.BlockSpec(memory_space=pl.ANY)
IN = dict(
    inputs=ANY, cotangent=ANY, lengths=SMEM, gain_a=VMEM, w_qkv_in=ANY, w_out_in=ANY,
    gain_b=VMEM, w_up_in=ANY, b_up=VMEM, w_down_in=ANY, b_down=VMEM,
)
OUT = dict(
    y_out=((ROWS, D), BF16),
    d_state_out=((ROWS, D), BF16),
    sum_qkv=((PART, 3 * D), F32),
    sum_out=((PART, D), F32),
    sum_up=((PART, FF), F32),
    sum_down=((4 * PART, D), F32),
    vec_sum=((8, WIDE), F32),
)
SHARED = 4
Z_UNITS = UNITS - 1
X_UNITS = UNITS - SHARED
ORDER = (
  (
    (
        (),
        (303, 302, 301,),
        (),
        (),
        (),
        (),
        (),
        (),
        (),
        (),
        (19, 18, 17, 16,),
        (23, 22, 21, 20,),
        (27, 26, 25, 24,),
        (),
        (),
        (),
        (),
        (),
        (),
        (107, 106, 105,),
        (111, 110, 109,),
        (115, 114, 113,),
        (),
        (),
        (),
        (600,),
        (),
        (),
        (),
        (601, 119, 602, 31, 118, 30, 117, 29, 28, 123, 122, 121, 35, 127, 126, 125, 34, 33, 32, 39, 38, 37, 36, 400, 204, 605, 131, 43, 208, 130, 42, 212, 129, 41, 40, 135, 47, 134, 133, 139, 138, 137, 46, 45, 44, 216, 500, 143, 142, 141, 147, 146, 145, 220, 224, 228, 232, 236, 240, 244,),
    ),
    (
        (),
        (),
        (),
        (),
        (),
        (),
        (),
        (),
        (),
        (),
        (19, 18, 16, 17,),
        (23, 22, 20, 21,),
        (27, 26, 24, 25,),
        (),
        (),
        (),
        (),
        (),
        (),
        (),
        (),
        (),
        (),
        (),
        (),
        (600,),
        (),
        (),
        (),
        (303, 601, 302, 602, 31, 30, 28, 29, 107, 35, 34, 603, 32, 33, 106, 39, 38, 36, 37, 300, 400, 111, 604, 110, 104, 205, 115, 114, 108, 209, 112, 213, 43, 42, 119, 118, 40, 123, 122, 127, 126, 41, 131, 47, 46, 116, 44, 130, 45, 500, 217, 135, 120, 221, 124, 225, 128, 229, 132, 134, 139, 138, 143, 233, 142, 136, 237, 140, 147, 146, 241, 144, 245,),
    ),
  ),
  (
    (
        (),
        (600, 303, 302, 301,),
        (19, 18, 17, 16,),
        (),
        (),
        (),
        (601,),
        (),
        (),
        (),
        (107, 106, 105,),
        (602, 111, 110, 109,),
        (115, 114, 113, 23, 119, 22, 21, 20, 118, 117, 605, 27, 123, 26, 25, 24, 122, 121, 400, 31, 127, 30, 126, 29, 28, 125, 500, 204, 35, 131, 34, 130, 33, 32, 129, 39, 135, 208, 212, 216, 220, 38, 134, 37, 36, 133, 43, 139, 224, 228, 42, 138, 232, 41, 40, 137, 47, 143, 46, 142, 236, 45, 141, 44, 147, 146, 145, 240, 244,),
    ),
    (
        (),
        (600,),
        (19, 18, 16, 17,),
        (),
        (),
        (),
        (),
        (601,),
        (),
        (),
        (),
        (),
        (602, 603, 604, 23, 22, 20, 21, 303, 302, 107, 106, 27, 26, 24, 25, 300, 111, 110, 115, 114, 400, 119, 118, 123, 122, 31, 104, 30, 28, 29, 500, 205, 127, 108, 209, 126, 112, 213, 35, 34, 32, 33, 116, 217, 131, 120, 221, 124, 225, 130, 128, 39, 135, 38, 36, 37, 229, 43, 132, 134, 139, 42, 233, 40, 41, 47, 138, 136, 237, 143, 46, 142, 44, 45, 140, 241, 147, 146, 144, 245,),
    ),
  ),
)

SCRATCH = dict(
    w_qkv=((D, 3 * D), BF16),
    w_out=((D, D), BF16),
    w_up=((D, FF), BF16),
    w_down=((FF, D), BF16),
    x=((ROWS, D), BF16),
    y=((ROWS, D), BF16),
    d_state=((ROWS, D), BF16),
    cos=((MICRO, SLOT, LANES), F32),
    sin=((MICRO, SLOT, LANES), F32),
    mask=((MICRO, SLOT, SLOT), F32),
    normed=((ROWS, D), F32),
    inv=((ROWS, LANES), F32),
    entry=((ROWS, D), BF16),
    q=((ROWS, D), BF16),
    k=((ROWS, D), BF16),
    v=((ROWS, D), BF16),
    probs=((MICRO * PAIRS, 2 * SLOT, SLOT), F32),
    mixed=((ROWS, D), BF16),
    hidden=((ROWS, D), F32),
    normed2=((ROWS, D), F32),
    inv2=((ROWS, LANES), F32),
    entry2=((ROWS, D), BF16),
    act=((ROWS, FF), BF16),
    slope=((ROWS, FF), F32),
    d_mixed=((ROWS, D), BF16),
    d_entry=((ROWS, D), F32),
    right=((RIGHTS, ROWS, WIDE), BF16),
    right_in=((RIGHTS, ROWS, WIDE), BF16),
    left_x=((2, SHARED - 1, 4, PART, ROWS), BF16),
    right_x=((2, ROWS, WIDE), BF16),
    left=((LEFTS, 8, PART, ROWS), BF16),
    left_out=((LEFTS, 8, PART, ROWS), BF16),
    left_in=((LEFTS, 8, PART, ROWS), BF16),
    grad=((UNITS, 2, 4, PART, WIDE), BF16),
    ax=((X_UNITS, 4, PART, WIDE), BF16),
    az=((Z_UNITS, 5, PART, WIDE), BF16),
    bz=((5, 2, PART, WIDE), BF16),
    bs=((PART, WIDE), BF16),
    bx=((PART, WIDE), BF16),
    vec=((8, WIDE), F32),
    vec_in=((5, 8, WIDE), F32),
    vec_part=((5, 8, WIDE), F32),
)
SEMS = dict(
    load=(7,), ys=(4,), yr=(4,), ls=(4,), lr=(4,), rs=(7,), rr=(7,),
    axs=(X_UNITS, 4), axr=(X_UNITS, 4), azs=(Z_UNITS, 5), azr=(Z_UNITS, 5),
    bzs=(5,), bzr=(5,), bxs=(1,), bxr=(1,), gs=(3, 2), gr=(3, 2), lxs=(2,), lxr=(2,),
    vs=(5,), vr=(5,),
)
LEFT_GROUPS = ((0, 4), (4, 1), (5, 1), (6, 1))
RIGHT_GROUPS = (None, (1, 1), (2, 1), (3, 1), (4, 1), (5, 1), (6, 3))


def kernel(*refs):
    names = (*IN, *OUT, *SCRATCH, *SEMS)
    R = SimpleNamespace(**dict(zip(names, refs)))
    place, section = lax.axis_index("dp"), lax.axis_index("section")
    core, x, z = place % 2, (place // 2) % 2, place // 4
    half = z // 2
    outer = (z == 0) | (z == 3)
    inner = (z == 1) | (z == 2)

    def dp_of(z_, x_, core_):
        return (z_ * 4 + x_ * 2 + core_, section)

    near_core = dp_of(z, x, 1 - core)
    near_x = dp_of(z, 1 - x, core)
    diagonal = dp_of(z, 1 - x, 1 - core)
    near_y = (place, 1 - section)
    near_side = dp_of(half * 2 + 1 - z % 2, x, core)
    near_mid = dp_of(3 - z, x, core)

    owners = [j + half * (3 - 2 * j) for j in range(4)]

    def owner(j):
        return owners[j]

    def copy(src, dst, send, recv, device):
        return pltpu.make_async_remote_copy(
            src_ref=src, dst_ref=dst, send_sem=send, recv_sem=recv,
            device_id=device, device_id_type=MESH,
        )

    weights_in = (R.w_qkv_in, R.w_out_in, R.w_up_in, R.w_down_in)
    weights = (R.w_qkv, R.w_out, R.w_up, R.w_down)
    loads = [
        pltpu.make_async_copy(src, dst, R.load.at[i])
        for i, (src, dst) in enumerate(zip(weights_in, weights))
    ]
    loads[0].start()

    def take(index, src, dst):
        @pl.when(section == index)
        def _():
            pltpu.make_async_copy(src, dst, R.load.at[4]).start()

    def taken(index, src, dst):
        @pl.when(section == index)
        def _():
            pltpu.make_async_copy(src, dst, R.load.at[4]).wait()

    take(0, R.inputs, R.x)
    take(1, R.cotangent, R.right.at[0])

    barrier = pltpu.get_barrier_semaphore()
    for device in (near_core, near_x, diagonal, near_y, near_side):
        pl.semaphore_signal(barrier, inc=1, device_id=device, device_id_type=MESH)

    @pl.when(inner)
    def _():
        pl.semaphore_signal(barrier, inc=1, device_id=near_mid, device_id_type=MESH)

    def all_here():
        pl.when(inner)(lambda: pl.semaphore_wait(barrier, 6))
        pl.when(outer)(lambda: pl.semaphore_wait(barrier, 5))

    build_tables(R.lengths, R.cos, R.sin, R.mask)
    def load_rest():
        for load in loads[1:]:
            load.start()

    pl.when(section == 1)(load_rest)

    def share(kind, m):
        rows = pl.ds(m * SLOT, SLOT)
        src, dst, device = (
            (R.right.at[0, rows], R.right_in.at[0, rows], near_core),
            (R.right.at[0, rows], R.right_x.at[0, rows], near_x),
            (R.right_x.at[0, rows], R.right_x.at[1, rows], near_core),
        )[kind]
        return copy(src, dst, R.gs.at[kind, m], R.gr.at[kind, m], device)

    def left_x_copy(kind):
        src, device = ((R.left, near_x), (R.left_out, diagonal))[kind]
        src = src.at[pl.ds(1, SHARED - 1), pl.ds((1 - x) * 4, 4)]
        return copy(src, R.left_x.at[kind], R.lxs.at[kind], R.lxr.at[kind], device)

    @pl.when(section == 1)
    def _():
        all_here()
        pltpu.make_async_copy(R.cotangent, R.right.at[0], R.load.at[4]).wait()
        for m in range(MICRO):
            share(0, m).start()
            share(1, m).start()

    def x_copy(m):
        rows = pl.ds(m * SLOT, SLOT)
        return copy(R.y.at[rows], R.x.at[rows], R.ys.at[m], R.yr.at[m], near_y)

    def g_copy(m):
        rows = pl.ds(m * SLOT, SLOT)
        return copy(
            R.d_state.at[rows], R.right.at[0, rows], R.ys.at[2 + m], R.yr.at[2 + m], near_y
        )

    taken(0, R.inputs, R.x)
    @pl.when(section == 0)
    def _():
        R.slope[...] = jnp.ones((ROWS, FF), F32)

    @pl.when(section == 1)
    def _():
        loads[3].wait()
        for t in range(FF // 256):
            cols = pl.ds(t * 256, 256)
            R.slope[:, cols] = dot_nt(R.right[0], R.w_down[cols, :])

    for m in range(MICRO):

        @pl.when(section == 1)
        def _():
            x_copy(m).wait_recv()

        def arrives(n):
            if m == 0 and n < 3:
                loads[n].wait()
                if n == 0:
                    pl.when(section == 0)(load_rest)
            elif m == 0:
                pl.when(section == 0)(lambda: loads[3].wait())

        forward(R, m, arrives)

        @pl.when(section == 0)
        def _():
            if m == 0:
                all_here()
            x_copy(m).start()

    leaves = (
        pltpu.make_async_copy(R.y, R.y_out, R.load.at[5]),
        pltpu.make_async_copy(R.d_state, R.d_state_out, R.load.at[6]),
    )
    leaves[0].start()

    def left_copy(i):
        a, n = LEFT_GROUPS[i]
        rows = pl.ds(a, n)
        return copy(
            R.left_out.at[rows], R.left_in.at[rows], R.ls.at[i], R.lr.at[i], near_core
        )

    def right_copy(i):
        a, n = RIGHT_GROUPS[i]
        rows = pl.ds(a, n)
        return copy(
            R.right.at[rows], R.right_in.at[rows], R.rs.at[i], R.rr.at[i], near_core
        )

    def send_lefts(groups):
        for group in groups:
            turn_lefts(R, core, group)
            left_copy(group).start()
        if 1 in groups:
            for kind in range(2):
                left_x_copy(kind).start()

    @pl.when(section == 0)
    def _():
        send_lefts(range(4))
        for m in range(MICRO):
            g_copy(m).wait_recv()
            share(0, m).start()
            share(1, m).start()


    def weight_unit(u):
        left, right = UNIT_LEFT[u], UNIT_RIGHT[u]
        own = R.left[left].reshape(8 * PART, ROWS)
        other = R.left_in[left].reshape(8 * PART, ROWS)
        total = dot(own, R.right[right]) + dot(other, R.right_in[right])
        R.grad[u] = total.astype(BF16).reshape(2, 4, PART, WIDE)

    def shared_unit(u):
        mine = pl.ds(x * 4, 4)
        factors = (
            (R.left[u, mine], R.right[0]),
            (R.left_in[u, mine], R.right_in[0]),
            (R.left_x[0, u - 1], R.right_x[0]),
            (R.left_x[1, u - 1], R.right_x[1]),
        )
        total = sum(dot(a.reshape(4 * PART, ROWS), b) for a, b in factors)
        R.grad[u, x] = total.astype(BF16).reshape(4, PART, WIDE)

    def place_of(u):
        if u < SHARED:
            return R.sum_down, u * PART, slice(None)
        if u < 8:
            return R.sum_up, 0, slice((u - 4) * WIDE, (u - 3) * WIDE)
        if u == 8:
            return R.sum_out, 0, slice(None)
        return R.sum_qkv, 0, slice((u - 9) * WIDE, (u - 8) * WIDE)

    def add_up(terms, ref, at, first=0, columns=slice(None)):
        def some_rows(r, _):
            rows = pl.ds(pl.multiple_of(r * 16, 16), 16)
            total = sum(array[(*index, rows)].astype(F32) for array, index in terms)
            to = pl.ds(pl.multiple_of(first + r * 16, 16), 16)
            ref[(*at, to, columns)] = total.astype(ref.dtype)
            return 0

        lax.fori_loop(0, PART // 16, some_rows, 0)

    def finish(u, terms):
        ref, first, columns = place_of(u)
        add_up(terms, ref, (), first, columns)

    def start(make, *operands):
        make(*operands).start()

    def ax_copy(u, j):
        i = u - SHARED
        return copy(
            R.grad.at[u, 1 - x, owner(j)], R.ax.at[i, j], R.axs.at[i, j], R.axr.at[i, j], near_x
        )

    def az_copy(u, src, at, slot, device):
        i = u - 1
        return copy(src.at[at], R.az.at[i, slot], R.azs.at[i, slot], R.azr.at[i, slot], device)

    def x_sum(u, j):
        own = (R.grad, (u, x, owner(j)))
        if u < SHARED:
            return [own]
        ax_copy(u, j).wait_recv()
        return [own, (R.ax, (u - SHARED, j))]

    def x_send(is_outer, u, j):
        start(ax_copy, u, j)

    def z_send(is_outer, u, j):
        if is_outer and u < SHARED:
            start(az_copy, u, R.grad, (u, x, owner(j)), j - 1, near_side)
            return
        total = x_sum(u, j)
        if is_outer:
            add_up(total, R.ax, (u - SHARED, j))
            start(az_copy, u, R.ax, (u - SHARED, j), j - 1, near_side)
            return
        slot, device = (j - 1, near_side) if j else (3, near_mid)
        at = (u - 1, slot)
        az_copy(u, R.az, at, slot, device).wait_recv()
        add_up(total + [(R.az, at)], R.az, at)
        if j:
            start(az_copy, u, R.az, at, 6 - j, near_mid)
        else:
            start(az_copy, u, R.az, at, 0, near_side)

    def z_last(is_outer, u, j):
        total = x_sum(u, j)
        for slot, device in ((0, near_side),) if is_outer else ((0, near_side), (4, near_mid)):
            az_copy(u, R.az, (u - 1, slot), slot, device).wait_recv()
            total.append((R.az, (u - 1, slot)))
        finish(u, total)

    def bz_copy(src, at, slot, device):
        return copy(src.at[at], R.bz.at[slot], R.bzs.at[slot], R.bzr.at[slot], device)

    def bx_copy():
        return copy(R.bs, R.bx, R.bxs.at[0], R.bxr.at[0], near_x)

    def bz_send(is_outer, u, j):
        if is_outer:
            start(bz_copy, R.grad, (0, slice(None), owner(j)), j - 1, near_side)
            return
        slot, device = (j - 1, near_side) if j else (3, near_mid)
        bz_copy(R.bz, slot, slot, device).wait_recv()
        for a in range(2):
            add_up([(R.bz, (slot, a)), (R.grad, (0, a, owner(j)))], R.bz, (slot, a))
        if j:
            start(bz_copy, R.bz, slot, 6 - j, near_mid)
        else:
            start(bz_copy, R.bz, slot, 0, near_side)

    def b_total(is_outer, a):
        terms = [(R.grad, (0, a, z)), (R.bz, (0, a)), (R.bz, (4, a))]
        return terms[:2] if is_outer else terms

    def bx_send(is_outer, u, j):
        bz_copy(R.bz, 0, 0, near_side).wait_recv()
        if not is_outer:
            bz_copy(R.bz, 4, 4, near_mid).wait_recv()
        add_up(b_total(is_outer, 1 - x), R.bs, ())
        start(bx_copy)

    def bx_last(is_outer, u, j):
        bx_copy().wait_recv()
        finish(0, b_total(is_outer, x) + [(R.bx, ())])

    def v_copy(stage, src, at, device):
        return copy(src.at[at] if at is not None else src, R.vec_in.at[stage], R.vs.at[stage], R.vr.at[stage], device)

    def v_step(is_outer, high, low):
        stage = 4 * high + low
        if stage == 0:
            R.vec_part[3] = R.vec[...]
            start(v_copy, 0, R.vec_part, 3, near_core)
        elif stage == 1:
            v_copy(0, R.vec_part, 3, near_core).wait_recv()
            R.vec_part[0] = R.vec[...] + R.vec_in[0]
            start(v_copy, 1, R.vec_part, 0, near_x)
        elif stage == 2:
            v_copy(1, R.vec_part, 0, near_x).wait_recv()
            R.vec_part[1] = R.vec_part[0] + R.vec_in[1]
            if is_outer:
                start(v_copy, 2, R.vec_part, 1, near_side)
        elif stage == 3:
            v_copy(2, R.vec_part, 1, near_side).wait_recv()
            R.vec_part[2] = R.vec_part[1] + R.vec_in[2]
            start(v_copy, 3, R.vec_part, 2, near_mid)
        elif stage == 4:
            v_copy(3, R.vec_part, 2, near_mid).wait_recv()
            R.vec_part[4] = R.vec_part[2] + R.vec_in[3]
            R.vec_sum[...] = R.vec_part[4]
            start(v_copy, 4, R.vec_part, 4, near_side)
        else:
            v_copy(4, R.vec_part, 3, near_side).wait_recv()
            R.vec_sum[...] = R.vec_in[4]

    steps = (x_send, z_send, z_last, bz_send, bx_send, bx_last, v_step)

    def serve(which, step):
        def run(is_outer, codes):
            for code in codes:
                kind, rest = divmod(code, 100)
                steps[kind](is_outer, rest // 4, rest % 4)

        codes_outer, codes_inner = (order[step] for order in ORDER[which])
        if codes_outer:
            pl.when(outer)(lambda: run(True, codes_outer))
        if codes_inner:
            pl.when(inner)(lambda: run(False, codes_inner))

    done = [0]

    def between(*more):
        @pl.when(section == 0)
        def _():
            for item in more or (None,):
                serve(0, done[0])
                done[0] += 1
                if item is not None:
                    item()

    def unit(u):
        return lambda: weight_unit(u)

    def shared_arrives(m):
        share(1, m).wait_recv()
        share(2, m).start()

    @pl.when(section == 1)
    def _():
        for m in range(MICRO):
            shared_arrives(m)

    R.vec[...] = jnp.zeros((8, WIDE), F32)

    @pl.when(section == 0)
    def _():
        left_copy(0).wait_recv()
        for m in range(MICRO):
            share(0, m).wait_recv()
        shared_arrives(0)

    def unit_up(i):
        def run():
            if i == 0:
                left_copy(1).wait_recv()
            right_copy(1 + i).wait_recv()
            weight_unit(SHARED + i)

        return run

    between(unit(0))
    for t in range(4):
        between()
        pl.when(section == 0)(lambda: feed_inner_matmul(R, t))
        feed_inner(R, t)
        right_copy(1 + t).start()
    for t in range(3):
        between()
        feed_entry(R, t)
    between()
    feed_norm(R)
    right_copy(5).start()
    between(*[unit_up(i) for i in range(4)])
    between()
    attention_mixed(R)

    def shared_units():
        for kind in range(2):
            left_x_copy(kind).wait_recv()
        for m in range(MICRO):
            share(2, m).wait_recv()

    for m in range(MICRO):
        for t in range(3):
            between()
            attention_pairs(R, m, t)
            if m == 0 and t == 0:
                pl.when(section == 0)(lambda: shared_arrives(1))
        between()
        attention_entry(R, m)
        if m == 0:
            pl.when(section == 0)(shared_units)
            between(*[lambda u=u: shared_unit(u) for u in range(1, SHARED)])

        @pl.when(section == 1)
        def _():
            g_copy(m).start()

    right_copy(6).start()
    leaves[1].start()

    @pl.when(section == 0)
    def _():
        for i in (2, 3):
            left_copy(i).wait_recv()
            right_copy(3 + i).wait_recv()

    between(*[unit(u) for u in range(8, UNITS)])
    pl.when(section == 0)(lambda: serve(0, done[0]))

    @pl.when(section == 1)
    def _():
        send_lefts(range(2))
        left_copy(0).wait_recv()
        for m in range(MICRO):
            share(0, m).wait_recv()
        for step, u in enumerate((0,) + tuple(range(4, UNITS)) + (1, 2, 3)):
            serve(1, step)
            if step == 1:
                send_lefts(range(2, 4))
                for i in range(1, 4):
                    left_copy(i).wait_recv()
                for i in range(1, 7):
                    right_copy(i).wait_recv()
            if u == 1:
                shared_units()
            if 0 < u < SHARED:
                shared_unit(u)
            else:
                weight_unit(u)
        serve(1, UNITS)

    for leave in leaves:
        leave.wait()
    for i in range(4):
        left_copy(i).wait_send()
    for i in range(1, 7):
        right_copy(i).wait_send()
    for kind in range(2):
        left_x_copy(kind).wait_send()
    for kind in range(3):
        for m in range(MICRO):
            share(kind, m).wait_send()

    def every_sent(is_outer):
        for u in range(SHARED, UNITS):
            for j in range(4):
                ax_copy(u, j).wait_send()
        for slot in (0, 1, 2) if is_outer else (3, 4, 0):
            for u in range(1, UNITS):
                az_copy(u, R.az, (u - 1, slot), slot, near_side).wait_send()
            bz_copy(R.bz, slot, slot, near_side).wait_send()
        bx_copy().wait_send()
        for stage in (0, 1, 2) if is_outer else (0, 1, 3, 4):
            v_copy(stage, R.vec_part, 0, near_side).wait_send()

    pl.when(outer)(lambda: every_sent(True))
    pl.when(inner)(lambda: every_sent(False))

    for m in range(MICRO):

        @pl.when(section == 0)
        def _():
            x_copy(m).wait_send()

        @pl.when(section == 1)
        def _():
            g_copy(m).wait_send()


def settle(vec, *refs):
    arrays, narrow, wide, held, sems = refs[:6], refs[6:10], refs[10:16], refs[16:22], refs[22]
    inward = [pltpu.make_async_copy(a, h, sems.at[0, i]) for i, (a, h) in enumerate(zip(arrays, held))]
    copies = [pltpu.make_async_copy(h, w, sems.at[1, i]) for i, (h, w) in enumerate(zip(held, wide))]
    for item in inward:
        item.start()
    for there, item in zip(inward, copies):
        there.wait()
        item.start()
    place = lax.axis_index("dp")
    near = pltpu.roll(vec[...], (16 - place) % 16 * PART, 1)
    for i in range(3):
        narrow[i][...] = near[i : i + 1, :PART]
    far = pltpu.roll(vec[...], (4 - place % 4) % 4 * (4 * PART), 1)
    row = lax.broadcasted_iota(jnp.int32, far.shape, 0)
    mine = jnp.sum(jnp.where(row == 3 + place // 4, far, 0.0), axis=0, keepdims=True)
    narrow[3][...] = mine[:, : 4 * PART]
    for item in copies:
        item.wait()


def layer_device(
    inputs, cotangent, lengths, gain_one, w_qkv, w_out, gain_two, w_up, b_up, w_down, b_down
):
    y, d_state, qkv, out, up, down, vec = pl.pallas_call(
        kernel,
        out_shape=[jax.ShapeDtypeStruct(s, d) for s, d in OUT.values()],
        in_specs=list(IN.values()),
        out_specs=[ANY] * 2 + [VMEM] * (len(OUT) - 2),
        scratch_shapes=[pltpu.VMEM(s, d) for s, d in SCRATCH.values()]
        + [pltpu.SemaphoreType.DMA(s) for s in SEMS.values()],
        compiler_params=pltpu.CompilerParams(
            collective_id=0, has_side_effects=True, vmem_limit_bytes=60 * 2**20
        ),
        name="layers",
    )(
        inputs.reshape(ROWS, D), cotangent.reshape(ROWS, D), lengths[:, 0], gain_one, w_qkv[0],
        w_out[0], gain_two, w_up[0], b_up, w_down[0], b_down,
    )
    totals = pl.pallas_call(
        settle,
        out_shape=[
            jax.ShapeDtypeStruct((1, PART), F32),
            jax.ShapeDtypeStruct((1, PART), F32),
            jax.ShapeDtypeStruct((1, PART), F32),
            jax.ShapeDtypeStruct((1, 4 * PART), F32),
        ]
        + [jax.ShapeDtypeStruct(s, d) for s, d in list(OUT.values())[:6]],
        in_specs=[VMEM] + [ANY] * 6,
        out_specs=[VMEM] * 4 + [ANY] * 6,
        scratch_shapes=[pltpu.VMEM(s, d) for s, d in list(OUT.values())[:6]]
        + [pltpu.SemaphoreType.DMA((2, 6))],
        name="settle",
    )(vec, y, d_state, qkv, out, up, down)
    gain_a, gain_b, bias_down, bias_up, y, d_state, qkv, out, up, down = totals
    return (
        y.reshape(1, MICRO, SLOT, D),
        d_state.reshape(1, MICRO, SLOT, D),
        gain_a,
        qkv[None],
        out[None],
        gain_b,
        up[None],
        bias_up,
        down[None],
        bias_down,
    )


def solution(mesh):
    placed = (
        P(None, "dp", None),
        P(None, "dp", None),
        P(None, "dp", None),
        P("section", None),
        P("section", None, None),
        P("section", None, None),
        P("section", None),
        P("section", None, None),
        P("section", None),
        P("section", None, None),
        P("section", None),
    )
    return jax.shard_map(
        layer_device if mesh.shape["dp"] == 16 else plain_device,
        mesh=mesh,
        in_specs=placed,
        out_specs=(
            P("section", None, "dp", None),
            P("section", None, "dp", None),
            P("section", "dp"),
            P("section", "dp", None),
            P("section", "dp", None),
            P("section", "dp"),
            P("section", "dp", None),
            P("section", "dp"),
            P("section", "dp", None),
            P("section", "dp"),
        ),
        check_vma=False,
    )
```
